128 devices in a mesh: dp: 32 (over y, x, z_lo), tensor: 4 (over z_hi, core).
Axes of the slice: x: 4, y: 4, z: 4 (z_hi: 2, z_lo: 2; z = z_hi * 2 + z_lo), core: 2. Of those that a mesh axis runs over, the one named last changes fastest.
Arguments:
- inputs: bfloat16 [16384, 2048], P(('dp', 'tensor')), may hold values from -6 to 6
- cotangent: bfloat16 [16384, 2048], P(('dp', 'tensor')), may hold values from -6 to 6
- lengths: int32 [32, 4], P('dp'), may hold values from 1 to 384, as said below
- qkv_weight: float32 [3, 2048, 2048], P(None, 'dp', 'tensor'), may hold values from -0.125 to 0.125
- out_weight: float32 [2048, 2048], P('tensor', 'dp'), may hold values from -0.5 to 0.5
- up_weight: float32 [2048, 8192], P('dp', 'tensor'), may hold values from -0.125 to 0.125
- down_weight: float32 [8192, 2048], P('tensor', 'dp'), may hold values from -0.0625 to 0.0625
- norm_vectors: float32 [13, 2048], P(None, 'dp'), may hold values from -0.8 to 1.4
- qkv_mean: float32 [3, 2048, 2048], P(None, 'dp', 'tensor'), may hold values from -32 to 32
- qkv_square: float32 [3, 2048, 2048], P(None, 'dp', 'tensor'), may hold values from 137.6256 to 557.056
- out_mean: float32 [2048, 2048], P('tensor', 'dp'), may hold values from -16 to 16
- out_square: float32 [2048, 2048], P('tensor', 'dp'), may hold values from 34.4064 to 137.6256
- up_mean: float32 [2048, 8192], P('dp', 'tensor'), may hold values from -24 to 24
- up_square: float32 [2048, 8192], P('dp', 'tensor'), may hold values from 77.0048 to 311.296
- down_mean: float32 [8192, 2048], P('tensor', 'dp'), may hold values from -56 to 56
- down_square: float32 [8192, 2048], P('tensor', 'dp'), may hold values from 360.448 to 1458.176
- vector_mean: float32 [13, 2048], P(None, 'dp'), may hold values from -48 to 48
- vector_square: float32 [13, 2048], P(None, 'dp'), may hold values from 163.84 to 1245.184
Outputs:
- block_out: bfloat16 [16384, 2048], P(('dp', 'tensor'))
- input_grad: float32 [16384, 2048], P(('dp', 'tensor'))
- qkv_updated: float32 [3, 2048, 2048], P(None, 'dp', 'tensor')
- qkv_moment: float32 [3, 2048, 2048], P(None, 'dp', 'tensor')
- qkv_squares: float32 [3, 2048, 2048], P(None, 'dp', 'tensor')
- out_updated: float32 [2048, 2048], P('tensor', 'dp')
- out_moment: float32 [2048, 2048], P('tensor', 'dp')
- out_squares: float32 [2048, 2048], P('tensor', 'dp')
- up_updated: float32 [2048, 8192], P('dp', 'tensor')
- up_moment: float32 [2048, 8192], P('dp', 'tensor')
- up_squares: float32 [2048, 8192], P('dp', 'tensor')
- down_updated: float32 [8192, 2048], P('tensor', 'dp')
- down_moment: float32 [8192, 2048], P('tensor', 'dp')
- down_squares: float32 [8192, 2048], P('tensor', 'dp')
- vector_updated: float32 [13, 2048], P(None, 'dp')
- vector_moment: float32 [13, 2048], P(None, 'dp')
- vector_squares: float32 [13, 2048], P(None, 'dp')
The draws below stay inside these ranges and needn't reach their ends.
Inputs may be any that keep to these rules, and one draw needn't show every extreme that they name: `lengths`: each row fills the 512 tokens of its group; its second entry is 384 and its first is under 128.
All inputs are finite; a program needn't handle non-finite values.
Results may differ from the reference program's by a relative error of at most 0.012.
Values may be sent and summed in bfloat16 or wider, within the bound.
A program may use at most 256 MiB of HBM per device.

```python
import math
import jax
import jax.numpy as jnp
from jax import lax

D = 2048
FF = 8192
HEADS = 8
HD = 256
ROT = 64
TOK_DEV = 128
UPDATE_STEP = 10
GROUP = 512
GROUPS = 32
TOKENS = 16384
MOST_LEN = 384
VROWS = 13


def draw_lengths(key, part):
    key = jax.random.fold_in(key, 11)
    keys = jax.random.split(key, 2)
    leading = jax.random.randint(keys[0], (GROUPS,), 1, TOK_DEV - 1).astype(jnp.int32)
    remains = TOK_DEV - leading
    raw_bits = jax.random.randint(keys[1], (GROUPS,), 0, 1 << 20).astype(jnp.int32)
    third_len = 1 + raw_bits % (remains - 1)
    fourth_len = remains - third_len
    longest = jnp.full((GROUPS,), MOST_LEN, jnp.int32)
    return jnp.stack([leading, longest, third_len, fourth_len], axis=1).astype(jnp.int32)


def draw_norm_vectors(key, part):
    key = jax.random.fold_in(key, 23)
    keys = jax.random.split(key, 2)
    noise = jnp.clip(jax.random.normal(keys[0], (VROWS, D), jnp.float32), -4.0, 4.0)
    gains = jax.random.uniform(keys[1], (VROWS, D), jnp.float32, 0.6, 1.4)
    row_ids = jnp.arange(VROWS)[:, None]
    is_gain = (row_ids == 0) | (row_ids == 2)
    return jnp.where(is_gain, gains, 0.2 * noise).astype(jnp.float32)


def shard_levels(rng, shape, cuts, least, largest):
    factor_of = 1.0
    for dim, parts in cuts:
        steps = jax.random.uniform(jax.random.fold_in(jax.random.fold_in(rng, 6), dim), (parts,), jnp.float32, least / len(cuts), largest / len(cuts))
        factor_of = factor_of * jnp.repeat(jnp.exp(steps), shape[dim] // parts).reshape((-1,) + (1,) * (len(shape) - 1 - dim))
    return factor_of


def normal_values(key, shape, spread, reach, pieces=(), held_as=jnp.bfloat16):
    values = spread * jax.random.normal(key, shape, jnp.float32)
    if pieces:
        values = values * shard_levels(key, shape, pieces, -0.22, 0.18)
    return jnp.clip(values, -reach, reach).astype(held_as)


def setup_inputs(seed: int = 0) -> dict:
    key_of = jax.random.split(jax.random.key(seed), 19)
    inputs = normal_values(key_of[0], (TOKENS, D), 1.0, 6.0, ((0, 128),))
    cotangent = normal_values(key_of[1], (TOKENS, D), 1.0, 6.0, ((0, 128),))
    lengths = draw_lengths(jax.random.fold_in(key_of[18], 71), 0)
    qkv_weight = normal_values(key_of[3], (3, D, D), D ** -0.5, 0.125, ((1, 32), (2, 4)), jnp.float32)
    out_weight = normal_values(key_of[4], (D, D), (D // 16) ** -0.5, 0.5, ((0, 4), (1, 32)), jnp.float32)
    up_weight = normal_values(key_of[5], (D, FF), D ** -0.5, 0.125, ((0, 32), (1, 4)), jnp.float32)
    down_weight = normal_values(key_of[6], (FF, D), FF ** -0.5, 0.0625, ((0, 4), (1, 32)), jnp.float32)
    norm_vectors = draw_norm_vectors(jax.random.fold_in(key_of[18], 71), 0)
    qkv_mean = normal_values(key_of[8], (3, D, D), (0.044 * TOKENS ** 0.5), 32.0, ((1, 32), (2, 4)), jnp.float32)
    qkv_square = jnp.clip(jnp.exp(math.log(557.056) - 1.3981289 * jax.random.uniform(key_of[9], (3, D, D), jnp.float32) ** shard_levels(key_of[9], (3, D, D), ((1, 32), (2, 4)), -0.2, 0.2)), 137.6256, 557.056)
    out_mean = normal_values(key_of[10], (D, D), (0.022 * TOKENS ** 0.5), 16.0, ((0, 4), (1, 32)), jnp.float32)
    out_square = jnp.clip(jnp.exp(math.log(137.6256) - 1.3862944 * jax.random.uniform(key_of[11], (D, D), jnp.float32) ** shard_levels(key_of[11], (D, D), ((0, 4), (1, 32)), -0.2, 0.2)), 34.4064, 137.6256)
    up_mean = normal_values(key_of[12], (D, FF), (0.033 * TOKENS ** 0.5), 24.0, ((0, 32), (1, 4)), jnp.float32)
    up_square = jnp.clip(jnp.exp(math.log(311.296) - 1.3968765 * jax.random.uniform(key_of[13], (D, FF), jnp.float32) ** shard_levels(key_of[13], (D, FF), ((0, 32), (1, 4)), -0.2, 0.2)), 77.0048, 311.296)
    down_mean = normal_values(key_of[14], (FF, D), (0.072 * TOKENS ** 0.5), 56.0, ((0, 4), (1, 32)), jnp.float32)
    down_square = jnp.clip(jnp.exp(math.log(1458.176) - 1.397594 * jax.random.uniform(key_of[15], (FF, D), jnp.float32) ** shard_levels(key_of[15], (FF, D), ((0, 4), (1, 32)), -0.2, 0.2)), 360.448, 1458.176)
    vector_mean = normal_values(key_of[16], (VROWS, D), (0.067 * TOKENS ** 0.5), 48.0, ((1, 32),), jnp.float32)
    vector_square = jnp.clip(jnp.exp(math.log(1245.184) - 2.0281482 * jax.random.uniform(key_of[17], (VROWS, D), jnp.float32) ** shard_levels(key_of[17], (VROWS, D), ((1, 32),), -0.2, 0.2)), 163.84, 1245.184)
    return {"inputs": inputs, "cotangent": cotangent, "lengths": lengths, "qkv_weight": qkv_weight, "out_weight": out_weight, "up_weight": up_weight, "down_weight": down_weight, "norm_vectors": norm_vectors, "qkv_mean": qkv_mean, "qkv_square": qkv_square, "out_mean": out_mean, "out_square": out_square, "up_mean": up_mean, "up_square": up_square, "down_mean": down_mean, "down_square": down_square, "vector_mean": vector_mean, "vector_square": vector_square}


@jax.custom_vjp
def low(v):
    return lax.optimization_barrier(v.astype(jnp.bfloat16)).astype(jnp.float32)

@jax.custom_vjp
def low_back(v):
    return v

def low_keep(v):
    return (low(v), None)

def low_pass(kept, grad):
    return (grad,)

def back_keep(v):
    return (v, None)

def back_low(kept, grad):
    return (low(grad),)
low.defvjp(low_keep, low_pass)
low_back.defvjp(back_keep, back_low)
norm_eps = 1e-05
beta_first = 0.9
beta_second = 0.95
adam_eps = 1e-08
matrix_rate = 0.02
vector_rate = 0.2
matrix_decay = 0.01
masked_score = -1e+30
highest = lax.Precision.HIGHEST

def rotary_tables(positions):
    half_rot = ROT // 2
    frequency = jnp.exp(jnp.arange(half_rot, dtype=jnp.float32) * (-2.0 * math.log(10000.0) / ROT))
    angles = positions.astype(jnp.float32)[:, None] * frequency[None, :]
    return (jnp.cos(angles), jnp.sin(angles))

def rotate(values_in, cos_table, sin_table):
    half_rot = ROT // 2
    lead_half = values_in[..., :half_rot]
    tail_half = values_in[..., half_rot:ROT]
    cos_part = cos_table[:, None, :]
    sin_part = sin_table[:, None, :]
    return jnp.concatenate([lead_half * cos_part - tail_half * sin_part, tail_half * cos_part + lead_half * sin_part, values_in[..., ROT:]], axis=-1)

def segment_layout(seq_lengths, total_rows):
    seq_ends = jnp.cumsum(seq_lengths).astype(jnp.int32)
    seq_starts = seq_ends - seq_lengths.astype(jnp.int32)
    row_index = jnp.arange(total_rows, dtype=jnp.int32)
    segment = lax.optimization_barrier(jnp.sum((row_index[:, None] >= seq_ends[None, :]).astype(jnp.int32), axis=1))
    chosen = segment[:, None] == jnp.arange(seq_lengths.shape[0], dtype=jnp.int32)[None, :]
    position = row_index - lax.optimization_barrier(jnp.sum(jnp.where(chosen, seq_starts[None, :], 0), axis=1)).astype(jnp.int32)
    return (segment, position)

def attend_group(query_rows, key_rows, value_rows, segment):
    total_rows = query_rows.shape[0]
    row_index = jnp.arange(total_rows, dtype=jnp.int32)
    allowed = (segment[:, None] == segment[None, :]) & (row_index[None, :] <= row_index[:, None])
    scores = jnp.einsum('qhd,khd->hqk', query_rows, key_rows, precision=highest) * HD ** (-0.5)
    scores = jnp.where(allowed[None], scores, masked_score)
    scores = low_back(scores)
    soft_weights = jax.nn.softmax(scores, axis=-1)
    return jnp.einsum('hqk,khd->qhd', low(soft_weights), value_rows, precision=highest)

def attend_item(item):
    return jax.checkpoint(attend_group)(item[0], item[1], item[2], item[3])

def layer(rows, qkv_w, out_w, up_w, down_w, vectors, segment, position):
    vectors = low(vectors)
    centred = rows - lax.optimization_barrier(jnp.mean(rows, axis=-1, keepdims=True))
    unit = centred * lax.rsqrt(lax.optimization_barrier(jnp.mean(centred * centred, axis=-1, keepdims=True)) + norm_eps)
    norm_one = low(unit * vectors[0] + vectors[1])
    norm_two = low(unit * vectors[2] + vectors[3])
    qkv_pre = jnp.einsum('td,cde->cte', norm_one, low(qkv_w), precision=highest) + vectors[4:7][:, None, :]
    qkv_pre = low_back(qkv_pre)
    cos_table, sin_table = rotary_tables(position)
    query_rows = low(rotate(qkv_pre[0].reshape(TOKENS, HEADS, HD), cos_table, sin_table))
    key_rows = low(rotate(qkv_pre[1].reshape(TOKENS, HEADS, HD), cos_table, sin_table))
    value_rows = low(qkv_pre[2].reshape(TOKENS, HEADS, HD))
    grouped = (query_rows.reshape(GROUPS, GROUP, HEADS, HD), key_rows.reshape(GROUPS, GROUP, HEADS, HD), value_rows.reshape(GROUPS, GROUP, HEADS, HD), segment.reshape(GROUPS, GROUP))
    mixed_heads = lax.map(attend_item, grouped).reshape(TOKENS, D)
    mixed_heads = low(low_back(mixed_heads))
    attention = jnp.dot(mixed_heads, low(out_w), precision=highest)
    hidden = low_back(jnp.dot(norm_two, low(up_w), precision=highest) + vectors[9:].reshape(FF))
    activated = low(jax.nn.gelu(hidden, approximate=False))
    feed_forward = jnp.dot(activated, low(down_w), precision=highest)
    return rows + attention + feed_forward + vectors[7] + vectors[8]

def adamw(weight, gradient, moment, square, step_rate, decay_rate):
    moment_new = beta_first * moment + (1.0 - beta_first) * gradient
    square_new = beta_second * square + (1.0 - beta_second) * gradient * gradient
    first_fix = 1.0 - beta_first ** UPDATE_STEP
    second_fix = 1.0 - beta_second ** UPDATE_STEP
    direction = moment_new / first_fix / (jnp.sqrt(square_new / second_fix) + adam_eps)
    weight_new = weight - step_rate * (direction + decay_rate * weight)
    return (weight_new, moment_new, square_new)

def group_layout(row_lengths):
    return segment_layout(row_lengths, GROUP)

def reference(inputs, cotangent, lengths, qkv_weight, out_weight, up_weight, down_weight, norm_vectors, qkv_mean, qkv_square, out_mean, out_square, up_mean, up_square, down_mean, down_square, vector_mean, vector_square):
    segment, position = jax.vmap(group_layout)(lengths)
    segment = segment.reshape(TOKENS)
    position = position.reshape(TOKENS)

    def forward(rows, qkv_w, out_w, up_w, down_w, vectors):
        return layer(rows, qkv_w, out_w, up_w, down_w, vectors, segment, position)
    result, pullback = jax.vjp(forward, inputs.astype(jnp.float32), qkv_weight, out_weight, up_weight, down_weight, norm_vectors)
    grads = pullback(cotangent.astype(jnp.float32))
    qkv_new = adamw(qkv_weight, grads[1], qkv_mean, qkv_square, matrix_rate, matrix_decay)
    out_new = adamw(out_weight, grads[2], out_mean, out_square, matrix_rate, matrix_decay)
    up_new = adamw(up_weight, grads[3], up_mean, up_square, matrix_rate, matrix_decay)
    down_new = adamw(down_weight, grads[4], down_mean, down_square, matrix_rate, matrix_decay)
    vector_new = adamw(norm_vectors, grads[5], vector_mean, vector_square, vector_rate, 0.0)
    return (result.astype(jnp.bfloat16), grads[0], qkv_new[0], qkv_new[1], qkv_new[2], out_new[0], out_new[1], out_new[2], up_new[0], up_new[1], up_new[2], down_new[0], down_new[1], down_new[2], vector_new[0], vector_new[1], vector_new[2])
```

```python
import functools
import math

import jax
import jax.numpy as jnp
from jax import lax
from jax.experimental import pallas as pl
from jax.experimental.pallas import tpu as pltpu
from jax.sharding import PartitionSpec as P

HD = 256
ROT = 64
UPDATE_STEP = 10
RING_SIZE = 4


norm_eps = 1e-05
beta_first = 0.9
beta_second = 0.95
adam_eps = 1e-08
matrix_rate = 0.02
vector_rate = 0.2
matrix_decay = 0.01
masked_score = -1e30
inv_root_two = 1.0 / math.sqrt(2.0)
inv_root_tau = 1.0 / math.sqrt(2.0 * math.pi)

MESH = pl.DeviceIdType.MESH
ANY = pl.BlockSpec(memory_space=pl.ANY)
VMEM = pl.BlockSpec(memory_space=pltpu.VMEM)


def place():
    dp, tensor = lax.axis_index("dp"), lax.axis_index("tensor")
    z = (tensor // 2) * 2 + dp % 2
    return dp // 8, (dp // 2) % RING_SIZE, z, tensor % 2


def device(y, x, z, core):
    return ((y * RING_SIZE + x) * 2 + z % 2, (z // 2) * 2 + core)


def around(i, step):
    return (i + step + RING_SIZE) % RING_SIZE


def greet(devices):
    barrier = pltpu.get_barrier_semaphore()
    for d in devices:
        pl.semaphore_signal(barrier, inc=1, device_id=d, device_id_type=MESH)


def meet(devices):
    pl.semaphore_wait(pltpu.get_barrier_semaphore(), len(devices))


def mailbox(note, send, recv, *lead):
    def post(k, src, dst, to):
        note[0] = (id(send), *lead, k)
        return pltpu.make_async_remote_copy(
            src_ref=src,
            dst_ref=dst,
            send_sem=send.at[(*lead, k)],
            recv_sem=recv.at[(*lead, k)],
            device_id=to,
            device_id_type=MESH,
        )

    return post


LOW = jnp.bfloat16
WIDE = jnp.float32
GROUP = 512
TILE = 256
WIDE_PART, REST = slice(0, 768), slice(768, 1280)
LANES = 128
PLANE_MESSAGES = 33
RING_MESSAGES = 8


VEC, UP, QKV, OD = range(4)
DY = 3
(
    SWAP,
    OWN,
    OTHER,
    ROUND_ONE_X,
    ROUND_ONE_Y,
    ROUND_TWO_A,
    ROUND_TWO_B,
    ROUND_TWO_C,
    ROUND_THREE,
    LAST_ROUND,
    RING,
    RING_ON,
    RING_FAR,
    TABLES,
    VECTORS_X,
    VECTORS_Y,
    VECTORS,
    NORM,
    FETCH,
    HIDDEN,
    PROJECT,
    ATTEND,
    OD_GRADS,
) = range(23)
(
    FIRST,
    NEAR,
    SECOND,
    FAR_SIDE,
    FINISH,
    Z_MATE,
    Z_FIRST,
    Z_SECOND,
    Z_FINISH,
    LOADS,
    VEC_ONE,
    VEC_TWO,
    VEC_THREE,
    SETTLE,
    CAT_GRADS,
    UP_GRADS,
    BRANCH,
    ATTEND_BACK,
    QKV_GRADS,
    NORM_GRADS,
) = range(20)
FORWARD_ORDER = (
    (OWN, UP), (SWAP, UP), (SWAP, QKV), (SWAP, VEC), (RING, 0), (OWN, QKV), (OTHER, UP),
    (VECTORS_X,), (OTHER, QKV), (VECTORS_Y,), (SWAP, OD), (ROUND_ONE_X, UP), (ROUND_ONE_Y, UP),
    (TABLES,), (ROUND_ONE_X, QKV), (ROUND_ONE_Y, QKV), (VECTORS,), (RING_ON, 0),
    (ROUND_TWO_A, UP), (RING, 1), (ROUND_TWO_B, UP), (NORM, 0), (ROUND_TWO_C, UP), (NORM, 4),
    (NORM, 2), (ROUND_THREE, UP), (RING_FAR, 0), (NORM, 1), (ROUND_TWO_B, QKV), (OTHER, OD),
    (NORM, 6), (LAST_ROUND, UP), (FETCH, UP), (OWN, OD), (HIDDEN, 0), (ROUND_TWO_A, QKV),
    (ROUND_TWO_C, QKV), (RING_ON, 1), (HIDDEN, 1), (ROUND_THREE, QKV), (ROUND_ONE_Y, OD),
    (HIDDEN, 2), (ROUND_ONE_X, OD), (HIDDEN, 3), (RING_FAR, 1), (LAST_ROUND, QKV),
    (ROUND_TWO_A, OD), (FETCH, QKV), (PROJECT, 0), (PROJECT, 1), (ATTEND, 0), (FETCH, DY),
    (ROUND_TWO_B, OD), (ATTEND, 1), (ROUND_TWO_C, OD), (OD_GRADS, 0), (ROUND_THREE, OD),
    (OD_GRADS, 1), (OD_GRADS, 2), (OD_GRADS, 3), (LAST_ROUND, OD),
)
BACKWARD_ORDER = (
    (FIRST, OD), (LOADS,), (CAT_GRADS, 0), (CAT_GRADS, 1), (CAT_GRADS, 2), (CAT_GRADS, 3),
    (UP_GRADS, 0), (UP_GRADS, 1), (UP_GRADS, 2), (UP_GRADS, 3), (FIRST, UP), (BRANCH, 0),
    (NEAR, OD, 0), (BRANCH, 1), (Z_MATE, 0), (NEAR, OD, 1), (BRANCH, 2), (BRANCH, 3),
    (ATTEND_BACK, 0), (Z_MATE, 1), (Z_FIRST, 0), (ATTEND_BACK, 1), (QKV_GRADS, 0), (QKV_GRADS, 1),
    (QKV_GRADS, 2), (Z_FIRST, 1), (Z_SECOND, 0), (QKV_GRADS, 3), (FIRST, QKV), (NEAR, UP, 0),
    (NORM_GRADS, 0), (NORM_GRADS, 1), (Z_MATE, 3), (Z_MATE, 2), (Z_SECOND, 1), (NORM_GRADS, 2),
    (Z_FINISH, 0), (Z_FIRST, 3), (NEAR, UP, 1), (NORM_GRADS, 3), (Z_FIRST, 2), (SECOND, OD, 1),
    (Z_SECOND, 3), (Z_MATE, 5), (SECOND, UP, 0), (VEC_ONE,), (NEAR, QKV, 1), (FAR_SIDE, OD, 1),
    (Z_SECOND, 2), (Z_MATE, 4), (Z_FIRST, 5), (SECOND, UP, 1), (FINISH, OD, 1), (NEAR, QKV, 0),
    (Z_FIRST, 4), (Z_FINISH, 1), (FAR_SIDE, UP, 0), (Z_SECOND, 5), (VEC_TWO,), (SECOND, OD, 0),
    (FAR_SIDE, UP, 1), (VEC_THREE,), (Z_FINISH, 3), (SECOND, QKV, 1), (Z_SECOND, 4),
    (SECOND, QKV, 0), (FAR_SIDE, OD, 0), (FINISH, UP, 1), (FAR_SIDE, QKV, 1), (FAR_SIDE, QKV, 0),
    (FINISH, QKV, 1), (Z_FINISH, 2), (FINISH, QKV, 0), (FINISH, OD, 0), (SETTLE,),
    (FINISH, UP, 0), (Z_FINISH, 5), (Z_FINISH, 4),
)


def wide(v):
    return v.astype(WIDE)


def nn(a, b):
    return jnp.dot(a, b, preferred_element_type=WIDE)


def nt(a, b):
    return lax.dot_general(a, b, (((1,), (1,)), ((), ())), preferred_element_type=WIDE)


def turn_over(eye, v):
    return nt(eye[...], v).astype(LOW)


def fill_eye(eye):
    row = lax.broadcasted_iota(jnp.int32, eye.shape, 0)
    eye[...] = wide(row == lax.broadcasted_iota(jnp.int32, eye.shape, 1)).astype(LOW)


def cols(k, size):
    return pl.ds(pl.multiple_of(k * size, size), size)


def turned(v, cos_table, sin_table):
    first = v[:, :LANES]
    lane = lax.broadcasted_iota(jnp.int32, first.shape, 1)
    swapped = jnp.where(
        lane < ROT // 2,
        pltpu.roll(first, LANES - ROT // 2, 1),
        pltpu.roll(first, ROT // 2, 1),
    )
    return jnp.concatenate([first * cos_table + swapped * sin_table, v[:, LANES:]], axis=1)


def soft_columns(query, key, start, first):
    scores = nt(key, query) * (HD**-0.5)
    key_at = lax.broadcasted_iota(jnp.int32, scores.shape, 0)
    query_at = lax.broadcasted_iota(jnp.int32, scores.shape, 1) + first
    allowed = (wide(key_at) >= start) & (key_at <= query_at)
    scores = jnp.where(allowed, scores, masked_score)
    powers = jnp.exp(scores - jnp.max(scores, axis=0, keepdims=True))
    return powers * (1.0 / jnp.sum(powers, axis=0, keepdims=True))


def streamed(count, copies, use):
    for c in copies(0, 0):
        c.start()

    @pl.loop(0, count)
    def _(k):
        slot = lax.rem(k, 2)

        @pl.when(k + 1 < count)
        def _():
            for c in copies(k + 1, 1 - slot):
                c.start()

        for c in copies(k, slot):
            c.wait()
        use(k, slot)


def play(order, loops, act):
    at = 0
    while at < len(order):
        kind = order[at][0]
        if kind not in loops:
            act(*order[at])
            at += 1
            continue
        hooks, due = {}, []
        end = max(k for k, entry in enumerate(order) if entry[0] == kind)
        for entry in order[at + 1 : end + 1]:
            if entry[0] == kind:
                if due:
                    hooks[entry[1]] = due
                due = []
            else:
                due.append(entry)
        loops[kind](hooks)
        at = end + 1


def forward_kernel(
    x_in, dy_in, lengths, vectors_in, up_in, qkv_in, out_in, down_in,
    dy_out, up_out, qkv_out, od_out, vecs_out, one_out, two_out, unit_out, heads_out, cat_out,
    slope_out, turn_out, soft_out, grad_out,
    xv, len_v, vec_w, one, two, unit, dy_v, up_w, qkv_w, cat, slope, heads, turn, flip_one, flip_two, stage,
    pre_one, pre_two, soft, begin, eye, len_in, vec_s, up_s, qkv_s, od_s, up_f, qkv_f, out_f, down_f,
    send, recv, ring_send, ring_recv, len_sems, local_sems, keep_sems, stage_sems, wide_sems,
):
    y, x, z, core = place()
    zl = z % 2
    tensor = (z // 2) * 2 + core
    head = tensor * 2 + zl
    other = 1 - zl
    partner = device(y, x, z + 1 - 2 * zl, core)
    xp, xm, yp, ym = around(x, 1), around(x, -1), around(y, 1), around(y, -1)
    zp, zm = around(z, 1), around(z, -1)
    xo, yo, zo = around(x, 2), around(y, 2), around(z, 2)
    to_xp, to_xm = device(y, xp, z, core), device(y, xm, z, core)
    to_yp, to_ym = device(yp, x, z, core), device(ym, x, z, core)
    to_zp, to_zm = device(y, x, zp, core), device(y, x, zm, core)
    mate = device(y, x, z, 1 - core)
    line_x = (to_xp, device(y, xo, z, core), to_xm)
    line_y = (to_yp, device(yo, x, z, core), to_ym)
    neighbours = [*line_x, *line_y, to_zp, to_zm, mate]
    greet(neighbours)

    wide_copies = [
        pltpu.make_async_copy(src, dst, wide_sems.at[k])
        for k, (src, dst) in enumerate(
            ((up_in, up_f), (qkv_in, qkv_f), (out_in, out_f), (down_in, down_f))
        )
    ]
    for c in wide_copies:
        c.start()
    for r in range(4):
        len_in[r : r + 1, :] = jnp.full((1, LANES), lengths[0, r].astype(WIDE))
    len_in[4:8, :] = jnp.zeros((4, LANES), WIDE)
    fill_eye(eye)
    vec_s[...] = jnp.zeros(vec_s.shape, WIDE)
    vec = wide(vectors_in[...].astype(LOW))
    for h in range(2):
        vec_s[h, 0 : vec.shape[0], 0 : vec.shape[1]] = vec

    def prepare(i):
        if i == UP:
            wide_copies[0].wait()
            n = up_s.shape[-1]
            for h in range(2):
                up_s[h] = up_f[:, h * n : (h + 1) * n].astype(LOW)
        elif i == QKV:
            wide_copies[1].wait()
            for h in range(2):
                for c in range(3):
                    at = slice(c * HD, (c + 1) * HD)
                    qkv_s[h, :, at] = qkv_f[c, :, h * HD : (h + 1) * HD].astype(LOW)
        else:
            wide_copies[2].wait()
            wide_copies[3].wait()
            n = od_s.shape[-1] - HD
            for h in range(2):
                od_s[h, :, 0:HD] = out_f[:, h * HD : (h + 1) * HD].astype(LOW)
                od_s[h, :, HD:] = down_f[:, h * n : (h + 1) * n].astype(LOW)

    w_in = (vec_s, up_s, qkv_s, od_s)
    w_out = (vec_w, up_out, qkv_out, od_out)
    started, note = {}, [None]

    def go(make):
        make().start()
        started[note[0]] = make

    def own_copy(k):
        if k < 4:
            src, dst = w_in[k].at[zl], w_out[k].at[y, x, zl]
        elif k < 6:
            src, dst = rings[k - 4][0], rings[k - 4][1].at[zl, tensor]
        else:
            src, dst = len_in, len_v.at[zl]
        return pltpu.make_async_copy(src, dst, local_sems.at[k])

    rings = ((x_in, xv), (dy_in, dy_out))
    for k in (VEC, 4, 5, 6):
        own_copy(k).start()
    for i in (UP, QKV, OD):
        prepare(i)
        own_copy(i).start()
    meet(neighbours)

    posts = [mailbox(note, send, recv, i) for i in range(4)]
    ring_posts = [mailbox(note, ring_send, ring_recv, j) for j in range(2)]
    four = (to_xp, to_xm, to_yp, to_ym)

    def slot_of(ref, zz, cc):
        return ref.at[zz % 2, (zz // 2) * 2 + cc]

    def arrived(i, k, ref):
        posts[i](k, ref, ref, mate).wait_recv()

    def ring_arrived(j, k, ref):
        ring_posts[j](k, ref, ref, mate).wait_recv()

    def halves_of(blk):
        n = blk.shape[0] // 2
        return blk.at[pl.ds(0, n)], blk.at[pl.ds(n, n)]

    def swap(i):
        go(lambda: posts[i](32, w_in[i].at[other], w_out[i].at[y, x, zl], partner))

    def own_half(i):
        for d in range(4):
            go(lambda d=d: posts[i](d, w_in[i].at[zl], w_out[i].at[y, x, zl], four[d]))

    def other_half(i):
        mine = lambda: w_out[i].at[y, x, other]
        arrived(i, 32, mine())
        for d in range(4):
            go(lambda d=d: posts[i](4 + d, mine(), mine(), four[d]))

    def round_one_x(i):
        w = w_out[i]
        blk = lambda: w.at[y, xm, zl]
        arrived(i, 0, blk())
        go(lambda blk=blk: posts[i](8, halves_of(blk())[0], halves_of(blk())[0], to_xp))
        go(lambda blk=blk: posts[i](12, blk(), blk(), to_yp))
        go(lambda blk=blk: posts[i](13, blk(), blk(), to_ym))
        blk = lambda: w.at[y, xp, zl]
        arrived(i, 1, blk())
        go(lambda blk=blk: posts[i](9, halves_of(blk())[1], halves_of(blk())[1], to_xm))
        go(lambda blk=blk: posts[i](14, blk(), blk(), to_yp))
        go(lambda blk=blk: posts[i](15, blk(), blk(), to_ym))

    def round_one_y(i):
        w = w_out[i]
        blk = lambda: w.at[ym, x, other]
        arrived(i, 6, blk())
        go(lambda blk=blk: posts[i](10, halves_of(blk())[0], halves_of(blk())[0], to_yp))
        go(lambda blk=blk: posts[i](18, blk(), blk(), to_xp))
        go(lambda blk=blk: posts[i](19, blk(), blk(), to_xm))
        blk = lambda: w.at[yp, x, other]
        arrived(i, 7, blk())
        go(lambda blk=blk: posts[i](11, halves_of(blk())[1], halves_of(blk())[1], to_ym))
        go(lambda blk=blk: posts[i](20, blk(), blk(), to_xp))
        go(lambda blk=blk: posts[i](21, blk(), blk(), to_xm))

    def round_two_a(i):
        w = w_out[i]
        blk = lambda: w.at[ym, x, zl]
        arrived(i, 2, blk())
        go(lambda blk=blk: posts[i](24, blk(), blk(), to_yp))
        blk = lambda: w.at[y, xm, other]
        arrived(i, 4, blk())
        go(lambda blk=blk: posts[i](28, blk(), blk(), to_xp))

    def round_two_b(i):
        w = w_out[i]
        blk = lambda: w.at[y, xo, zl]
        arrived(i, 8, halves_of(blk())[0])
        arrived(i, 9, halves_of(blk())[1])
        go(lambda blk=blk: posts[i](16, blk(), blk(), to_yp))
        go(lambda blk=blk: posts[i](17, blk(), blk(), to_ym))
        blk = lambda: w.at[yo, x, other]
        arrived(i, 10, halves_of(blk())[0])
        arrived(i, 11, halves_of(blk())[1])
        go(lambda blk=blk: posts[i](22, blk(), blk(), to_xp))
        go(lambda blk=blk: posts[i](23, blk(), blk(), to_xm))

    def round_two_c(i):
        w = w_out[i]
        blk = lambda: w.at[ym, xm, zl]
        arrived(i, 12, blk())
        go(lambda blk=blk: posts[i](25, blk(), blk(), to_yp))
        blk = lambda: w.at[yp, xp, zl]
        arrived(i, 15, blk())
        go(lambda blk=blk: posts[i](26, blk(), blk(), to_ym))
        blk = lambda: w.at[ym, xm, other]
        arrived(i, 18, blk())
        go(lambda blk=blk: posts[i](29, blk(), blk(), to_xp))
        blk = lambda: w.at[yp, xp, other]
        arrived(i, 21, blk())
        go(lambda blk=blk: posts[i](30, blk(), blk(), to_xm))

    def round_three(i):
        w = w_out[i]
        blk = lambda: w.at[yp, xo, zl]
        arrived(i, 17, blk())
        go(lambda blk=blk: posts[i](27, blk(), blk(), to_ym))
        blk = lambda: w.at[yo, xp, other]
        arrived(i, 23, blk())
        go(lambda blk=blk: posts[i](31, blk(), blk(), to_xm))

    def last_round(i):
        if i == OD:
            for key in list(started)[:-20]:
                started.pop(key)().wait_send()
        w = w_out[i]
        arrived(i, 3, w.at[yp, x, zl])
        arrived(i, 5, w.at[y, xp, other])
        arrived(i, 13, w.at[yp, xm, zl])
        arrived(i, 14, w.at[ym, xp, zl])
        arrived(i, 16, w.at[ym, xo, zl])
        arrived(i, 19, w.at[ym, xp, other])
        arrived(i, 20, w.at[yp, xm, other])
        arrived(i, 22, w.at[yo, xm, other])
        arrived(i, 24, w.at[yo, x, zl])
        arrived(i, 25, w.at[yo, xm, zl])
        arrived(i, 26, w.at[yo, xp, zl])
        arrived(i, 27, w.at[yo, xo, zl])
        arrived(i, 28, w.at[y, xo, other])
        arrived(i, 29, w.at[ym, xo, other])
        arrived(i, 30, w.at[yp, xo, other])
        arrived(i, 31, w.at[yo, xo, other])

    def ring_own(j):
        a, b = rings[j]
        for k, to in enumerate((to_zp, to_zm, mate)):
            go(lambda k=k, to=to: ring_posts[j](k, a, slot_of(b, z, core), to))

    def ring_on(j):
        b = rings[j][1]
        blk = lambda: slot_of(b, zm, core)
        ring_arrived(j, 0, blk())
        go(lambda blk=blk: ring_posts[j](3, halves_of(blk())[0], halves_of(blk())[0], to_zp))
        go(lambda blk=blk: ring_posts[j](5, blk(), blk(), mate))
        blk = lambda: slot_of(b, zp, core)
        ring_arrived(j, 1, blk())
        go(lambda blk=blk: ring_posts[j](4, halves_of(blk())[1], halves_of(blk())[1], to_zm))
        go(lambda blk=blk: ring_posts[j](6, blk(), blk(), mate))

    def ring_far(j):
        blk = lambda: slot_of(rings[j][1], zo, core)
        ring_arrived(j, 3, halves_of(blk())[0])
        ring_arrived(j, 4, halves_of(blk())[1])
        go(lambda blk=blk: ring_posts[j](7, blk(), blk(), mate))

    def ring_last(j):
        b = rings[j][1]
        ring_arrived(j, 2, slot_of(b, z, 1 - core))
        ring_arrived(j, 5, slot_of(b, zm, 1 - core))
        ring_arrived(j, 6, slot_of(b, zp, 1 - core))
        ring_arrived(j, 7, slot_of(b, zo, 1 - core))

    kept = {}

    def keep(k, src, dst):
        make = lambda: pltpu.make_async_copy(src, dst, keep_sems.at[k])
        make().start()
        kept[k] = make

    def fetch(k, src, dst):
        fetched[k] = lambda: pltpu.make_async_copy(src, dst, local_sems.at[7 + k])
        fetched[k]().start()

    def fetch_for(i):
        if i == UP:
            own_copy(UP).wait()
            fetch(0, up_out, up_w)
        elif i == QKV:
            own_copy(QKV).wait()
            fetch(1, qkv_out, qkv_w)
        else:
            own_copy(5).wait()
            ring_last(1)
            fetch(2, dy_out, dy_v)

    def tables():
        lengths_copy().wait_recv()
        own_copy(6).wait()

        @pl.loop(0, 8)
        def _(k):
            g, part = k // 4, k % 4
            shape = (LANES, LANES)
            row = wide(lax.broadcasted_iota(jnp.int32, shape, 0) + part * LANES)
            lane = lax.broadcasted_iota(jnp.int32, shape, 1)
            start = jnp.zeros(shape, WIDE)
            end = jnp.zeros((1, LANES), WIDE)
            for s in range(4):
                end = end + len_v[g, s : s + 1, :]
                start = jnp.where(row >= end, jnp.broadcast_to(end, shape), start)
            half_rot = ROT // 2
            step = wide(lane % half_rot) * (-2.0 * math.log(10000.0) / ROT)
            angle = (row - start) * jnp.exp(step)
            sine = jnp.sin(angle)
            rows = cols(k, LANES)
            turn[0, rows] = jnp.where(lane < ROT, jnp.cos(angle), 1.0)
            turn[1, rows] = jnp.where(lane < half_rot, -sine, jnp.where(lane < ROT, sine, 0.0))

        for g in range(2):
            column = wide(lax.broadcasted_iota(jnp.int32, (1, GROUP), 1))
            start = jnp.zeros((1, GROUP), WIDE)
            end = jnp.zeros((1, LANES), WIDE)
            for r in range(4):
                end = end + len_v[g, r : r + 1, :]
                ends = jnp.concatenate([end] * (GROUP // LANES), axis=1)
                start = jnp.where(column >= ends, ends, start)
            begin[g : g + 1, :] = start

        keep(0, turn, turn_out)

    def vectors_x():
        own_copy(VEC).wait()
        arrived(VEC, 32, vec_w.at[y, x, other])
        for k in range(3):
            go(lambda k=k: posts[VEC](k, vec_w.at[y, x], vec_w.at[y, x], line_x[k]))

    def vectors_y():
        for k in range(3):
            arrived(VEC, k, vec_w.at[y, x])
        for k in range(3):
            go(lambda k=k: posts[VEC](3 + k, vec_w.at[y], vec_w.at[y], line_y[k]))

    def vectors():
        for k in range(3):
            arrived(VEC, 3 + k, vec_w.at[y])
        for p in range(RING_SIZE * RING_SIZE):
            lead, tail = vec_w[p // RING_SIZE, p % RING_SIZE, 0], vec_w[p // RING_SIZE, p % RING_SIZE, 1]
            vecs_out[:, p * LANES : (p + 1) * LANES] = lead + pltpu.roll(tail, LANES // 2, 1)

    def norm(zz, cc):
        b = (zz % 2) * RING_SIZE + (zz // 2) * 2 + cc

        @pl.loop(0, 4)
        def _(k):
            v = wide(xv[zz % 2, (zz // 2) * 2 + cc, cols(k, 32)])
            centred = v - jnp.mean(v, axis=-1, keepdims=True)
            var = jnp.mean(centred * centred, axis=-1, keepdims=True)
            u = centred * lax.rsqrt(var + norm_eps)
            to = cols(b * 4 + k, 32)
            unit[to] = u.astype(LOW)
            one[to] = (u * vecs_out[0:1, :] + vecs_out[1:2, :]).astype(LOW)
            two[to] = (u * vecs_out[2:3, :] + vecs_out[3:4, :]).astype(LOW)

    def norms(k):
        if k == 0:
            own_copy(4).wait()
            norm(z, core)
        elif k == 1:
            ring_arrived(0, 2, slot_of(xv, z, 1 - core))
            norm(z, 1 - core)
        elif k == 2:
            norm(zm, core)
            norm(zp, core)
        elif k == 4:
            ring_arrived(0, 5, slot_of(xv, zm, 1 - core))
            norm(zm, 1 - core)
            ring_arrived(0, 6, slot_of(xv, zp, 1 - core))
            norm(zp, 1 - core)
        else:
            norm(zo, core)
            ring_arrived(0, 7, slot_of(xv, zo, 1 - core))
            norm(zo, 1 - core)

    def at_step(hooks, k):
        for due, entries in hooks.items():

            @pl.when(k == due)
            def _():
                for entry in entries:
                    act(*entry)

    def keep_rows():
        if 1 not in kept:
            keep(1, one, one_out)
            keep(2, two, two_out)
            keep(3, unit, unit_out)

    def gelu(pre, m, n):
        size = pre.shape[1]
        rows = pl.ds(m * GROUP, GROUP)
        at = pl.ds(pl.multiple_of(n * size + TILE, TILE), size)
        hidden = pre[...]
        cdf = 0.5 * (1.0 + lax.erf(hidden * inv_root_two))
        cat[rows, at] = (hidden * cdf).astype(LOW)
        bell = hidden * jnp.exp(-0.5 * hidden * hidden) * inv_root_tau
        slope[rows, at] = (cdf + bell).astype(LOW)

    def hidden_tiles(hooks):
        keep_rows()
        fetched[0]().wait()
        size = pre_one.shape[1]
        last = up_w.shape[-1] // size

        @pl.loop(0, last)
        def _(n):
            w = up_w[:, :, :, :, cols(n, size)].reshape(-1, size)
            bias = vecs_out[pl.ds(9 + head // 2, 1), cols((head % 2) * last + n, size)]
            at_step(hooks, 2 * n)
            gelu(pre_two, 1, (n + last - 1) % last)
            pre_one[...] = nn(two[0:GROUP], w) + bias
            at_step(hooks, 2 * n + 1)
            gelu(pre_one, 0, n)
            pre_two[...] = nn(two[GROUP:], w) + bias

        gelu(pre_two, 1, last - 1)
        slope[:, 0:TILE] = jnp.ones((2 * GROUP, TILE), LOW)
        keep(4, slope, slope_out)

    def project(hooks):
        keep_rows()
        fetched[1]().wait()

        @pl.loop(0, 2)
        def _(m):
            at_step(hooks, m)
            rows = cols(m, GROUP)
            all_three = nn(one[rows], qkv_w[...].reshape(-1, 3 * HD))
            for c in range(3):
                pre = all_three[:, c * HD : (c + 1) * HD] + vecs_out[4 + c : 5 + c, cols(head, HD)]
                if c < 2:
                    pre = turned(pre, turn[0, rows], turn[1, rows])
                heads[c, rows] = pre.astype(LOW)

        keep(5, heads, heads_out)

    def attend(hooks):
        @pl.loop(0, 2)
        def _(g):
            at_step(hooks, g)
            for part in range(2):
                rows, keys = cols(2 * g + part, TILE), pl.ds(cols(g, GROUP).start, (part + 1) * TILE)
                start = begin[pl.ds(g, 1), part * TILE : (part + 1) * TILE]
                columns = soft_columns(heads[0, rows], heads[1, keys], start, part * TILE)
                columns = columns.astype(LOW)
                soft[g, part, 0 : (part + 1) * TILE] = columns
                cat[rows, 0:HD] = nn(turn_over(eye, columns), heads[2, keys]).astype(LOW)

        keep(7, soft, soft_out)

    def od_grads(hooks):
        keep(6, cat, cat_out)
        fetched[2]().wait()
        flips = (flip_one, flip_two)

        def flip(to, k, e):
            tile = dy_v[:, :, :, cols(2 * k + e, TILE)].reshape(-1, TILE)
            to[e * TILE : (e + 1) * TILE, :] = turn_over(eye, tile)

        def staged(k, half):
            return pltpu.make_async_copy(stage.at[half], grad_out.at[k], stage_sems.at[half])

        for e in range(2):
            flip(flip_one, 0, e)

        @pl.loop(0, 2)
        def _(kk):
            for half in range(2):
                k = 2 * kk + half
                at_step(hooks, k)

                @pl.when(kk > 0)
                def _():
                    staged(k - 2, half).wait()

                for part, at in enumerate((WIDE_PART, REST)):
                    res = nn(flips[half][...], cat[:, at]).astype(LOW)
                    flip(flips[1 - half], (k + 1) % RING_SIZE, part)
                    stage[half, :, :, :, at] = res.reshape(RING_SIZE, 2, -1, at.stop - at.start)

                staged(k, half).start()

        for half in range(2):
            staged(2 + half, half).wait()

    fetched = {}
    def lengths_copy():
        return pltpu.make_async_remote_copy(
            src_ref=len_in,
            dst_ref=len_v.at[zl],
            send_sem=len_sems.at[0],
            recv_sem=len_sems.at[1],
            device_id=partner,
            device_id_type=MESH,
        )

    moves = {
        SWAP: swap,
        OWN: own_half,
        OTHER: other_half,
        ROUND_ONE_X: round_one_x,
        ROUND_ONE_Y: round_one_y,
        ROUND_TWO_A: round_two_a,
        ROUND_TWO_B: round_two_b,
        ROUND_TWO_C: round_two_c,
        ROUND_THREE: round_three,
        LAST_ROUND: last_round,
        RING: ring_own,
        RING_ON: ring_on,
        RING_FAR: ring_far,
        TABLES: tables,
        VECTORS_X: vectors_x,
        VECTORS_Y: vectors_y,
        VECTORS: vectors,
        NORM: norms,
        FETCH: fetch_for,
    }

    def act(kind, *args):
        moves[kind](*args)

    loops = {HIDDEN: hidden_tiles, PROJECT: project, ATTEND: attend, OD_GRADS: od_grads}
    lengths_copy().start()
    play(FORWARD_ORDER, loops, act)
    own_copy(3).wait()
    lengths_copy().wait_send()
    for make in started.values():
        make().wait_send()
    for make in kept.values():
        make().wait()


def forward(rows, cot, lengths, vectors, weights):
    tokens, model = rows.shape
    total = 2 * RING_SIZE * tokens
    up, qkv, out_w, down = weights
    owned = up.shape[0]
    widths = (LANES, up.shape[1] // 2, 3 * HD, (out_w.shape[1] + down.shape[1]) // 2)
    halves = [(2, 16, LANES), *((2, owned, w) for w in widths[1:])]
    plane = [(RING_SIZE, RING_SIZE, *h) for h in halves]
    cat_cols = widths[3]
    shape = jax.ShapeDtypeStruct
    out = [
        shape((2, RING_SIZE, tokens, model), LOW),
        shape(plane[1], LOW),
        shape(plane[2], LOW),
        shape(plane[3], LOW),
        shape((16, model), WIDE),
        shape((total, model), LOW),
        shape((total, model), LOW),
        shape((total, model), LOW),
        shape((3, total, HD), LOW),
        shape((total, cat_cols), LOW),
        shape((total, cat_cols), LOW),
        shape((2, total, LANES), WIDE),
        shape((2, 2, GROUP, TILE), LOW),
        shape(plane[3], LOW),
    ]
    specs = [VMEM if k == 4 else ANY for k in range(len(out))]
    return pl.pallas_call(
        forward_kernel,
        out_shape=out,
        in_specs=[ANY, ANY, pl.BlockSpec(memory_space=pltpu.SMEM), VMEM, ANY, ANY, ANY, ANY],
        out_specs=specs,
        scratch_shapes=[
            pltpu.VMEM((2, RING_SIZE, tokens, model), LOW),
            pltpu.VMEM((2, 8, LANES), WIDE),
            pltpu.VMEM(plane[0], WIDE),
            pltpu.VMEM((total, model), LOW),
            pltpu.VMEM((total, model), LOW),
            pltpu.VMEM((total, model), LOW),
            pltpu.VMEM((2, RING_SIZE, tokens, model), LOW),
            pltpu.VMEM(plane[1], LOW),
            pltpu.VMEM(plane[2], LOW),
            pltpu.VMEM((total, cat_cols), LOW),
            pltpu.VMEM((total, cat_cols), LOW),
            pltpu.VMEM((3, total, HD), LOW),
            pltpu.VMEM((2, total, LANES), WIDE),
            pltpu.VMEM((GROUP, total), LOW),
            pltpu.VMEM((GROUP, total), LOW),
            pltpu.VMEM((2, RING_SIZE, 2, owned, cat_cols), LOW),
            pltpu.VMEM((GROUP, GROUP), WIDE),
            pltpu.VMEM((GROUP, GROUP), WIDE),
            pltpu.VMEM((2, 2, GROUP, TILE), LOW),
            pltpu.VMEM((8, GROUP), WIDE),
            pltpu.VMEM((TILE, TILE), LOW),
            pltpu.VMEM((8, LANES), WIDE),
            pltpu.VMEM(halves[0], WIDE),
            *(pltpu.VMEM(h, LOW) for h in halves[1:]),
            *(pltpu.VMEM(w.shape, WIDE) for w in weights),
            pltpu.SemaphoreType.DMA((4, PLANE_MESSAGES)),
            pltpu.SemaphoreType.DMA((4, PLANE_MESSAGES)),
            pltpu.SemaphoreType.DMA((2, RING_MESSAGES)),
            pltpu.SemaphoreType.DMA((2, RING_MESSAGES)),
            pltpu.SemaphoreType.DMA((2,)),
            pltpu.SemaphoreType.DMA((10,)),
            pltpu.SemaphoreType.DMA((8,)),
            pltpu.SemaphoreType.DMA((2,)),
            pltpu.SemaphoreType.DMA((4,)),
        ],
        compiler_params=pltpu.CompilerParams(
            collective_id=0, has_side_effects=True, vmem_limit_bytes=62 * 2**20
        ),
        name="forward_and_gather",
    )(rows, cot, lengths, vectors, *weights)


def backward_kernel(
    dy_in, up_in, qkv_in, od_in, vecs, one_in, two_in, unit_in, heads_in, cat_in, slope_in,
    turn_in, soft_in, od_grad,
    own_od_out, own_up_out, own_qkv_out, swap_od, swap_up, swap_qkv, vec_out, u_zero_out, u_one_out,
    own_od, own_up, own_qkv, u_zero, u_one,
    up_grad, qkv_grad, dcat, cat, heads, turn, soft, flip_one, flip_two, vecg, vec_block,
    od_near, od_me, od_full, tiles, eye,
    part_zero, both_zero, zfar_zero, znear_zero, part_one, both_one, zfar_one, znear_one,
    far_od, near_od, far2_od, near2_od, out_od,
    far_up, near_up, far2_up, near2_up, out_up,
    far_qkv, near_qkv, far2_qkv, near2_qkv, out_qkv,
    vec_x, vec_y, vec_z, vec_row, vec_own,
    send, recv, z_send, z_recv, v_send, v_recv, load_sems, stream_sems, out_sems,
):
    y, x, z, core = place()
    zl = z % 2
    head = ((z // 2) * 2 + core) * 2 + zl
    other = 1 - zl
    partner = device(y, x, z + 1 - 2 * zl, core)
    xp, xm, yp, ym = around(x, 1), around(x, -1), around(y, 1), around(y, -1)
    zp, zm = around(z, 1), around(z, -1)
    xo, yo, zo = around(x, 2), around(y, 2), around(z, 2)
    to_x = (device(y, xp, z, core), device(y, xm, z, core))
    to_y = (device(yp, x, z, core), device(ym, x, z, core))
    to_z = (partner, device(y, x, around(z, 2 * zl - 1), core))
    mate = device(y, x, z, 1 - core)
    line_x = (to_x[0], device(y, xo, z, core), to_x[1])
    line_y = (to_y[0], device(yo, x, z, core), to_y[1])
    line_z = [mate]
    for k in (1, 2, 3):
        for c in (0, 1):
            line_z.append(device(y, x, around(z, k), (core + c) % 2))
    neighbours = [*line_x, *line_y, *line_z]
    greet(neighbours)

    def load(k, src, dst):
        copy = pltpu.make_async_copy(src, dst, load_sems.at[k])
        copy.start()
        return copy

    half_model = part_zero.shape[-1]
    loads = [load(0, slope_in, dcat)]
    for c in range(2):
        at = slice(c * half_model, (c + 1) * half_model)
        loads.append(load(1 + c, dy_in.at[:, :, :, :, at], part_zero.at[c]))
    od_loads = [load(13 + k, od_in.at[k], od_full.at[k]) for k in range(RING_SIZE)]
    near_loads = []
    for way, half in enumerate((zl, other)):
        for d in range(2):
            two = pl.ds(2 * d, 2)
            src = (two, (xp, xm)[d], half) if way == 0 else ((yp, ym)[d], two, half)
            near_loads.append(load(3 + 2 * way + d, od_grad.at[src], od_near.at[way, d]))
        every = pl.ds(0, RING_SIZE)
        src = (every, x, half) if way == 0 else (y, every, half)
        near_loads.append(load(7 + way, od_grad.at[src], od_me.at[way]))
    late = [
        load(9, heads_in, heads),
        load(10, turn_in, turn),
        load(11, cat_in, cat),
        load(12, soft_in, soft),
    ]
    meet(neighbours)

    started, note = {}, [None]

    def go(make):
        make().start()
        started[note[0]] = make

    g_ref = {OD: od_grad, UP: up_grad, QKV: qkv_grad}
    bufs = {
        OD: (far_od, near_od, far2_od, near2_od, out_od, own_od, swap_od),
        UP: (far_up, near_up, far2_up, near2_up, out_up, own_up, swap_up),
        QKV: (far_qkv, near_qkv, far2_qkv, near2_qkv, out_qkv, own_qkv, swap_qkv),
    }
    posts = {i: mailbox(note, send, recv, i - 1) for i in (UP, QKV, OD)}
    z_posts = [mailbox(note, z_send, z_recv, j) for j in range(6)]
    v_post = mailbox(note, v_send, v_recv)

    def arrived(i, k, ref):
        posts[i](k, ref, ref, mate).wait_recv()

    def z_arrived(j, k, ref):
        z_posts[j](k, ref, ref, mate).wait_recv()

    halves = (zl, other)
    first_to, second_to = (to_x, to_y), (to_y, to_x)
    first = ((xp, xm, xo, x), (yp, ym, yo, y))
    second = ((yp, ym, yo, y), (xp, xm, xo, x))
    pair = (pl.ds(0, 2), pl.ds(2, 2))
    part_rows = (pl.ds(0, 32), pl.ds(32, 32))

    def block(i, way, along, across):
        if way == 0:
            return g_ref[i].at[across, along, halves[0]]
        return g_ref[i].at[along, across, halves[1]]

    def near_value(i, way, d, k):
        if i == OD:
            return od_near[way, d, k]
        return block(i, way, first[way][d], k + 2 * d)[...]

    def me_value(i, way, k, rows):
        if i == OD:
            return od_me[way, k, rows]
        return block(i, way, first[way][3], k).at[rows][...]

    def send_first(i):
        far, near = bufs[i][:2]
        for way in range(2):
            for d in range(2):
                go(
                    lambda way=way, d=d: posts[i](
                        way * 12 + d,
                        block(i, way, first[way][2], pair[d]),
                        far.at[way, d],
                        first_to[way][d],
                    )
                )
        for way in range(2):
            for d in range(2):
                go(
                    lambda way=way, d=d: posts[i](
                        way * 12 + 2 + d,
                        block(i, way, first[way][d], pair[1 - d]),
                        near.at[way, d, pair[1 - d]],
                        first_to[way][d],
                    )
                )

    def send_near(i, way):
        far, near = bufs[i][:2]
        for d in range(2):
            arrived(i, way * 12 + d, far.at[way, d])
            for k in range(2):
                far[way, d, k] = far[way, d, k] + near_value(i, way, d, k)
            go(
                lambda d=d: posts[i](
                    way * 12 + 4 + d, far.at[way, d], near.at[way, d, pair[d]], first_to[way][d]
                )
            )

    def send_second(i, way):
        far, near, far_two, near_two = bufs[i][:4]
        for d in range(2):
            arrived(i, way * 12 + 2 + d, near.at[way, d, pair[1 - d]])
            arrived(i, way * 12 + 4 + d, near.at[way, d, pair[d]])

        @pl.loop(0, 2 * RING_SIZE)
        def _(t):
            k, rows = t // 2, cols(t % 2, 32)
            total = near[way, 0, k, rows] + near[way, 1, k, rows]
            near[way, 0, k, rows] = total + me_value(i, way, k, rows)

        for d in range(2):
            go(
                lambda d=d: posts[i](
                    way * 12 + 6 + d,
                    near.at[way, 0, second[way][2], part_rows[d]],
                    far_two.at[way, d],
                    second_to[way][d],
                )
            )
        for d in range(2):
            go(
                lambda d=d: posts[i](
                    way * 12 + 8 + d,
                    near.at[way, 0, second[way][d], part_rows[1 - d]],
                    near_two.at[way, d, part_rows[1 - d]],
                    second_to[way][d],
                )
            )

    def send_last(i, way):
        far, near, far_two, near_two = bufs[i][:4]
        for d in range(2):
            arrived(i, way * 12 + 6 + d, far_two.at[way, d])
            rows = part_rows[d]
            far_two[way, d] = far_two[way, d] + near[way, 0, second[way][d], rows]
            go(
                lambda d=d: posts[i](
                    way * 12 + 10 + d,
                    far_two.at[way, d],
                    near_two.at[way, d, part_rows[d]],
                    second_to[way][d],
                )
            )

    def finish(i, way):
        near, near_two, out, mine, swapped = (bufs[i][k] for k in (1, 3, 4, 5, 6))
        for d in range(2):
            arrived(i, way * 12 + 8 + d, near_two.at[way, d, part_rows[1 - d]])
            arrived(i, way * 12 + 10 + d, near_two.at[way, d, part_rows[d]])
        total = wide(near[way, 0, second[way][3]]) + wide(near_two[way, 0]) + wide(near_two[way, 1])
        if way == 1:
            out[...] = total.astype(LOW)
            go(lambda: posts[i](24, out, swapped, partner))
        else:
            mine[...] = total.astype(LOW)
            out_copy(i - 1).start()

    def z_bufs(j):
        if j < 2:
            return [r.at[j] for r in (part_zero, both_zero, zfar_zero, znear_zero)]
        return [r.at[j - 2] for r in (part_one, both_one, zfar_one, znear_one)]

    def z_rows(j):
        lead = 64 if j < 2 else 16
        return pl.ds(0, lead), pl.ds(lead, near_rows - lead)

    near_rows = znear_zero.shape[2]
    z_ends = (z + 1 - 2 * zl, around(z, 2 * zl - 1))

    def z_to_mate(j):
        go(lambda: z_posts[j](0, z_bufs(j)[0].at[:, :, 1 - core], z_bufs(j)[1], mate))

    def z_block(j, zz):
        return z_bufs(j)[1].at[zz % 2, zz // 2]

    def z_first(j):
        part, both, far, near = z_bufs(j)
        z_arrived(j, 0, both)

        @pl.loop(0, 8)
        def _(k):
            b, c, rows = k // 4, (k // 2) % 2, cols(k % 2, 64)
            both[b, c, rows] = both[b, c, rows] + part[b, c, core, rows]

        rows = z_rows(j)
        for d in range(2):
            go(
                lambda d=d: z_posts[j](
                    1 + d, z_block(j, zo).at[rows[d]], z_bufs(j)[2].at[rows[d]], to_z[d]
                )
            )
        for d in range(2):
            go(
                lambda d=d: z_posts[j](
                    3 + d,
                    z_block(j, z_ends[d]).at[rows[d]],
                    z_bufs(j)[3].at[d, rows[d]],
                    to_z[d],
                )
            )

    def z_second(j):
        part, both, far, near = z_bufs(j)
        rows = z_rows(j)
        for d in range(2):
            z_arrived(j, 1 + d, far.at[rows[d]])
            zz = z_ends[1 - d]
            far[rows[d]] = far[rows[d]] + both[zz % 2, zz // 2, rows[d]]
            go(
                lambda d=d: z_posts[j](
                    6 - d, z_bufs(j)[2].at[rows[d]], z_bufs(j)[3].at[1 - d, rows[d]], to_z[1 - d]
                )
            )

    def z_finish(j):
        part, both, far, near = z_bufs(j)
        rows = z_rows(j)
        for d in range(2):
            z_arrived(j, 3 + d, near.at[d, rows[d]])
            z_arrived(j, 5 + d, near.at[d, rows[1 - d]])
        out, at = (u_zero, j) if j < 2 else (u_one, j - 2)
        width = near.shape[-1]
        for k in range(2):
            rows = pl.ds(64 * k, 64)
            total = wide(both[zl, z // 2, rows]) + wide(near[0, rows]) + wide(near[1, rows])
            out[rows, at * width : (at + 1) * width] = total.astype(LOW)
        out_copy(3 + j).start()

    def at_step(hooks, k):
        for due, entries in hooks.items():

            @pl.when(k == due)
            def _():
                for entry in entries:
                    act(*entry)

    def out_copy(k):
        if k < 3:
            src, dst = ((own_up, own_up_out), (own_qkv, own_qkv_out), (own_od, own_od_out))[k]
        else:
            j = k - 3
            src, dst = (u_zero, u_zero_out) if j < 2 else (u_one, u_one_out)
            width = src.shape[1] // (2 if j < 2 else 4)
            at = pl.ds((j if j < 2 else j - 2) * width, width)
            src, dst = src.at[:, at], dst.at[:, at]
        return pltpu.make_async_copy(src, dst, out_sems.at[k])

    def cat_grads(hooks):
        for c in od_loads:
            c.wait()
        thirds = (slice(0, 512), slice(512, 1024), slice(1024, 1280))
        for step, (m, at) in enumerate(((m, at) for at in thirds for m in range(2))):
            for entry in hooks.get(step, ()):
                act(*entry)
            w = od_full[:, :, :, :, at].reshape(-1, at.stop - at.start)
            rows = pl.ds(m * GROUP, GROUP)
            grad = nn(part_zero[0, m].reshape(GROUP, -1), w[:half_model])
            grad = grad + nn(part_zero[1, m].reshape(GROUP, -1), w[half_model:])
            dcat[rows, at] = (grad * wide(dcat[rows, at])).astype(LOW)

    def weight_grads(hooks, sem, source, rights, to, bias):
        flips = (flip_one, flip_two)
        size = to.shape[-1] // len(rights)

        def copy(k, half):
            at = stream_sems.at[sem, half]
            return pltpu.make_async_copy(source.at[:, cols(k, GROUP)], tiles.at[half], at)

        def flip(half, e):
            at = slice(e * TILE, (e + 1) * TILE)
            flips[half][at, :] = turn_over(eye, tiles[half, :, at])

        for half in range(2):
            copy(half, half).start()
        copy(0, 0).wait()

        for e in range(2):
            flip(0, e)

        @pl.loop(0, 2)
        def _(kk):
            for half in range(2):
                k = 2 * kk + half
                at_step(hooks, k)
                if half == 0:
                    copy(k + 1, 1).wait()
                else:

                    @pl.when(kk == 0)
                    def _():
                        copy(k + 1, 0).wait()

                @pl.when(kk == 0)
                def _():
                    copy(k + 2, half).start()

                for n, right in enumerate(rights):
                    res = nn(flips[half][...], right[...])
                    row, at = bias(n)
                    vecg[row, at] = res[GROUP : GROUP + 1]
                    part = res[0:GROUP].astype(LOW)
                    to[k, :, :, :, n * size : (n + 1) * size] = part.reshape(RING_SIZE, 2, -1, size)
                for e in range(2):
                    flip(1 - half, e)

    def attend_back(hooks):
        @pl.loop(0, 2)
        def _(g):
            at_step(hooks, g)
            dkey, dvalue = [], []
            for part in range(2):
                rows, count = cols(2 * g + part, TILE), (part + 1) * TILE
                keys = pl.ds(cols(g, GROUP).start, count)
                columns = soft[g, part, 0:count]
                query, key, grad = heads[0, rows], heads[1, keys], dcat[rows, 0:HD]
                dsoft = nt(heads[2, keys], grad)
                inner = jnp.sum(wide(columns) * dsoft, axis=0, keepdims=True)
                dscore = (wide(columns) * (dsoft - inner)).astype(LOW)
                dquery = nn(turn_over(eye, dscore), key) * (HD**-0.5)
                heads[0, rows] = turned(dquery, turn[0, rows], -turn[1, rows]).astype(LOW)
                dkey.append(nn(dscore, query))
                dvalue.append(nn(columns, grad))
            for part in range(2):
                rows, at = cols(2 * g + part, TILE), slice(part * TILE, (part + 1) * TILE)
                whole_key, whole_value = dkey[1][at], dvalue[1][at]
                if part == 0:
                    whole_key, whole_value = whole_key + dkey[0], whole_value + dvalue[0]
                whole_key = turned(whole_key * (HD**-0.5), turn[0, rows], -turn[1, rows])
                heads[1, rows] = whole_key.astype(LOW)
                heads[2, rows] = whole_value.astype(LOW)

    def branch(hooks):
        @pl.loop(0, RING_SIZE)
        def _(k):
            at_step(hooks, k)
            w = od_full[k].reshape(GROUP, -1)
            for m in range(2):
                res = nt(cat[m * GROUP : (m + 1) * GROUP], w).astype(LOW)
                part_zero[k // 2, m, :, :, :, cols(k % 2, GROUP)] = res.reshape(2, 2, -1, GROUP)

    def norm_grads(hooks):
        up_at, qkv_at = slice(0, up_in.shape[-1]), slice(0, qkv_in.shape[-1])

        def copies(k, slot):
            return [
                pltpu.make_async_copy(
                    qkv_in.at[k], od_full.at[2 + slot, :, :, :, qkv_at], stream_sems.at[2, slot]
                ),
                pltpu.make_async_copy(
                    up_in.at[k], od_full.at[slot, :, :, :, up_at], stream_sems.at[3, slot]
                ),
                pltpu.make_async_copy(
                    unit_in.at[:, cols(k, GROUP)], tiles.at[slot], stream_sems.at[4, slot]
                ),
            ]

        def use(k, slot):
            at_step(hooks, k)
            w_one = od_full[2 + slot, :, :, :, qkv_at].reshape(GROUP, -1)
            w_two = od_full[slot, :, :, :, up_at].reshape(GROUP, -1)
            at = cols(k, GROUP)
            sums = [jnp.zeros((1, GROUP), WIDE)] * 4
            for part in range(4):
                m, inner = part // 2, part % 2
                rows = pl.ds(part * TILE, TILE)
                a = nt(heads[0, rows], w_one[:, 0:HD])
                for c in (1, 2):
                    a = a + nt(heads[c, rows], w_one[:, c * HD : (c + 1) * HD])
                b = nt(dcat[rows, TILE:], w_two)
                u = wide(tiles[slot, rows])
                res = (a * vecs[0:1, at] + b * vecs[2:3, at]).astype(LOW)
                part_one[k, m, inner] = res.reshape(2, -1, GROUP)
                new = (a * u, a, b * u, b)
                sums = [s + jnp.sum(v, axis=0, keepdims=True) for s, v in zip(sums, new)]
            for r in range(4):
                vecg[r : r + 1, at] = sums[r]

        streamed(RING_SIZE, copies, use)

    def vec_first():
        lane = lax.broadcasted_iota(jnp.int32, (16, LANES), 1)
        for p in range(RING_SIZE * RING_SIZE):
            v = vecg[:, p * LANES : (p + 1) * LANES]
            lead = jnp.where(lane < LANES // 2, v, 0.0)
            tail = jnp.where(lane < LANES // 2, pltpu.roll(v, LANES // 2, 1), 0.0)
            vec_block[p // RING_SIZE, p % RING_SIZE, 0] = lead
            vec_block[p // RING_SIZE, p % RING_SIZE, 1] = tail
        for k in range(3):
            go(lambda k=k: v_post(k, vec_block.at[:, around(x, k + 1)], vec_x.at[k], line_x[k]))

    def vec_second():
        for k in range(3):
            v_post(k, vec_x.at[k], vec_x.at[k], mate).wait_recv()
        for r in range(RING_SIZE):
            vec_row[r] = vec_block[r, x] + vec_x[0, r] + vec_x[1, r] + vec_x[2, r]
        for k in range(3):
            go(lambda k=k: v_post(3 + k, vec_row.at[around(y, k + 1)], vec_y.at[k], line_y[k]))

    def vec_third():
        for k in range(3):
            v_post(3 + k, vec_y.at[k], vec_y.at[k], mate).wait_recv()
        vec_own[...] = vec_row[y] + vec_y[0] + vec_y[1] + vec_y[2]
        for k in range(7):
            there = lambda k=k: zl if k == 0 else (z + (k + 1) // 2) % 2
            go(
                lambda k=k, there=there: v_post(
                    6 + k, vec_own.at[there()], vec_z.at[k], line_z[k]
                )
            )

    def vec_finish():
        total = vec_own[zl]
        for k in range(7):
            v_post(6 + k, vec_z.at[k], vec_z.at[k], mate).wait_recv()
            total = total + vec_z[k]
        vec_out[...] = total

    def wait_loads():
        vecg[...] = jnp.zeros(vecg.shape, WIDE)
        fill_eye(eye)
        for ref in (flip_one, flip_two):
            ref[GROUP:, :] = jnp.ones((16, ref.shape[1]), LOW)
        for c in loads:
            c.wait()
        for c in range(2):
            total = jnp.sum(wide(part_zero[c, zl, z // 2, core]), axis=0, keepdims=True)
            for r in (7, 8):
                vecg[r : r + 1, c * half_model : (c + 1) * half_model] = total

    def up_weight_grads(hooks):
        for c in near_loads:
            c.wait()
        def bias(n):
            return pl.ds(9 + head // 2, 1), cols((head % 2) * 2 + n, GROUP)

        rights = [dcat.at[:, TILE + n * GROUP : TILE + (n + 1) * GROUP] for n in range(2)]
        weight_grads(hooks, 5, two_in, rights, up_grad, bias)
        for c in late:
            c.wait()

    def qkv_weight_grads(hooks):
        def bias(n):
            return pl.ds(4 + n, 1), cols(head, HD)

        weight_grads(hooks, 6, one_in, [heads.at[c] for c in range(3)], qkv_grad, bias)

    def settle():
        for key in list(started)[:-20]:
            started.pop(key)().wait_send()

    moves = {
        SETTLE: settle,
        FIRST: send_first,
        NEAR: send_near,
        SECOND: send_second,
        FAR_SIDE: send_last,
        FINISH: finish,
        Z_MATE: z_to_mate,
        Z_FIRST: z_first,
        Z_SECOND: z_second,
        Z_FINISH: z_finish,
        LOADS: wait_loads,
        VEC_ONE: vec_first,
        VEC_TWO: vec_second,
        VEC_THREE: vec_third,
    }

    def act(kind, *args):
        moves[kind](*args)

    loops = {
        CAT_GRADS: cat_grads,
        UP_GRADS: up_weight_grads,
        BRANCH: branch,
        ATTEND_BACK: attend_back,
        QKV_GRADS: qkv_weight_grads,
        NORM_GRADS: norm_grads,
    }
    play(BACKWARD_ORDER, loops, act)
    vec_finish()
    for i in (UP, QKV, OD):
        arrived(i, 24, bufs[i][6])
    for k in range(9):
        out_copy(k).wait()
    for make in started.values():
        make().wait_send()


def backward(held):
    dy, up_full, qkv_full, od_full, vecs, one, two, unit, heads, cat, slope, turn, soft, _ = held
    total, model = one.shape
    tokens = dy.shape[2]
    owned = od_full.shape[3]
    widths = [w.shape[-1] for w in (od_full, up_full, qkv_full)]
    shape = jax.ShapeDtypeStruct
    out = [shape((owned, w), LOW) for w in widths]
    out += [shape((owned, w), LOW) for w in widths]
    out += [shape((16, LANES), WIDE)]
    out += [shape((tokens, model), LOW)] * 2
    plane = (RING_SIZE, RING_SIZE, 2, owned)
    scratch = [pltpu.VMEM((owned, w), LOW) for w in widths]
    scratch += [pltpu.VMEM((tokens, model), LOW)] * 2
    scratch += [
        pltpu.VMEM((*plane, widths[1]), LOW),
        pltpu.VMEM((*plane, widths[2]), LOW),
        pltpu.VMEM(slope.shape, LOW),
        pltpu.VMEM(cat.shape, LOW),
        pltpu.VMEM(heads.shape, LOW),
        pltpu.VMEM(turn.shape, WIDE),
        pltpu.VMEM(soft.shape, LOW),
        pltpu.VMEM((GROUP + 16, total), LOW),
        pltpu.VMEM((GROUP + 16, total), LOW),
        pltpu.VMEM((16, model), WIDE),
        pltpu.VMEM((RING_SIZE, RING_SIZE, 2, 16, LANES), WIDE),
        pltpu.VMEM((2, 2, 2, owned, widths[0]), LOW),
        pltpu.VMEM((2, RING_SIZE, owned, widths[0]), LOW),
        pltpu.VMEM((*plane, widths[0]), LOW),
        pltpu.VMEM((2, total, GROUP), LOW),
        pltpu.VMEM((TILE, TILE), LOW),
    ]
    for n in (2, 4):
        w = model // n
        scratch += [
            pltpu.VMEM((n, 2, 2, 2, tokens, w), LOW),
            pltpu.VMEM((n, 2, 2, tokens, w), LOW),
            pltpu.VMEM((n, tokens, w), LOW),
            pltpu.VMEM((n, 2, tokens, w), LOW),
        ]
    for w in widths:
        scratch += [
            pltpu.VMEM((2, 2, 2, owned, w), LOW),
            pltpu.VMEM((2, 2, RING_SIZE, owned, w), LOW),
            pltpu.VMEM((2, 2, owned // 2, w), LOW),
            pltpu.VMEM((2, 2, owned, w), LOW),
            pltpu.VMEM((owned, w), LOW),
        ]
    scratch += [
        pltpu.VMEM((3, RING_SIZE, 2, 16, LANES), WIDE),
        pltpu.VMEM((3, 2, 16, LANES), WIDE),
        pltpu.VMEM((7, 16, LANES), WIDE),
        pltpu.VMEM((RING_SIZE, 2, 16, LANES), WIDE),
        pltpu.VMEM((2, 16, LANES), WIDE),
        pltpu.SemaphoreType.DMA((3, 25)),
        pltpu.SemaphoreType.DMA((3, 25)),
        pltpu.SemaphoreType.DMA((6, 7)),
        pltpu.SemaphoreType.DMA((6, 7)),
        pltpu.SemaphoreType.DMA((13,)),
        pltpu.SemaphoreType.DMA((13,)),
        pltpu.SemaphoreType.DMA((17,)),
        pltpu.SemaphoreType.DMA((7, 2)),
        pltpu.SemaphoreType.DMA((9,)),
    ]
    specs = [VMEM if k == 4 else ANY for k in range(14)]
    return pl.pallas_call(
        backward_kernel,
        out_shape=out,
        in_specs=specs,
        out_specs=[VMEM if k == 6 else ANY for k in range(len(out))],
        scratch_shapes=scratch,
        compiler_params=pltpu.CompilerParams(
            collective_id=1, has_side_effects=True, vmem_limit_bytes=63 * 2**20
        ),
        name="backward_and_reduce",
    )(dy.reshape(2, 2, 2, tokens, model), *held[1:])


def adamw(weight, gradient, moment, square, step_rate, decay_rate):
    moment_new = beta_first * moment + (1.0 - beta_first) * gradient
    square_new = beta_second * square + (1.0 - beta_second) * gradient * gradient
    first_fix = 1.0 / (1.0 - beta_first**UPDATE_STEP)
    second_fix = 1.0 / (1.0 - beta_second**UPDATE_STEP)
    fixed = square_new * second_fix
    below = fixed * lax.rsqrt(fixed) + adam_eps
    inverse = pl.reciprocal(below, approx=True)
    inverse = inverse * (2.0 - below * inverse)
    direction = moment_new * first_fix * inverse
    weight_new = weight - step_rate * (direction + decay_rate * weight)
    return (weight_new, moment_new, square_new)


def update_kernel(*refs):
    (own_od, own_up, own_qkv, swap_od, swap_up, swap_qkv, vec_sum, u_zero, u_one, x_in, dy_in) = refs[:11]
    vecs, state, outs = refs[11], refs[12:27], refs[27:44]
    grads, rows_in, held = refs[44:50], refs[50:54], refs[54:69]
    block_v, grad_v, in_sems, out_sems = refs[69:]
    zl = lax.axis_index("dp") % 2
    started = []

    def load(src, dst):
        copy = pltpu.make_async_copy(src, dst, in_sems.at[len(started)])
        copy.start()
        started.append(copy)
        return copy

    stored = []

    def store(src, dst):
        copy = pltpu.make_async_copy(src, dst, out_sems.at[len(stored)])
        copy.start()
        stored.append(copy)

    sources = (own_od, own_up, own_qkv, swap_od, swap_up, swap_qkv)
    waits = {}
    for i, parts in ((2, (1, 4)), (0, (2, 5)), (1, (0, 3)), (3, ())):
        waits[i] = [load(sources[k], grads[k]) for k in parts]
        waits[i] += [load(state[3 * i + k], held[3 * i + k]) for k in range(3)]
    row_waits = [load(a, b) for a, b in zip((x_in, u_zero, u_one, dy_in), rows_in)]
    vec_waits = [load(state[12 + k], held[12 + k]) for k in range(3)]

    def new(i, at, gradient, rate, decay):
        three = held[3 * i : 3 * i + 3]
        weight, moment, square = (r[at] for r in three)
        for r, v in zip(three, adamw(weight, gradient, moment, square, rate, decay)):
            r[at] = v

    def done(i):
        for k in range(3):
            store(held[3 * i + k], outs[2 + 3 * i + k])

    def part(k, h, at):
        return wide(jnp.where(zl == h, grads[k][at], grads[k + 3][at]))

    def rows_of(k, size):
        return pl.ds(pl.multiple_of(k * size, size), size)

    for c in waits[2]:
        c.wait()

    @pl.loop(0, 4)
    def _(k):
        rows = rows_of(k, 16)
        for h in range(2):
            n = grads[1].shape[1]
            new(2, (rows, slice(h * n, (h + 1) * n)), part(1, h, (rows, slice(0, n))), matrix_rate, matrix_decay)

    done(2)
    for c in waits[0]:
        c.wait()
    for c in range(3):

        @pl.loop(0, 2)
        def _(k):
            rows = rows_of(k, 32)
            for h in range(2):
                g = part(2, h, (rows, slice(c * HD, (c + 1) * HD)))
                new(0, (c, rows, slice(h * HD, (h + 1) * HD)), g, matrix_rate, matrix_decay)

    done(0)
    for c in (*waits[1], *waits[3]):
        c.wait()

    @pl.loop(0, 4)
    def _(k):
        rows = rows_of(k, 16)
        n = grads[0].shape[1] - HD
        for h in range(2):
            g = part(0, h, (rows, slice(0, HD)))
            new(1, (rows, slice(h * HD, (h + 1) * HD)), g, matrix_rate, matrix_decay)
            g = part(0, h, (rows, slice(HD, HD + n)))
            new(3, (rows, slice(h * n, (h + 1) * n)), g, matrix_rate, matrix_decay)

    done(1)
    done(3)
    for c in (*row_waits, *vec_waits):
        c.wait()
    x_v, zero_v, one_v, dy_v = rows_in

    @pl.loop(0, 4)
    def _(k):
        rows = rows_of(k, 32)
        v = wide(x_v[rows])
        block_v[rows] = (v + wide(zero_v[rows]) + vecs[7:8, :] + vecs[8:9, :]).astype(LOW)
        centred = v - jnp.mean(v, axis=-1, keepdims=True)
        scale = lax.rsqrt(jnp.mean(centred * centred, axis=-1, keepdims=True) + norm_eps)
        unit = centred * scale
        g = wide(one_v[rows])
        g = g - jnp.mean(g, axis=-1, keepdims=True) - unit * jnp.mean(g * unit, axis=-1, keepdims=True)
        grad_v[rows] = wide(dy_v[rows]) + scale * g

    store(block_v, outs[0])
    store(grad_v, outs[1])
    at = (slice(None), slice(None))
    shape = held[12].shape
    new(4, at, vec_sum[0 : shape[0], 0 : shape[1]], vector_rate, 0.0)
    done(4)
    for c in stored:
        c.wait()


def update(reduced, rows, cot, vecs, state):
    own, vec_sum, sums = reduced[:6], reduced[6], reduced[7:]
    shape = jax.ShapeDtypeStruct
    out = [shape(rows.shape, LOW), shape(rows.shape, WIDE)]
    out += [shape(a.shape, WIDE) for a in state]
    scratch = [pltpu.VMEM(a.shape, a.dtype) for a in (*own, rows, *sums, cot, *state)]
    scratch += [
        pltpu.VMEM(rows.shape, LOW),
        pltpu.VMEM(rows.shape, WIDE),
        pltpu.SemaphoreType.DMA((25,)),
        pltpu.SemaphoreType.DMA((17,)),
    ]
    specs = [ANY] * 6 + [VMEM] + [ANY] * 4 + [VMEM] + [ANY] * 15
    return pl.pallas_call(
        update_kernel,
        out_shape=out,
        in_specs=specs,
        out_specs=[ANY] * len(out),
        scratch_shapes=scratch,
        compiler_params=pltpu.CompilerParams(vmem_limit_bytes=63 * 2**20),
        name="update",
    )(*own, vec_sum, *sums, rows, cot, vecs, *state)


def local(
    inputs,
    cotangent,
    lengths,
    qkv_weight,
    out_weight,
    up_weight,
    down_weight,
    norm_vectors,
    qkv_mean,
    qkv_square,
    out_mean,
    out_square,
    up_mean,
    up_square,
    down_mean,
    down_square,
    vector_mean,
    vector_square,
):
    weights = (up_weight, qkv_weight, out_weight.T, down_weight.T)
    held = forward(inputs, cotangent, lengths, norm_vectors, weights)
    state = (
        *(qkv_weight, qkv_mean, qkv_square),
        *(out_weight.T, out_mean.T, out_square.T),
        *(up_weight, up_mean, up_square),
        *(down_weight.T, down_mean.T, down_square.T),
        *(norm_vectors, vector_mean, vector_square),
    )
    out = list(update(backward(held), inputs, cotangent, held[4], state))
    for k in (5, 6, 7, 11, 12, 13):
        out[k] = out[k].T
    return tuple(out)


def solution(mesh):
    placed = (
        P(("dp", "tensor"), None),
        P(("dp", "tensor"), None),
        P("dp", None),
        P(None, "dp", "tensor"),
        P("tensor", "dp"),
        P("dp", "tensor"),
        P("tensor", "dp"),
        P(None, "dp"),
        P(None, "dp", "tensor"),
        P(None, "dp", "tensor"),
        P("tensor", "dp"),
        P("tensor", "dp"),
        P("dp", "tensor"),
        P("dp", "tensor"),
        P("tensor", "dp"),
        P("tensor", "dp"),
        P(None, "dp"),
        P(None, "dp"),
    )
    return jax.shard_map(
        local,
        mesh=mesh,
        in_specs=placed,
        out_specs=(
            P(("dp", "tensor"), None),
            P(("dp", "tensor"), None),
            P(None, "dp", "tensor"),
            P(None, "dp", "tensor"),
            P(None, "dp", "tensor"),
            P("tensor", "dp"),
            P("tensor", "dp"),
            P("tensor", "dp"),
            P("dp", "tensor"),
            P("dp", "tensor"),
            P("dp", "tensor"),
            P("tensor", "dp"),
            P("tensor", "dp"),
            P("tensor", "dp"),
            P(None, "dp"),
            P(None, "dp"),
            P(None, "dp"),
        ),
        check_vma=False,
    )
```

```python
import functools
import math

import jax
import jax.numpy as jnp
from jax import lax
from jax.experimental import pallas as pl
from jax.experimental.pallas import tpu as pltpu
from jax.sharding import PartitionSpec as P

HD = 256
ROT = 64
UPDATE_STEP = 10
RING_SIZE = 4


norm_eps = 1e-05
beta_first = 0.9
beta_second = 0.95
adam_eps = 1e-08
matrix_rate = 0.02
vector_rate = 0.2
matrix_decay = 0.01
masked_score = -1e30
inv_root_two = 1.0 / math.sqrt(2.0)
inv_root_tau = 1.0 / math.sqrt(2.0 * math.pi)

MESH = pl.DeviceIdType.MESH
ANY = pl.BlockSpec(memory_space=pl.ANY)
VMEM = pl.BlockSpec(memory_space=pltpu.VMEM)


def place():
    dp, tensor = lax.axis_index("dp"), lax.axis_index("tensor")
    z = (tensor // 2) * 2 + dp % 2
    return dp // 8, (dp // 2) % RING_SIZE, z, tensor % 2


def device(y, x, z, core):
    return ((y * RING_SIZE + x) * 2 + z % 2, (z // 2) * 2 + core)


def around(i, step):
    return (i + step + RING_SIZE) % RING_SIZE


def greet(devices):
    barrier = pltpu.get_barrier_semaphore()
    for d in devices:
        pl.semaphore_signal(barrier, inc=1, device_id=d, device_id_type=MESH)


def meet(devices):
    pl.semaphore_wait(pltpu.get_barrier_semaphore(), len(devices))


def mailbox(note, send, recv, *lead):
    def post(k, src, dst, to):
        note[0] = (id(send), *lead, k)
        return pltpu.make_async_remote_copy(
            src_ref=src,
            dst_ref=dst,
            send_sem=send.at[(*lead, k)],
            recv_sem=recv.at[(*lead, k)],
            device_id=to,
            device_id_type=MESH,
        )

    return post


LOW = jnp.bfloat16
WIDE = jnp.float32
GROUP = 512
TILE = 256
WIDE_PART, REST = slice(0, 768), slice(768, 1280)
LANES = 128
PLANE_MESSAGES = 33
RING_MESSAGES = 8


VEC, UP, QKV, OD = range(4)
DY = 3
(
    SWAP,
    OWN,
    OTHER,
    ROUND_ONE_X,
    ROUND_ONE_Y,
    ROUND_TWO_A,
    ROUND_TWO_B,
    ROUND_TWO_C,
    ROUND_THREE,
    LAST_ROUND,
    RING,
    RING_ON,
    RING_FAR,
    TABLES,
    VECTORS_X,
    VECTORS_Y,
    VECTORS,
    NORM,
    FETCH,
    HIDDEN,
    PROJECT,
    ATTEND,
    OD_GRADS,
) = range(23)
(
    FIRST,
    NEAR,
    SECOND,
    FAR_SIDE,
    FINISH,
    Z_MATE,
    Z_FIRST,
    Z_SECOND,
    Z_FINISH,
    LOADS,
    VEC_ONE,
    VEC_TWO,
    VEC_THREE,
    SETTLE,
    CAT_GRADS,
    UP_GRADS,
    BRANCH,
    ATTEND_BACK,
    QKV_GRADS,
    NORM_GRADS,
) = range(20)
FORWARD_ORDER = (
    (OWN, UP), (SWAP, UP), (SWAP, QKV), (SWAP, VEC), (RING, 0), (OWN, QKV), (OTHER, UP),
    (VECTORS_X,), (OTHER, QKV), (VECTORS_Y,), (SWAP, OD), (ROUND_ONE_X, UP), (ROUND_ONE_Y, UP),
    (TABLES,), (ROUND_ONE_X, QKV), (ROUND_ONE_Y, QKV), (VECTORS,), (RING_ON, 0),
    (ROUND_TWO_A, UP), (RING, 1), (ROUND_TWO_B, UP), (NORM, 0), (ROUND_TWO_C, UP), (NORM, 4),
    (NORM, 2), (ROUND_THREE, UP), (RING_FAR, 0), (NORM, 1), (ROUND_TWO_B, QKV), (OTHER, OD),
    (NORM, 6), (LAST_ROUND, UP), (FETCH, UP), (OWN, OD), (HIDDEN, 0), (ROUND_TWO_A, QKV),
    (ROUND_TWO_C, QKV), (RING_ON, 1), (HIDDEN, 1), (ROUND_THREE, QKV), (ROUND_ONE_Y, OD),
    (HIDDEN, 2), (ROUND_ONE_X, OD), (HIDDEN, 3), (RING_FAR, 1), (LAST_ROUND, QKV),
    (ROUND_TWO_A, OD), (FETCH, QKV), (PROJECT, 0), (PROJECT, 1), (ATTEND, 0), (FETCH, DY),
    (ROUND_TWO_B, OD), (ATTEND, 1), (ROUND_TWO_C, OD), (OD_GRADS, 0), (ROUND_THREE, OD),
    (OD_GRADS, 1), (OD_GRADS, 2), (OD_GRADS, 3), (LAST_ROUND, OD),
)
BACKWARD_ORDER = (
    (FIRST, OD), (LOADS,), (CAT_GRADS, 0), (CAT_GRADS, 1), (CAT_GRADS, 2), (CAT_GRADS, 3),
    (UP_GRADS, 0), (NEAR, OD, 1), (UP_GRADS, 1), (UP_GRADS, 2), (UP_GRADS, 3), (FIRST, UP),
    (BRANCH, 0), (BRANCH, 1), (Z_MATE, 0), (BRANCH, 2), (BRANCH, 3), (Z_MATE, 1),
    (ATTEND_BACK, 0), (Z_FIRST, 0), (NEAR, OD, 0), (ATTEND_BACK, 1), (QKV_GRADS, 0),
    (Z_SECOND, 0), (QKV_GRADS, 1), (Z_FIRST, 1), (SECOND, OD, 1), (QKV_GRADS, 2), (QKV_GRADS, 3),
    (FIRST, QKV), (NORM_GRADS, 0), (Z_MATE, 2), (Z_SECOND, 1), (FAR_SIDE, OD, 1), (NORM_GRADS, 1),
    (Z_MATE, 3), (Z_FIRST, 2), (NEAR, UP, 0), (NEAR, UP, 1), (NORM_GRADS, 2), (Z_FIRST, 3),
    (NEAR, QKV, 1), (Z_MATE, 4), (Z_SECOND, 2), (NORM_GRADS, 3), (Z_FINISH, 0), (FINISH, OD, 1),
    (Z_FIRST, 4), (Z_MATE, 5), (SECOND, UP, 1), (VEC_ONE,), (SECOND, OD, 0), (Z_SECOND, 3),
    (NEAR, QKV, 0), (SECOND, UP, 0), (Z_FIRST, 5), (Z_SECOND, 4), (FAR_SIDE, OD, 0),
    (FAR_SIDE, UP, 1), (VEC_TWO,), (SECOND, QKV, 1), (Z_FINISH, 2), (Z_FINISH, 1), (VEC_THREE,),
    (Z_SECOND, 5), (FAR_SIDE, UP, 0), (FINISH, UP, 1), (FAR_SIDE, QKV, 1), (SECOND, QKV, 0),
    (FINISH, QKV, 1), (Z_FINISH, 3), (FINISH, UP, 0), (Z_FINISH, 4), (FINISH, OD, 0), (SETTLE,),
    (FAR_SIDE, QKV, 0), (Z_FINISH, 5), (FINISH, QKV, 0),
)


def wide(v):
    return v.astype(WIDE)


def nn(a, b):
    return jnp.dot(a, b, preferred_element_type=WIDE)


def nt(a, b):
    return lax.dot_general(a, b, (((1,), (1,)), ((), ())), preferred_element_type=WIDE)


def turn_over(eye, v):
    return nt(eye[...], v).astype(LOW)


def fill_eye(eye):
    row = lax.broadcasted_iota(jnp.int32, eye.shape, 0)
    eye[...] = wide(row == lax.broadcasted_iota(jnp.int32, eye.shape, 1)).astype(LOW)


def cols(k, size):
    return pl.ds(pl.multiple_of(k * size, size), size)


def turned(v, cos_table, sin_table):
    first = v[:, :LANES]
    lane = lax.broadcasted_iota(jnp.int32, first.shape, 1)
    swapped = jnp.where(
        lane < ROT // 2,
        pltpu.roll(first, LANES - ROT // 2, 1),
        pltpu.roll(first, ROT // 2, 1),
    )
    return jnp.concatenate([first * cos_table + swapped * sin_table, v[:, LANES:]], axis=1)


def soft_columns(query, key, start, first):
    scores = nt(key, query) * (HD**-0.5)
    key_at = lax.broadcasted_iota(jnp.int32, scores.shape, 0)
    query_at = lax.broadcasted_iota(jnp.int32, scores.shape, 1) + first
    allowed = (wide(key_at) >= start) & (key_at <= query_at)
    scores = jnp.where(allowed, scores, masked_score)
    powers = jnp.exp(scores - jnp.max(scores, axis=0, keepdims=True))
    return powers * (1.0 / jnp.sum(powers, axis=0, keepdims=True))


def streamed(count, copies, use):
    for c in copies(0, 0):
        c.start(priority=1)

    @pl.loop(0, count)
    def _(k):
        slot = lax.rem(k, 2)

        @pl.when(k + 1 < count)
        def _():
            for c in copies(k + 1, 1 - slot):
                c.start(priority=1)

        for c in copies(k, slot):
            c.wait()
        use(k, slot)


def play(order, loops, act):
    at = 0
    while at < len(order):
        kind = order[at][0]
        if kind not in loops:
            act(*order[at])
            at += 1
            continue
        hooks, due = {}, []
        end = max(k for k, entry in enumerate(order) if entry[0] == kind)
        for entry in order[at + 1 : end + 1]:
            if entry[0] == kind:
                if due:
                    hooks[entry[1]] = due
                due = []
            else:
                due.append(entry)
        loops[kind](hooks)
        at = end + 1


def forward_kernel(
    x_in, dy_in, lengths, vectors_in, up_in, qkv_in, out_in, down_in,
    dy_out, up_out, qkv_out, od_out, vecs_out, one_out, two_out, unit_out, heads_out, cat_out,
    slope_out, turn_out, soft_out, grad_out,
    xv, len_v, vec_w, one, two, unit, dy_v, up_w, qkv_w, cat, slope, heads, turn, flip_one, flip_two, stage,
    pre_one, pre_two, soft, begin, eye, len_in, vec_s, up_s, qkv_s, od_s, up_f, qkv_f, out_f, down_f,
    send, recv, ring_send, ring_recv, len_sems, local_sems, keep_sems, stage_sems, wide_sems,
):
    y, x, z, core = place()
    zl = z % 2
    tensor = (z // 2) * 2 + core
    head = tensor * 2 + zl
    other = 1 - zl
    partner = device(y, x, z + 1 - 2 * zl, core)
    xp, xm, yp, ym = around(x, 1), around(x, -1), around(y, 1), around(y, -1)
    zp, zm = around(z, 1), around(z, -1)
    xo, yo, zo = around(x, 2), around(y, 2), around(z, 2)
    to_xp, to_xm = device(y, xp, z, core), device(y, xm, z, core)
    to_yp, to_ym = device(yp, x, z, core), device(ym, x, z, core)
    to_zp, to_zm = device(y, x, zp, core), device(y, x, zm, core)
    mate = device(y, x, z, 1 - core)
    line_x = (to_xp, device(y, xo, z, core), to_xm)
    line_y = (to_yp, device(yo, x, z, core), to_ym)
    neighbours = [*line_x, *line_y, to_zp, to_zm, mate]
    greet(neighbours)

    wide_copies = [
        pltpu.make_async_copy(src, dst, wide_sems.at[k])
        for k, (src, dst) in enumerate(
            ((up_in, up_f), (qkv_in, qkv_f), (out_in, out_f), (down_in, down_f))
        )
    ]
    for c in wide_copies:
        c.start(priority=1)
    for r in range(4):
        len_in[r : r + 1, :] = jnp.full((1, LANES), lengths[0, r].astype(WIDE))
    len_in[4:8, :] = jnp.zeros((4, LANES), WIDE)
    fill_eye(eye)
    vec_s[...] = jnp.zeros(vec_s.shape, WIDE)
    vec = wide(vectors_in[...].astype(LOW))
    for h in range(2):
        vec_s[h, 0 : vec.shape[0], 0 : vec.shape[1]] = vec

    def prepare(i):
        if i == UP:
            wide_copies[0].wait()
            n = up_s.shape[-1]
            for h in range(2):
                up_s[h] = up_f[:, h * n : (h + 1) * n].astype(LOW)
        elif i == QKV:
            wide_copies[1].wait()
            for h in range(2):
                for c in range(3):
                    at = slice(c * HD, (c + 1) * HD)
                    qkv_s[h, :, at] = qkv_f[c, :, h * HD : (h + 1) * HD].astype(LOW)
        else:
            wide_copies[2].wait()
            wide_copies[3].wait()
            n = od_s.shape[-1] - HD
            for h in range(2):
                od_s[h, :, 0:HD] = out_f[:, h * HD : (h + 1) * HD].astype(LOW)
                od_s[h, :, HD:] = down_f[:, h * n : (h + 1) * n].astype(LOW)

    w_in = (vec_s, up_s, qkv_s, od_s)
    w_out = (vec_w, up_out, qkv_out, od_out)
    started, note = {}, [None]

    def go(make):
        make().start()
        started[note[0]] = make

    def own_copy(k):
        if k < 4:
            src, dst = w_in[k].at[zl], w_out[k].at[y, x, zl]
        elif k < 6:
            src, dst = rings[k - 4][0], rings[k - 4][1].at[zl, tensor]
        else:
            src, dst = len_in, len_v.at[zl]
        return pltpu.make_async_copy(src, dst, local_sems.at[k])

    rings = ((x_in, xv), (dy_in, dy_out))
    for k in (VEC, 4, 5, 6):
        own_copy(k).start(priority=1)
    for i in (UP, QKV, OD):
        prepare(i)
        own_copy(i).start(priority=1)
    meet(neighbours)

    posts = [mailbox(note, send, recv, i) for i in range(4)]
    ring_posts = [mailbox(note, ring_send, ring_recv, j) for j in range(2)]
    four = (to_xp, to_xm, to_yp, to_ym)

    def slot_of(ref, zz, cc):
        return ref.at[zz % 2, (zz // 2) * 2 + cc]

    def arrived(i, k, ref):
        posts[i](k, ref, ref, mate).wait_recv()

    def ring_arrived(j, k, ref):
        ring_posts[j](k, ref, ref, mate).wait_recv()

    def halves_of(blk):
        n = blk.shape[0] // 2
        return blk.at[pl.ds(0, n)], blk.at[pl.ds(n, n)]

    def swap(i):
        go(lambda: posts[i](32, w_in[i].at[other], w_out[i].at[y, x, zl], partner))

    def own_half(i):
        for d in range(4):
            go(lambda d=d: posts[i](d, w_in[i].at[zl], w_out[i].at[y, x, zl], four[d]))

    def other_half(i):
        mine = lambda: w_out[i].at[y, x, other]
        arrived(i, 32, mine())
        for d in range(4):
            go(lambda d=d: posts[i](4 + d, mine(), mine(), four[d]))

    def round_one_x(i):
        w = w_out[i]
        blk = lambda: w.at[y, xm, zl]
        arrived(i, 0, blk())
        go(lambda blk=blk: posts[i](8, halves_of(blk())[0], halves_of(blk())[0], to_xp))
        go(lambda blk=blk: posts[i](12, blk(), blk(), to_yp))
        go(lambda blk=blk: posts[i](13, blk(), blk(), to_ym))
        blk = lambda: w.at[y, xp, zl]
        arrived(i, 1, blk())
        go(lambda blk=blk: posts[i](9, halves_of(blk())[1], halves_of(blk())[1], to_xm))
        go(lambda blk=blk: posts[i](14, blk(), blk(), to_yp))
        go(lambda blk=blk: posts[i](15, blk(), blk(), to_ym))

    def round_one_y(i):
        w = w_out[i]
        blk = lambda: w.at[ym, x, other]
        arrived(i, 6, blk())
        go(lambda blk=blk: posts[i](10, halves_of(blk())[0], halves_of(blk())[0], to_yp))
        go(lambda blk=blk: posts[i](18, blk(), blk(), to_xp))
        go(lambda blk=blk: posts[i](19, blk(), blk(), to_xm))
        blk = lambda: w.at[yp, x, other]
        arrived(i, 7, blk())
        go(lambda blk=blk: posts[i](11, halves_of(blk())[1], halves_of(blk())[1], to_ym))
        go(lambda blk=blk: posts[i](20, blk(), blk(), to_xp))
        go(lambda blk=blk: posts[i](21, blk(), blk(), to_xm))

    def round_two_a(i):
        w = w_out[i]
        blk = lambda: w.at[ym, x, zl]
        arrived(i, 2, blk())
        go(lambda blk=blk: posts[i](24, blk(), blk(), to_yp))
        blk = lambda: w.at[y, xm, other]
        arrived(i, 4, blk())
        go(lambda blk=blk: posts[i](28, blk(), blk(), to_xp))

    def round_two_b(i):
        w = w_out[i]
        blk = lambda: w.at[y, xo, zl]
        arrived(i, 8, halves_of(blk())[0])
        arrived(i, 9, halves_of(blk())[1])
        go(lambda blk=blk: posts[i](16, blk(), blk(), to_yp))
        go(lambda blk=blk: posts[i](17, blk(), blk(), to_ym))
        blk = lambda: w.at[yo, x, other]
        arrived(i, 10, halves_of(blk())[0])
        arrived(i, 11, halves_of(blk())[1])
        go(lambda blk=blk: posts[i](22, blk(), blk(), to_xp))
        go(lambda blk=blk: posts[i](23, blk(), blk(), to_xm))

    def round_two_c(i):
        w = w_out[i]
        blk = lambda: w.at[ym, xm, zl]
        arrived(i, 12, blk())
        go(lambda blk=blk: posts[i](25, blk(), blk(), to_yp))
        blk = lambda: w.at[yp, xp, zl]
        arrived(i, 15, blk())
        go(lambda blk=blk: posts[i](26, blk(), blk(), to_ym))
        blk = lambda: w.at[ym, xm, other]
        arrived(i, 18, blk())
        go(lambda blk=blk: posts[i](29, blk(), blk(), to_xp))
        blk = lambda: w.at[yp, xp, other]
        arrived(i, 21, blk())
        go(lambda blk=blk: posts[i](30, blk(), blk(), to_xm))

    def round_three(i):
        w = w_out[i]
        blk = lambda: w.at[yp, xo, zl]
        arrived(i, 17, blk())
        go(lambda blk=blk: posts[i](27, blk(), blk(), to_ym))
        blk = lambda: w.at[yo, xp, other]
        arrived(i, 23, blk())
        go(lambda blk=blk: posts[i](31, blk(), blk(), to_xm))

    def last_round(i):
        if i == OD:
            for key in list(started)[:-20]:
                started.pop(key)().wait_send()
        w = w_out[i]
        arrived(i, 3, w.at[yp, x, zl])
        arrived(i, 5, w.at[y, xp, other])
        arrived(i, 13, w.at[yp, xm, zl])
        arrived(i, 14, w.at[ym, xp, zl])
        arrived(i, 16, w.at[ym, xo, zl])
        arrived(i, 19, w.at[ym, xp, other])
        arrived(i, 20, w.at[yp, xm, other])
        arrived(i, 22, w.at[yo, xm, other])
        arrived(i, 24, w.at[yo, x, zl])
        arrived(i, 25, w.at[yo, xm, zl])
        arrived(i, 26, w.at[yo, xp, zl])
        arrived(i, 27, w.at[yo, xo, zl])
        arrived(i, 28, w.at[y, xo, other])
        arrived(i, 29, w.at[ym, xo, other])
        arrived(i, 30, w.at[yp, xo, other])
        arrived(i, 31, w.at[yo, xo, other])

    def ring_own(j):
        a, b = rings[j]
        for k, to in enumerate((to_zp, to_zm, mate)):
            go(lambda k=k, to=to: ring_posts[j](k, a, slot_of(b, z, core), to))

    def ring_on(j):
        b = rings[j][1]
        blk = lambda: slot_of(b, zm, core)
        ring_arrived(j, 0, blk())
        go(lambda blk=blk: ring_posts[j](3, halves_of(blk())[0], halves_of(blk())[0], to_zp))
        go(lambda blk=blk: ring_posts[j](5, blk(), blk(), mate))
        blk = lambda: slot_of(b, zp, core)
        ring_arrived(j, 1, blk())
        go(lambda blk=blk: ring_posts[j](4, halves_of(blk())[1], halves_of(blk())[1], to_zm))
        go(lambda blk=blk: ring_posts[j](6, blk(), blk(), mate))

    def ring_far(j):
        blk = lambda: slot_of(rings[j][1], zo, core)
        ring_arrived(j, 3, halves_of(blk())[0])
        ring_arrived(j, 4, halves_of(blk())[1])
        go(lambda blk=blk: ring_posts[j](7, blk(), blk(), mate))

    def ring_last(j):
        b = rings[j][1]
        ring_arrived(j, 2, slot_of(b, z, 1 - core))
        ring_arrived(j, 5, slot_of(b, zm, 1 - core))
        ring_arrived(j, 6, slot_of(b, zp, 1 - core))
        ring_arrived(j, 7, slot_of(b, zo, 1 - core))

    kept = {}

    def keep(k, src, dst):
        make = lambda: pltpu.make_async_copy(src, dst, keep_sems.at[k])
        make().start(priority=1)
        kept[k] = make

    def fetch(k, src, dst):
        fetched[k] = lambda: pltpu.make_async_copy(src, dst, local_sems.at[7 + k])
        fetched[k]().start(priority=1)

    def fetch_for(i):
        if i == UP:
            own_copy(UP).wait()
            fetch(0, up_out, up_w)
        elif i == QKV:
            own_copy(QKV).wait()
            fetch(1, qkv_out, qkv_w)
        else:
            own_copy(5).wait()
            ring_last(1)
            fetch(2, dy_out, dy_v)

    def tables():
        lengths_copy().wait_recv()
        own_copy(6).wait()

        @pl.loop(0, 8)
        def _(k):
            g, part = k // 4, k % 4
            shape = (LANES, LANES)
            row = wide(lax.broadcasted_iota(jnp.int32, shape, 0) + part * LANES)
            lane = lax.broadcasted_iota(jnp.int32, shape, 1)
            start = jnp.zeros(shape, WIDE)
            end = jnp.zeros((1, LANES), WIDE)
            for s in range(4):
                end = end + len_v[g, s : s + 1, :]
                start = jnp.where(row >= end, jnp.broadcast_to(end, shape), start)
            half_rot = ROT // 2
            step = wide(lane % half_rot) * (-2.0 * math.log(10000.0) / ROT)
            angle = (row - start) * jnp.exp(step)
            sine = jnp.sin(angle)
            rows = cols(k, LANES)
            turn[0, rows] = jnp.where(lane < ROT, jnp.cos(angle), 1.0)
            turn[1, rows] = jnp.where(lane < half_rot, -sine, jnp.where(lane < ROT, sine, 0.0))

        for g in range(2):
            column = wide(lax.broadcasted_iota(jnp.int32, (1, GROUP), 1))
            start = jnp.zeros((1, GROUP), WIDE)
            end = jnp.zeros((1, LANES), WIDE)
            for r in range(4):
                end = end + len_v[g, r : r + 1, :]
                ends = jnp.concatenate([end] * (GROUP // LANES), axis=1)
                start = jnp.where(column >= ends, ends, start)
            begin[g : g + 1, :] = start

        keep(0, turn, turn_out)

    def vectors_x():
        own_copy(VEC).wait()
        arrived(VEC, 32, vec_w.at[y, x, other])
        for k in range(3):
            go(lambda k=k: posts[VEC](k, vec_w.at[y, x], vec_w.at[y, x], line_x[k]))

    def vectors_y():
        for k in range(3):
            arrived(VEC, k, vec_w.at[y, x])
        for k in range(3):
            go(lambda k=k: posts[VEC](3 + k, vec_w.at[y], vec_w.at[y], line_y[k]))

    def vectors():
        for k in range(3):
            arrived(VEC, 3 + k, vec_w.at[y])
        for p in range(RING_SIZE * RING_SIZE):
            lead, tail = vec_w[p // RING_SIZE, p % RING_SIZE, 0], vec_w[p // RING_SIZE, p % RING_SIZE, 1]
            vecs_out[:, p * LANES : (p + 1) * LANES] = lead + pltpu.roll(tail, LANES // 2, 1)

    def norm(zz, cc):
        b = (zz % 2) * RING_SIZE + (zz // 2) * 2 + cc

        @pl.loop(0, 4)
        def _(k):
            v = wide(xv[zz % 2, (zz // 2) * 2 + cc, cols(k, 32)])
            centred = v - jnp.mean(v, axis=-1, keepdims=True)
            var = jnp.mean(centred * centred, axis=-1, keepdims=True)
            u = centred * lax.rsqrt(var + norm_eps)
            to = cols(b * 4 + k, 32)
            unit[to] = u.astype(LOW)
            one[to] = (u * vecs_out[0:1, :] + vecs_out[1:2, :]).astype(LOW)
            two[to] = (u * vecs_out[2:3, :] + vecs_out[3:4, :]).astype(LOW)

    def norms(k):
        if k == 0:
            own_copy(4).wait()
            norm(z, core)
        elif k == 1:
            ring_arrived(0, 2, slot_of(xv, z, 1 - core))
            norm(z, 1 - core)
        elif k == 2:
            norm(zm, core)
            norm(zp, core)
        elif k == 4:
            ring_arrived(0, 5, slot_of(xv, zm, 1 - core))
            norm(zm, 1 - core)
            ring_arrived(0, 6, slot_of(xv, zp, 1 - core))
            norm(zp, 1 - core)
        else:
            norm(zo, core)
            ring_arrived(0, 7, slot_of(xv, zo, 1 - core))
            norm(zo, 1 - core)

    def at_step(hooks, k):
        for due, entries in hooks.items():

            @pl.when(k == due)
            def _():
                for entry in entries:
                    act(*entry)

    def keep_rows():
        if 1 not in kept:
            keep(1, one, one_out)
            keep(2, two, two_out)
            keep(3, unit, unit_out)

    def gelu(pre, m, n):
        size = pre.shape[1]
        rows = pl.ds(m * GROUP, GROUP)
        at = pl.ds(pl.multiple_of(n * size + TILE, TILE), size)
        hidden = pre[...]
        cdf = 0.5 * (1.0 + lax.erf(hidden * inv_root_two))
        cat[rows, at] = (hidden * cdf).astype(LOW)
        bell = hidden * jnp.exp(-0.5 * hidden * hidden) * inv_root_tau
        slope[rows, at] = (cdf + bell).astype(LOW)

    def hidden_tiles(hooks):
        keep_rows()
        fetched[0]().wait()
        size = pre_one.shape[1]
        last = up_w.shape[-1] // size

        @pl.loop(0, last)
        def _(n):
            w = up_w[:, :, :, :, cols(n, size)].reshape(-1, size)
            bias = vecs_out[pl.ds(9 + head // 2, 1), cols((head % 2) * last + n, size)]
            at_step(hooks, 2 * n)
            gelu(pre_two, 1, (n + last - 1) % last)
            pre_one[...] = nn(two[0:GROUP], w) + bias
            at_step(hooks, 2 * n + 1)
            gelu(pre_one, 0, n)
            pre_two[...] = nn(two[GROUP:], w) + bias

        gelu(pre_two, 1, last - 1)
        slope[:, 0:TILE] = jnp.ones((2 * GROUP, TILE), LOW)
        keep(4, slope, slope_out)

    def project(hooks):
        keep_rows()
        fetched[1]().wait()

        @pl.loop(0, 2)
        def _(m):
            at_step(hooks, m)
            rows = cols(m, GROUP)
            all_three = nn(one[rows], qkv_w[...].reshape(-1, 3 * HD))
            for c in range(3):
                pre = all_three[:, c * HD : (c + 1) * HD] + vecs_out[4 + c : 5 + c, cols(head, HD)]
                if c < 2:
                    pre = turned(pre, turn[0, rows], turn[1, rows])
                heads[c, rows] = pre.astype(LOW)

        keep(5, heads, heads_out)

    def attend(hooks):
        @pl.loop(0, 2)
        def _(g):
            at_step(hooks, g)
            for part in range(2):
                rows, keys = cols(2 * g + part, TILE), pl.ds(cols(g, GROUP).start, (part + 1) * TILE)
                start = begin[pl.ds(g, 1), part * TILE : (part + 1) * TILE]
                columns = soft_columns(heads[0, rows], heads[1, keys], start, part * TILE)
                columns = columns.astype(LOW)
                soft[g, part, 0 : (part + 1) * TILE] = columns
                cat[rows, 0:HD] = nn(turn_over(eye, columns), heads[2, keys]).astype(LOW)

        keep(7, soft, soft_out)

    def od_grads(hooks):
        keep(6, cat, cat_out)
        fetched[2]().wait()
        flips = (flip_one, flip_two)

        def flip(to, k, e):
            tile = dy_v[:, :, :, cols(2 * k + e, TILE)].reshape(-1, TILE)
            to[e * TILE : (e + 1) * TILE, :] = turn_over(eye, tile)

        def staged(k, half):
            return pltpu.make_async_copy(stage.at[half], grad_out.at[k], stage_sems.at[half])

        for e in range(2):
            flip(flip_one, 0, e)

        @pl.loop(0, 2)
        def _(kk):
            for half in range(2):
                k = 2 * kk + half
                at_step(hooks, k)

                @pl.when(kk > 0)
                def _():
                    staged(k - 2, half).wait()

                for part, at in enumerate((WIDE_PART, REST)):
                    res = nn(flips[half][...], cat[:, at]).astype(LOW)
                    flip(flips[1 - half], (k + 1) % RING_SIZE, part)
                    stage[half, :, :, :, at] = res.reshape(RING_SIZE, 2, -1, at.stop - at.start)

                staged(k, half).start(priority=1)

        for half in range(2):
            staged(2 + half, half).wait()

    fetched = {}
    def lengths_copy():
        return pltpu.make_async_remote_copy(
            src_ref=len_in,
            dst_ref=len_v.at[zl],
            send_sem=len_sems.at[0],
            recv_sem=len_sems.at[1],
            device_id=partner,
            device_id_type=MESH,
        )

    moves = {
        SWAP: swap,
        OWN: own_half,
        OTHER: other_half,
        ROUND_ONE_X: round_one_x,
        ROUND_ONE_Y: round_one_y,
        ROUND_TWO_A: round_two_a,
        ROUND_TWO_B: round_two_b,
        ROUND_TWO_C: round_two_c,
        ROUND_THREE: round_three,
        LAST_ROUND: last_round,
        RING: ring_own,
        RING_ON: ring_on,
        RING_FAR: ring_far,
        TABLES: tables,
        VECTORS_X: vectors_x,
        VECTORS_Y: vectors_y,
        VECTORS: vectors,
        NORM: norms,
        FETCH: fetch_for,
    }

    def act(kind, *args):
        moves[kind](*args)

    loops = {HIDDEN: hidden_tiles, PROJECT: project, ATTEND: attend, OD_GRADS: od_grads}
    lengths_copy().start()
    play(FORWARD_ORDER, loops, act)
    own_copy(3).wait()
    lengths_copy().wait_send()
    for make in started.values():
        make().wait_send()
    for make in kept.values():
        make().wait()


def forward(rows, cot, lengths, vectors, weights):
    tokens, model = rows.shape
    total = 2 * RING_SIZE * tokens
    up, qkv, out_w, down = weights
    owned = up.shape[0]
    widths = (LANES, up.shape[1] // 2, 3 * HD, (out_w.shape[1] + down.shape[1]) // 2)
    halves = [(2, 16, LANES), *((2, owned, w) for w in widths[1:])]
    plane = [(RING_SIZE, RING_SIZE, *h) for h in halves]
    cat_cols = widths[3]
    shape = jax.ShapeDtypeStruct
    out = [
        shape((2, RING_SIZE, tokens, model), LOW),
        shape(plane[1], LOW),
        shape(plane[2], LOW),
        shape(plane[3], LOW),
        shape((16, model), WIDE),
        shape((total, model), LOW),
        shape((total, model), LOW),
        shape((total, model), LOW),
        shape((3, total, HD), LOW),
        shape((total, cat_cols), LOW),
        shape((total, cat_cols), LOW),
        shape((2, total, LANES), WIDE),
        shape((2, 2, GROUP, TILE), LOW),
        shape(plane[3], LOW),
    ]
    specs = [VMEM if k == 4 else ANY for k in range(len(out))]
    return pl.pallas_call(
        forward_kernel,
        out_shape=out,
        in_specs=[ANY, ANY, pl.BlockSpec(memory_space=pltpu.SMEM), VMEM, ANY, ANY, ANY, ANY],
        out_specs=specs,
        scratch_shapes=[
            pltpu.VMEM((2, RING_SIZE, tokens, model), LOW),
            pltpu.VMEM((2, 8, LANES), WIDE),
            pltpu.VMEM(plane[0], WIDE),
            pltpu.VMEM((total, model), LOW),
            pltpu.VMEM((total, model), LOW),
            pltpu.VMEM((total, model), LOW),
            pltpu.VMEM((2, RING_SIZE, tokens, model), LOW),
            pltpu.VMEM(plane[1], LOW),
            pltpu.VMEM(plane[2], LOW),
            pltpu.VMEM((total, cat_cols), LOW),
            pltpu.VMEM((total, cat_cols), LOW),
            pltpu.VMEM((3, total, HD), LOW),
            pltpu.VMEM((2, total, LANES), WIDE),
            pltpu.VMEM((GROUP, total), LOW),
            pltpu.VMEM((GROUP, total), LOW),
            pltpu.VMEM((2, RING_SIZE, 2, owned, cat_cols), LOW),
            pltpu.VMEM((GROUP, GROUP), WIDE),
            pltpu.VMEM((GROUP, GROUP), WIDE),
            pltpu.VMEM((2, 2, GROUP, TILE), LOW),
            pltpu.VMEM((8, GROUP), WIDE),
            pltpu.VMEM((TILE, TILE), LOW),
            pltpu.VMEM((8, LANES), WIDE),
            pltpu.VMEM(halves[0], WIDE),
            *(pltpu.VMEM(h, LOW) for h in halves[1:]),
            *(pltpu.VMEM(w.shape, WIDE) for w in weights),
            pltpu.SemaphoreType.DMA((4, PLANE_MESSAGES)),
            pltpu.SemaphoreType.DMA((4, PLANE_MESSAGES)),
            pltpu.SemaphoreType.DMA((2, RING_MESSAGES)),
            pltpu.SemaphoreType.DMA((2, RING_MESSAGES)),
            pltpu.SemaphoreType.DMA((2,)),
            pltpu.SemaphoreType.DMA((10,)),
            pltpu.SemaphoreType.DMA((8,)),
            pltpu.SemaphoreType.DMA((2,)),
            pltpu.SemaphoreType.DMA((4,)),
        ],
        compiler_params=pltpu.CompilerParams(
            collective_id=0, has_side_effects=True, vmem_limit_bytes=62 * 2**20
        ),
        name="forward_and_gather",
    )(rows, cot, lengths, vectors, *weights)


def backward_kernel(
    dy_in, up_in, qkv_in, od_in, vecs, one_in, two_in, unit_in, heads_in, cat_in, slope_in,
    turn_in, soft_in, od_grad,
    own_od_out, own_up_out, own_qkv_out, swap_od, swap_up, swap_qkv, vec_out, u_zero_out, u_one_out,
    own_od, own_up, own_qkv, u_zero, u_one,
    up_grad, qkv_grad, dcat, cat, heads, turn, soft, flip_one, flip_two, vecg, vec_block,
    od_near, od_me, od_full, tiles, eye,
    part_zero, both_zero, zfar_zero, znear_zero, part_one, both_one, zfar_one, znear_one,
    far_od, near_od, far2_od, near2_od, out_od,
    far_up, near_up, far2_up, near2_up, out_up,
    far_qkv, near_qkv, far2_qkv, near2_qkv, out_qkv,
    vec_x, vec_y, vec_z, vec_row, vec_own,
    send, recv, z_send, z_recv, v_send, v_recv, load_sems, stream_sems, out_sems,
):
    y, x, z, core = place()
    zl = z % 2
    head = ((z // 2) * 2 + core) * 2 + zl
    other = 1 - zl
    partner = device(y, x, z + 1 - 2 * zl, core)
    xp, xm, yp, ym = around(x, 1), around(x, -1), around(y, 1), around(y, -1)
    zp, zm = around(z, 1), around(z, -1)
    xo, yo, zo = around(x, 2), around(y, 2), around(z, 2)
    to_x = (device(y, xp, z, core), device(y, xm, z, core))
    to_y = (device(yp, x, z, core), device(ym, x, z, core))
    to_z = (partner, device(y, x, around(z, 2 * zl - 1), core))
    mate = device(y, x, z, 1 - core)
    line_x = (to_x[0], device(y, xo, z, core), to_x[1])
    line_y = (to_y[0], device(yo, x, z, core), to_y[1])
    line_z = [mate]
    for k in (1, 2, 3):
        for c in (0, 1):
            line_z.append(device(y, x, around(z, k), (core + c) % 2))
    neighbours = [*line_x, *line_y, *line_z]
    greet(neighbours)

    def load(k, src, dst):
        copy = pltpu.make_async_copy(src, dst, load_sems.at[k])
        copy.start(priority=1)
        return copy

    half_model = part_zero.shape[-1]
    loads = [load(0, slope_in, dcat)]
    for c in range(2):
        at = slice(c * half_model, (c + 1) * half_model)
        loads.append(load(1 + c, dy_in.at[:, :, :, :, at], part_zero.at[c]))
    od_loads = [load(13 + k, od_in.at[k], od_full.at[k]) for k in range(RING_SIZE)]
    near_loads = []
    for way, half in enumerate((zl, other)):
        for d in range(2):
            two = pl.ds(2 * d, 2)
            src = (two, (xp, xm)[d], half) if way == 0 else ((yp, ym)[d], two, half)
            near_loads.append(load(3 + 2 * way + d, od_grad.at[src], od_near.at[way, d]))
        every = pl.ds(0, RING_SIZE)
        src = (every, x, half) if way == 0 else (y, every, half)
        near_loads.append(load(7 + way, od_grad.at[src], od_me.at[way]))
    late = [
        load(9, heads_in, heads),
        load(10, turn_in, turn),
        load(11, cat_in, cat),
        load(12, soft_in, soft),
    ]
    meet(neighbours)

    started, note = {}, [None]

    def go(make):
        make().start()
        started[note[0]] = make

    g_ref = {OD: od_grad, UP: up_grad, QKV: qkv_grad}
    bufs = {
        OD: (far_od, near_od, far2_od, near2_od, out_od, own_od, swap_od),
        UP: (far_up, near_up, far2_up, near2_up, out_up, own_up, swap_up),
        QKV: (far_qkv, near_qkv, far2_qkv, near2_qkv, out_qkv, own_qkv, swap_qkv),
    }
    posts = {i: mailbox(note, send, recv, i - 1) for i in (UP, QKV, OD)}
    z_posts = [mailbox(note, z_send, z_recv, j) for j in range(6)]
    v_post = mailbox(note, v_send, v_recv)

    def arrived(i, k, ref):
        posts[i](k, ref, ref, mate).wait_recv()

    def z_arrived(j, k, ref):
        z_posts[j](k, ref, ref, mate).wait_recv()

    halves = (zl, other)
    first_to, second_to = (to_x, to_y), (to_y, to_x)
    first = ((xp, xm, xo, x), (yp, ym, yo, y))
    second = ((yp, ym, yo, y), (xp, xm, xo, x))
    pair = (pl.ds(0, 2), pl.ds(2, 2))
    part_rows = (pl.ds(0, 32), pl.ds(32, 32))

    def block(i, way, along, across):
        if way == 0:
            return g_ref[i].at[across, along, halves[0]]
        return g_ref[i].at[along, across, halves[1]]

    def near_value(i, way, d, k):
        if i == OD:
            return od_near[way, d, k]
        return block(i, way, first[way][d], k + 2 * d)[...]

    def me_value(i, way, k, rows):
        if i == OD:
            return od_me[way, k, rows]
        return block(i, way, first[way][3], k).at[rows][...]

    def send_first(i):
        far, near = bufs[i][:2]
        for way in range(2):
            for d in range(2):
                go(
                    lambda way=way, d=d: posts[i](
                        way * 12 + d,
                        block(i, way, first[way][2], pair[d]),
                        far.at[way, d],
                        first_to[way][d],
                    )
                )
        for way in range(2):
            for d in range(2):
                go(
                    lambda way=way, d=d: posts[i](
                        way * 12 + 2 + d,
                        block(i, way, first[way][d], pair[1 - d]),
                        near.at[way, d, pair[1 - d]],
                        first_to[way][d],
                    )
                )

    def send_near(i, way):
        far, near = bufs[i][:2]
        for d in range(2):
            arrived(i, way * 12 + d, far.at[way, d])
            for k in range(2):
                far[way, d, k] = far[way, d, k] + near_value(i, way, d, k)
            go(
                lambda d=d: posts[i](
                    way * 12 + 4 + d, far.at[way, d], near.at[way, d, pair[d]], first_to[way][d]
                )
            )

    def send_second(i, way):
        far, near, far_two, near_two = bufs[i][:4]
        for d in range(2):
            arrived(i, way * 12 + 2 + d, near.at[way, d, pair[1 - d]])
            arrived(i, way * 12 + 4 + d, near.at[way, d, pair[d]])

        @pl.loop(0, 2 * RING_SIZE)
        def _(t):
            k, rows = t // 2, cols(t % 2, 32)
            total = near[way, 0, k, rows] + near[way, 1, k, rows]
            near[way, 0, k, rows] = total + me_value(i, way, k, rows)

        for d in range(2):
            go(
                lambda d=d: posts[i](
                    way * 12 + 6 + d,
                    near.at[way, 0, second[way][2], part_rows[d]],
                    far_two.at[way, d],
                    second_to[way][d],
                )
            )
        for d in range(2):
            go(
                lambda d=d: posts[i](
                    way * 12 + 8 + d,
                    near.at[way, 0, second[way][d], part_rows[1 - d]],
                    near_two.at[way, d, part_rows[1 - d]],
                    second_to[way][d],
                )
            )

    def send_last(i, way):
        far, near, far_two, near_two = bufs[i][:4]
        for d in range(2):
            arrived(i, way * 12 + 6 + d, far_two.at[way, d])
            rows = part_rows[d]
            far_two[way, d] = far_two[way, d] + near[way, 0, second[way][d], rows]
            go(
                lambda d=d: posts[i](
                    way * 12 + 10 + d,
                    far_two.at[way, d],
                    near_two.at[way, d, part_rows[d]],
                    second_to[way][d],
                )
            )

    def finish(i, way):
        near, near_two, out, mine, swapped = (bufs[i][k] for k in (1, 3, 4, 5, 6))
        for d in range(2):
            arrived(i, way * 12 + 8 + d, near_two.at[way, d, part_rows[1 - d]])
            arrived(i, way * 12 + 10 + d, near_two.at[way, d, part_rows[d]])
        total = wide(near[way, 0, second[way][3]]) + wide(near_two[way, 0]) + wide(near_two[way, 1])
        if way == 1:
            out[...] = total.astype(LOW)
            go(lambda: posts[i](24, out, swapped, partner))
        else:
            mine[...] = total.astype(LOW)
            out_copy(i - 1).start(priority=1)

    def z_bufs(j):
        if j < 2:
            return [r.at[j] for r in (part_zero, both_zero, zfar_zero, znear_zero)]
        return [r.at[j - 2] for r in (part_one, both_one, zfar_one, znear_one)]

    def z_rows(j):
        lead = 64 if j < 2 else 16
        return pl.ds(0, lead), pl.ds(lead, near_rows - lead)

    near_rows = znear_zero.shape[2]
    z_ends = (z + 1 - 2 * zl, around(z, 2 * zl - 1))

    def z_to_mate(j):
        go(lambda: z_posts[j](0, z_bufs(j)[0].at[:, :, 1 - core], z_bufs(j)[1], mate))

    def z_block(j, zz):
        return z_bufs(j)[1].at[zz % 2, zz // 2]

    def z_first(j):
        part, both, far, near = z_bufs(j)
        z_arrived(j, 0, both)

        @pl.loop(0, 8)
        def _(k):
            b, c, rows = k // 4, (k // 2) % 2, cols(k % 2, 64)
            both[b, c, rows] = both[b, c, rows] + part[b, c, core, rows]

        rows = z_rows(j)
        for d in range(2):
            go(
                lambda d=d: z_posts[j](
                    1 + d, z_block(j, zo).at[rows[d]], z_bufs(j)[2].at[rows[d]], to_z[d]
                )
            )
        for d in range(2):
            go(
                lambda d=d: z_posts[j](
                    3 + d,
                    z_block(j, z_ends[d]).at[rows[d]],
                    z_bufs(j)[3].at[d, rows[d]],
                    to_z[d],
                )
            )

    def z_second(j):
        part, both, far, near = z_bufs(j)
        rows = z_rows(j)
        for d in range(2):
            z_arrived(j, 1 + d, far.at[rows[d]])
            zz = z_ends[1 - d]
            far[rows[d]] = far[rows[d]] + both[zz % 2, zz // 2, rows[d]]
            go(
                lambda d=d: z_posts[j](
                    6 - d, z_bufs(j)[2].at[rows[d]], z_bufs(j)[3].at[1 - d, rows[d]], to_z[1 - d]
                )
            )

    def z_finish(j):
        part, both, far, near = z_bufs(j)
        rows = z_rows(j)
        for d in range(2):
            z_arrived(j, 3 + d, near.at[d, rows[d]])
            z_arrived(j, 5 + d, near.at[d, rows[1 - d]])
        out, at = (u_zero, j) if j < 2 else (u_one, j - 2)
        width = near.shape[-1]
        for k in range(2):
            rows = pl.ds(64 * k, 64)
            total = wide(both[zl, z // 2, rows]) + wide(near[0, rows]) + wide(near[1, rows])
            out[rows, at * width : (at + 1) * width] = total.astype(LOW)
        out_copy(3 + j).start(priority=1)

    def at_step(hooks, k):
        for due, entries in hooks.items():

            @pl.when(k == due)
            def _():
                for entry in entries:
                    act(*entry)

    def out_copy(k):
        if k < 3:
            src, dst = ((own_up, own_up_out), (own_qkv, own_qkv_out), (own_od, own_od_out))[k]
        else:
            j = k - 3
            src, dst = (u_zero, u_zero_out) if j < 2 else (u_one, u_one_out)
            width = src.shape[1] // (2 if j < 2 else 4)
            at = pl.ds((j if j < 2 else j - 2) * width, width)
            src, dst = src.at[:, at], dst.at[:, at]
        return pltpu.make_async_copy(src, dst, out_sems.at[k])

    def cat_grads(hooks):
        for c in od_loads:
            c.wait()
        thirds = (slice(0, 512), slice(512, 1024), slice(1024, 1280))
        for step, (m, at) in enumerate(((m, at) for at in thirds for m in range(2))):
            for entry in hooks.get(step, ()):
                act(*entry)
            w = od_full[:, :, :, :, at].reshape(-1, at.stop - at.start)
            rows = pl.ds(m * GROUP, GROUP)
            grad = nn(part_zero[0, m].reshape(GROUP, -1), w[:half_model])
            grad = grad + nn(part_zero[1, m].reshape(GROUP, -1), w[half_model:])
            dcat[rows, at] = (grad * wide(dcat[rows, at])).astype(LOW)

    def weight_grads(hooks, sem, source, rights, to, bias):
        flips = (flip_one, flip_two)
        size = to.shape[-1] // len(rights)

        def copy(k, half):
            at = stream_sems.at[sem, half]
            return pltpu.make_async_copy(source.at[:, cols(k, GROUP)], tiles.at[half], at)

        def flip(half, e):
            at = slice(e * TILE, (e + 1) * TILE)
            flips[half][at, :] = turn_over(eye, tiles[half, :, at])

        for half in range(2):
            copy(half, half).start(priority=1)
        copy(0, 0).wait()

        for e in range(2):
            flip(0, e)

        @pl.loop(0, 2)
        def _(kk):
            for half in range(2):
                k = 2 * kk + half
                at_step(hooks, k)
                if half == 0:
                    copy(k + 1, 1).wait()
                else:

                    @pl.when(kk == 0)
                    def _():
                        copy(k + 1, 0).wait()

                @pl.when(kk == 0)
                def _():
                    copy(k + 2, half).start(priority=1)

                for n, right in enumerate(rights):
                    res = nn(flips[half][...], right[...])
                    row, at = bias(n)
                    vecg[row, at] = res[GROUP : GROUP + 1]
                    part = res[0:GROUP].astype(LOW)
                    to[k, :, :, :, n * size : (n + 1) * size] = part.reshape(RING_SIZE, 2, -1, size)
                for e in range(2):
                    flip(1 - half, e)

    def attend_back(hooks):
        @pl.loop(0, 2)
        def _(g):
            at_step(hooks, g)
            dkey, dvalue = [], []
            for part in range(2):
                rows, count = cols(2 * g + part, TILE), (part + 1) * TILE
                keys = pl.ds(cols(g, GROUP).start, count)
                columns = soft[g, part, 0:count]
                query, key, grad = heads[0, rows], heads[1, keys], dcat[rows, 0:HD]
                dsoft = nt(heads[2, keys], grad)
                inner = jnp.sum(wide(columns) * dsoft, axis=0, keepdims=True)
                dscore = (wide(columns) * (dsoft - inner)).astype(LOW)
                dquery = nn(turn_over(eye, dscore), key) * (HD**-0.5)
                heads[0, rows] = turned(dquery, turn[0, rows], -turn[1, rows]).astype(LOW)
                dkey.append(nn(dscore, query))
                dvalue.append(nn(columns, grad))
            for part in range(2):
                rows, at = cols(2 * g + part, TILE), slice(part * TILE, (part + 1) * TILE)
                whole_key, whole_value = dkey[1][at], dvalue[1][at]
                if part == 0:
                    whole_key, whole_value = whole_key + dkey[0], whole_value + dvalue[0]
                whole_key = turned(whole_key * (HD**-0.5), turn[0, rows], -turn[1, rows])
                heads[1, rows] = whole_key.astype(LOW)
                heads[2, rows] = whole_value.astype(LOW)

    def branch(hooks):
        @pl.loop(0, RING_SIZE)
        def _(k):
            at_step(hooks, k)
            w = od_full[k].reshape(GROUP, -1)
            for m in range(2):
                res = nt(cat[m * GROUP : (m + 1) * GROUP], w).astype(LOW)
                part_zero[k // 2, m, :, :, :, cols(k % 2, GROUP)] = res.reshape(2, 2, -1, GROUP)

    def norm_grads(hooks):
        up_at, qkv_at = slice(0, up_in.shape[-1]), slice(0, qkv_in.shape[-1])

        def copies(k, slot):
            return [
                pltpu.make_async_copy(
                    qkv_in.at[k], od_full.at[2 + slot, :, :, :, qkv_at], stream_sems.at[2, slot]
                ),
                pltpu.make_async_copy(
                    up_in.at[k], od_full.at[slot, :, :, :, up_at], stream_sems.at[3, slot]
                ),
                pltpu.make_async_copy(
                    unit_in.at[:, cols(k, GROUP)], tiles.at[slot], stream_sems.at[4, slot]
                ),
            ]

        def use(k, slot):
            at_step(hooks, k)
            w_one = od_full[2 + slot, :, :, :, qkv_at].reshape(GROUP, -1)
            w_two = od_full[slot, :, :, :, up_at].reshape(GROUP, -1)
            at = cols(k, GROUP)
            sums = [jnp.zeros((1, GROUP), WIDE)] * 4
            for part in range(4):
                m, inner = part // 2, part % 2
                rows = pl.ds(part * TILE, TILE)
                a = nt(heads[0, rows], w_one[:, 0:HD])
                for c in (1, 2):
                    a = a + nt(heads[c, rows], w_one[:, c * HD : (c + 1) * HD])
                b = nt(dcat[rows, TILE:], w_two)
                u = wide(tiles[slot, rows])
                res = (a * vecs[0:1, at] + b * vecs[2:3, at]).astype(LOW)
                part_one[k, m, inner] = res.reshape(2, -1, GROUP)
                new = (a * u, a, b * u, b)
                sums = [s + jnp.sum(v, axis=0, keepdims=True) for s, v in zip(sums, new)]
            for r in range(4):
                vecg[r : r + 1, at] = sums[r]

        streamed(RING_SIZE, copies, use)

    def vec_first():
        lane = lax.broadcasted_iota(jnp.int32, (16, LANES), 1)
        for p in range(RING_SIZE * RING_SIZE):
            v = vecg[:, p * LANES : (p + 1) * LANES]
            lead = jnp.where(lane < LANES // 2, v, 0.0)
            tail = jnp.where(lane < LANES // 2, pltpu.roll(v, LANES // 2, 1), 0.0)
            vec_block[p // RING_SIZE, p % RING_SIZE, 0] = lead
            vec_block[p // RING_SIZE, p % RING_SIZE, 1] = tail
        for k in range(3):
            go(lambda k=k: v_post(k, vec_block.at[:, around(x, k + 1)], vec_x.at[k], line_x[k]))

    def vec_second():
        for k in range(3):
            v_post(k, vec_x.at[k], vec_x.at[k], mate).wait_recv()
        for r in range(RING_SIZE):
            vec_row[r] = vec_block[r, x] + vec_x[0, r] + vec_x[1, r] + vec_x[2, r]
        for k in range(3):
            go(lambda k=k: v_post(3 + k, vec_row.at[around(y, k + 1)], vec_y.at[k], line_y[k]))

    def vec_third():
        for k in range(3):
            v_post(3 + k, vec_y.at[k], vec_y.at[k], mate).wait_recv()
        vec_own[...] = vec_row[y] + vec_y[0] + vec_y[1] + vec_y[2]
        for k in range(7):
            there = lambda k=k: zl if k == 0 else (z + (k + 1) // 2) % 2
            go(
                lambda k=k, there=there: v_post(
                    6 + k, vec_own.at[there()], vec_z.at[k], line_z[k]
                )
            )

    def vec_finish():
        total = vec_own[zl]
        for k in range(7):
            v_post(6 + k, vec_z.at[k], vec_z.at[k], mate).wait_recv()
            total = total + vec_z[k]
        vec_out[...] = total

    def wait_loads():
        vecg[...] = jnp.zeros(vecg.shape, WIDE)
        fill_eye(eye)
        for ref in (flip_one, flip_two):
            ref[GROUP:, :] = jnp.ones((16, ref.shape[1]), LOW)
        for c in loads:
            c.wait()
        for c in range(2):
            total = jnp.sum(wide(part_zero[c, zl, z // 2, core]), axis=0, keepdims=True)
            for r in (7, 8):
                vecg[r : r + 1, c * half_model : (c + 1) * half_model] = total

    def up_weight_grads(hooks):
        for c in near_loads:
            c.wait()
        def bias(n):
            return pl.ds(9 + head // 2, 1), cols((head % 2) * 2 + n, GROUP)

        rights = [dcat.at[:, TILE + n * GROUP : TILE + (n + 1) * GROUP] for n in range(2)]
        weight_grads(hooks, 5, two_in, rights, up_grad, bias)
        for c in late:
            c.wait()

    def qkv_weight_grads(hooks):
        def bias(n):
            return pl.ds(4 + n, 1), cols(head, HD)

        weight_grads(hooks, 6, one_in, [heads.at[c] for c in range(3)], qkv_grad, bias)

    def settle():
        for key in list(started)[:-20]:
            started.pop(key)().wait_send()

    moves = {
        SETTLE: settle,
        FIRST: send_first,
        NEAR: send_near,
        SECOND: send_second,
        FAR_SIDE: send_last,
        FINISH: finish,
        Z_MATE: z_to_mate,
        Z_FIRST: z_first,
        Z_SECOND: z_second,
        Z_FINISH: z_finish,
        LOADS: wait_loads,
        VEC_ONE: vec_first,
        VEC_TWO: vec_second,
        VEC_THREE: vec_third,
    }

    def act(kind, *args):
        moves[kind](*args)

    loops = {
        CAT_GRADS: cat_grads,
        UP_GRADS: up_weight_grads,
        BRANCH: branch,
        ATTEND_BACK: attend_back,
        QKV_GRADS: qkv_weight_grads,
        NORM_GRADS: norm_grads,
    }
    play(BACKWARD_ORDER, loops, act)
    vec_finish()
    for i in (UP, QKV, OD):
        arrived(i, 24, bufs[i][6])
    for k in range(9):
        out_copy(k).wait()
    for make in started.values():
        make().wait_send()


def backward(held):
    dy, up_full, qkv_full, od_full, vecs, one, two, unit, heads, cat, slope, turn, soft, _ = held
    total, model = one.shape
    tokens = dy.shape[2]
    owned = od_full.shape[3]
    widths = [w.shape[-1] for w in (od_full, up_full, qkv_full)]
    shape = jax.ShapeDtypeStruct
    out = [shape((owned, w), LOW) for w in widths]
    out += [shape((owned, w), LOW) for w in widths]
    out += [shape((16, LANES), WIDE)]
    out += [shape((tokens, model), LOW)] * 2
    plane = (RING_SIZE, RING_SIZE, 2, owned)
    scratch = [pltpu.VMEM((owned, w), LOW) for w in widths]
    scratch += [pltpu.VMEM((tokens, model), LOW)] * 2
    scratch += [
        pltpu.VMEM((*plane, widths[1]), LOW),
        pltpu.VMEM((*plane, widths[2]), LOW),
        pltpu.VMEM(slope.shape, LOW),
        pltpu.VMEM(cat.shape, LOW),
        pltpu.VMEM(heads.shape, LOW),
        pltpu.VMEM(turn.shape, WIDE),
        pltpu.VMEM(soft.shape, LOW),
        pltpu.VMEM((GROUP + 16, total), LOW),
        pltpu.VMEM((GROUP + 16, total), LOW),
        pltpu.VMEM((16, model), WIDE),
        pltpu.VMEM((RING_SIZE, RING_SIZE, 2, 16, LANES), WIDE),
        pltpu.VMEM((2, 2, 2, owned, widths[0]), LOW),
        pltpu.VMEM((2, RING_SIZE, owned, widths[0]), LOW),
        pltpu.VMEM((*plane, widths[0]), LOW),
        pltpu.VMEM((2, total, GROUP), LOW),
        pltpu.VMEM((TILE, TILE), LOW),
    ]
    for n in (2, 4):
        w = model // n
        scratch += [
            pltpu.VMEM((n, 2, 2, 2, tokens, w), LOW),
            pltpu.VMEM((n, 2, 2, tokens, w), LOW),
            pltpu.VMEM((n, tokens, w), LOW),
            pltpu.VMEM((n, 2, tokens, w), LOW),
        ]
    for w in widths:
        scratch += [
            pltpu.VMEM((2, 2, 2, owned, w), LOW),
            pltpu.VMEM((2, 2, RING_SIZE, owned, w), LOW),
            pltpu.VMEM((2, 2, owned // 2, w), LOW),
            pltpu.VMEM((2, 2, owned, w), LOW),
            pltpu.VMEM((owned, w), LOW),
        ]
    scratch += [
        pltpu.VMEM((3, RING_SIZE, 2, 16, LANES), WIDE),
        pltpu.VMEM((3, 2, 16, LANES), WIDE),
        pltpu.VMEM((7, 16, LANES), WIDE),
        pltpu.VMEM((RING_SIZE, 2, 16, LANES), WIDE),
        pltpu.VMEM((2, 16, LANES), WIDE),
        pltpu.SemaphoreType.DMA((3, 25)),
        pltpu.SemaphoreType.DMA((3, 25)),
        pltpu.SemaphoreType.DMA((6, 7)),
        pltpu.SemaphoreType.DMA((6, 7)),
        pltpu.SemaphoreType.DMA((13,)),
        pltpu.SemaphoreType.DMA((13,)),
        pltpu.SemaphoreType.DMA((17,)),
        pltpu.SemaphoreType.DMA((7, 2)),
        pltpu.SemaphoreType.DMA((9,)),
    ]
    specs = [VMEM if k == 4 else ANY for k in range(14)]
    return pl.pallas_call(
        backward_kernel,
        out_shape=out,
        in_specs=specs,
        out_specs=[VMEM if k == 6 else ANY for k in range(len(out))],
        scratch_shapes=scratch,
        compiler_params=pltpu.CompilerParams(
            collective_id=1, has_side_effects=True, vmem_limit_bytes=63 * 2**20
        ),
        name="backward_and_reduce",
    )(dy.reshape(2, 2, 2, tokens, model), *held[1:])


def adamw(weight, gradient, moment, square, step_rate, decay_rate):
    moment_new = beta_first * moment + (1.0 - beta_first) * gradient
    square_new = beta_second * square + (1.0 - beta_second) * gradient * gradient
    first_fix = 1.0 / (1.0 - beta_first**UPDATE_STEP)
    second_fix = 1.0 / (1.0 - beta_second**UPDATE_STEP)
    fixed = square_new * second_fix
    below = fixed * lax.rsqrt(fixed) + adam_eps
    inverse = pl.reciprocal(below, approx=True)
    inverse = inverse * (2.0 - below * inverse)
    direction = moment_new * first_fix * inverse
    weight_new = weight - step_rate * (direction + decay_rate * weight)
    return (weight_new, moment_new, square_new)


def update_kernel(*refs):
    (own_od, own_up, own_qkv, swap_od, swap_up, swap_qkv, vec_sum, u_zero, u_one, x_in, dy_in) = refs[:11]
    vecs, state, outs = refs[11], refs[12:27], refs[27:44]
    grads, rows_in, held = refs[44:50], refs[50:54], refs[54:69]
    block_v, grad_v, in_sems, out_sems = refs[69:]
    zl = lax.axis_index("dp") % 2
    started = []

    def load(src, dst):
        copy = pltpu.make_async_copy(src, dst, in_sems.at[len(started)])
        copy.start(priority=len(started) % 2)
        started.append(copy)
        return copy

    stored = []

    def store(src, dst):
        copy = pltpu.make_async_copy(src, dst, out_sems.at[len(stored)])
        copy.start(priority=len(stored) % 2)
        stored.append(copy)

    sources = (own_od, own_up, own_qkv, swap_od, swap_up, swap_qkv)
    row_waits = [load(a, b) for a, b in zip((x_in, u_zero, u_one, dy_in), rows_in)]
    waits = {}
    for i, parts in ((2, (1, 4)), (3, (0, 3)), (0, (2, 5)), (1, ())):
        waits[i] = [load(sources[k], grads[k]) for k in parts]
        waits[i] += [load(state[3 * i + k], held[3 * i + k]) for k in range(3)]
    vec_waits = [load(state[12 + k], held[12 + k]) for k in range(3)]

    def new(i, at, gradient, rate, decay):
        three = held[3 * i : 3 * i + 3]
        weight, moment, square = (r[at] for r in three)
        for r, v in zip(three, adamw(weight, gradient, moment, square, rate, decay)):
            r[at] = v

    def done(i):
        for k in range(3):
            store(held[3 * i + k], outs[2 + 3 * i + k])

    def part(k, h, at):
        return wide(jnp.where(zl == h, grads[k][at], grads[k + 3][at]))

    def rows_of(k, size):
        return pl.ds(pl.multiple_of(k * size, size), size)

    for c in row_waits:
        c.wait()
    x_v, zero_v, one_v, dy_v = rows_in

    @pl.loop(0, 4)
    def _(k):
        rows = rows_of(k, 32)
        v = wide(x_v[rows])
        block_v[rows] = (v + wide(zero_v[rows]) + vecs[7:8, :] + vecs[8:9, :]).astype(LOW)
        centred = v - jnp.mean(v, axis=-1, keepdims=True)
        scale = lax.rsqrt(jnp.mean(centred * centred, axis=-1, keepdims=True) + norm_eps)
        unit = centred * scale
        g = wide(one_v[rows])
        g = g - jnp.mean(g, axis=-1, keepdims=True) - unit * jnp.mean(g * unit, axis=-1, keepdims=True)
        grad_v[rows] = wide(dy_v[rows]) + scale * g

    store(block_v, outs[0])
    store(grad_v, outs[1])
    for c in waits[2]:
        c.wait()

    @pl.loop(0, 4)
    def _(k):
        rows = rows_of(k, 16)
        for h in range(2):
            n = grads[1].shape[1]
            g = part(1, h, (rows, slice(0, n)))
            new(2, (rows, slice(h * n, (h + 1) * n)), g, matrix_rate, matrix_decay)

    done(2)
    for c in waits[3]:
        c.wait()

    @pl.loop(0, 4)
    def _(k):
        rows = rows_of(k, 16)
        n = grads[0].shape[1] - HD
        for h in range(2):
            g = part(0, h, (rows, slice(HD, HD + n)))
            new(3, (rows, slice(h * n, (h + 1) * n)), g, matrix_rate, matrix_decay)

    done(3)
    for c in waits[0]:
        c.wait()

    @pl.loop(0, 4)
    def _(k):
        rows = rows_of(k, 16)
        for c in range(3):
            for h in range(2):
                g = part(2, h, (rows, slice(c * HD, (c + 1) * HD)))
                new(0, (c, rows, slice(h * HD, (h + 1) * HD)), g, matrix_rate, matrix_decay)

    done(0)
    for c in waits[1]:
        c.wait()

    @pl.loop(0, 4)
    def _(k):
        rows = rows_of(k, 16)
        for h in range(2):
            g = part(0, h, (rows, slice(0, HD)))
            new(1, (rows, slice(h * HD, (h + 1) * HD)), g, matrix_rate, matrix_decay)

    done(1)
    for c in vec_waits:
        c.wait()
    at = (slice(None), slice(None))
    shape = held[12].shape
    new(4, at, vec_sum[0 : shape[0], 0 : shape[1]], vector_rate, 0.0)
    done(4)
    for c in stored:
        c.wait()


def update(reduced, rows, cot, vecs, state):
    own, vec_sum, sums = reduced[:6], reduced[6], reduced[7:]
    shape = jax.ShapeDtypeStruct
    out = [shape(rows.shape, LOW), shape(rows.shape, WIDE)]
    out += [shape(a.shape, WIDE) for a in state]
    scratch = [pltpu.VMEM(a.shape, a.dtype) for a in (*own, rows, *sums, cot, *state)]
    scratch += [
        pltpu.VMEM(rows.shape, LOW),
        pltpu.VMEM(rows.shape, WIDE),
        pltpu.SemaphoreType.DMA((25,)),
        pltpu.SemaphoreType.DMA((17,)),
    ]
    specs = [ANY] * 6 + [VMEM] + [ANY] * 4 + [VMEM] + [ANY] * 15
    return pl.pallas_call(
        update_kernel,
        out_shape=out,
        in_specs=specs,
        out_specs=[ANY] * len(out),
        scratch_shapes=scratch,
        compiler_params=pltpu.CompilerParams(vmem_limit_bytes=63 * 2**20),
        name="update",
    )(*own, vec_sum, *sums, rows, cot, vecs, *state)


def local(
    inputs,
    cotangent,
    lengths,
    qkv_weight,
    out_weight,
    up_weight,
    down_weight,
    norm_vectors,
    qkv_mean,
    qkv_square,
    out_mean,
    out_square,
    up_mean,
    up_square,
    down_mean,
    down_square,
    vector_mean,
    vector_square,
):
    weights = (up_weight, qkv_weight, out_weight.T, down_weight.T)
    held = forward(inputs, cotangent, lengths, norm_vectors, weights)
    state = (
        *(qkv_weight, qkv_mean, qkv_square),
        *(out_weight.T, out_mean.T, out_square.T),
        *(up_weight, up_mean, up_square),
        *(down_weight.T, down_mean.T, down_square.T),
        *(norm_vectors, vector_mean, vector_square),
    )
    out = list(update(backward(held), inputs, cotangent, held[4], state))
    for k in (5, 6, 7, 11, 12, 13):
        out[k] = out[k].T
    return tuple(out)


def solution(mesh):
    placed = (
        P(("dp", "tensor"), None),
        P(("dp", "tensor"), None),
        P("dp", None),
        P(None, "dp", "tensor"),
        P("tensor", "dp"),
        P("dp", "tensor"),
        P("tensor", "dp"),
        P(None, "dp"),
        P(None, "dp", "tensor"),
        P(None, "dp", "tensor"),
        P("tensor", "dp"),
        P("tensor", "dp"),
        P("dp", "tensor"),
        P("dp", "tensor"),
        P("tensor", "dp"),
        P("tensor", "dp"),
        P(None, "dp"),
        P(None, "dp"),
    )
    return jax.shard_map(
        local,
        mesh=mesh,
        in_specs=placed,
        out_specs=(
            P(("dp", "tensor"), None),
            P(("dp", "tensor"), None),
            P(None, "dp", "tensor"),
            P(None, "dp", "tensor"),
            P(None, "dp", "tensor"),
            P("tensor", "dp"),
            P("tensor", "dp"),
            P("tensor", "dp"),
            P("dp", "tensor"),
            P("dp", "tensor"),
            P("dp", "tensor"),
            P("tensor", "dp"),
            P("tensor", "dp"),
            P("tensor", "dp"),
            P(None, "dp"),
            P(None, "dp"),
            P(None, "dp"),
        ),
        check_vma=False,
    )
```

```python
import functools
import math

import jax
import jax.numpy as jnp
from jax import lax
from jax.experimental import pallas as pl
from jax.experimental.pallas import tpu as pltpu
from jax.sharding import PartitionSpec as P

HD = 256
ROT = 64
UPDATE_STEP = 10
RING_SIZE = 4


norm_eps = 1e-05
beta_first = 0.9
beta_second = 0.95
adam_eps = 1e-08
matrix_rate = 0.02
vector_rate = 0.2
matrix_decay = 0.01
masked_score = -1e30
inv_root_two = 1.0 / math.sqrt(2.0)
inv_root_tau = 1.0 / math.sqrt(2.0 * math.pi)

MESH = pl.DeviceIdType.MESH
ANY = pl.BlockSpec(memory_space=pl.ANY)
VMEM = pl.BlockSpec(memory_space=pltpu.VMEM)


def place():
    dp, tensor = lax.axis_index("dp"), lax.axis_index("tensor")
    z = (tensor // 2) * 2 + dp % 2
    return dp // 8, (dp // 2) % RING_SIZE, z, tensor % 2


def device(y, x, z, core):
    return ((y * RING_SIZE + x) * 2 + z % 2, (z // 2) * 2 + core)


def around(i, step):
    return (i + step + RING_SIZE) % RING_SIZE


def greet(devices):
    barrier = pltpu.get_barrier_semaphore()
    for d in devices:
        pl.semaphore_signal(barrier, inc=1, device_id=d, device_id_type=MESH)


def meet(devices):
    pl.semaphore_wait(pltpu.get_barrier_semaphore(), len(devices))


def mailbox(note, send, recv, *lead):
    def post(k, src, dst, to):
        note[0] = (id(send), *lead, k)
        return pltpu.make_async_remote_copy(
            src_ref=src,
            dst_ref=dst,
            send_sem=send.at[(*lead, k)],
            recv_sem=recv.at[(*lead, k)],
            device_id=to,
            device_id_type=MESH,
        )

    return post


LOW = jnp.bfloat16
WIDE = jnp.float32
GROUP = 512
TILE = 256
WIDE_PART, REST = slice(0, 768), slice(768, 1280)
LANES = 128
PLANE_MESSAGES = 33
RING_MESSAGES = 8


VEC, UP, QKV, OD = range(4)
DY = 3
(
    SWAP,
    OWN,
    OTHER,
    ROUND_ONE_X,
    ROUND_ONE_Y,
    ROUND_TWO_A,
    ROUND_TWO_B,
    ROUND_TWO_C,
    ROUND_THREE,
    LAST_ROUND,
    RING,
    RING_ON,
    RING_FAR,
    TABLES,
    VECTORS_X,
    VECTORS_Y,
    VECTORS,
    NORM,
    FETCH,
    HIDDEN,
    PROJECT,
    ATTEND,
    OD_GRADS,
) = range(23)
(
    FIRST,
    NEAR,
    SECOND,
    FAR_SIDE,
    FINISH,
    Z_MATE,
    Z_FIRST,
    Z_SECOND,
    Z_FINISH,
    LOADS,
    VEC_ONE,
    VEC_TWO,
    VEC_THREE,
    SETTLE,
    CAT_GRADS,
    UP_GRADS,
    BRANCH,
    ATTEND_BACK,
    QKV_GRADS,
    NORM_GRADS,
) = range(20)
FORWARD_ORDER = (
    (OWN, UP), (SWAP, UP), (SWAP, QKV), (SWAP, VEC), (RING, 0), (OWN, QKV), (OTHER, UP),
    (VECTORS_X,), (OTHER, QKV), (VECTORS_Y,), (SWAP, OD), (ROUND_ONE_X, UP), (ROUND_ONE_Y, UP),
    (TABLES,), (ROUND_ONE_X, QKV), (ROUND_ONE_Y, QKV), (VECTORS,), (RING_ON, 0),
    (ROUND_TWO_A, UP), (RING, 1), (ROUND_TWO_B, UP), (NORM, 0), (ROUND_TWO_C, UP), (NORM, 4),
    (NORM, 2), (ROUND_THREE, UP), (RING_FAR, 0), (NORM, 1), (ROUND_TWO_B, QKV), (OTHER, OD),
    (NORM, 6), (LAST_ROUND, UP), (FETCH, UP), (OWN, OD), (HIDDEN, 0), (ROUND_TWO_A, QKV),
    (ROUND_TWO_C, QKV), (RING_ON, 1), (HIDDEN, 1), (ROUND_THREE, QKV), (ROUND_ONE_Y, OD),
    (HIDDEN, 2), (ROUND_ONE_X, OD), (HIDDEN, 3), (RING_FAR, 1), (LAST_ROUND, QKV),
    (ROUND_TWO_A, OD), (FETCH, QKV), (PROJECT, 0), (PROJECT, 1), (ATTEND, 0), (FETCH, DY),
    (ROUND_TWO_B, OD), (ATTEND, 1), (ROUND_TWO_C, OD), (OD_GRADS, 0), (ROUND_THREE, OD),
    (OD_GRADS, 1), (OD_GRADS, 2), (OD_GRADS, 3), (LAST_ROUND, OD),
)
BACKWARD_ORDER = (
    (FIRST, OD), (LOADS,), (CAT_GRADS, 0), (CAT_GRADS, 1), (CAT_GRADS, 2), (CAT_GRADS, 3),
    (UP_GRADS, 0), (UP_GRADS, 1), (UP_GRADS, 2), (UP_GRADS, 3), (FIRST, UP), (BRANCH, 0),
    (NEAR, OD, 0), (BRANCH, 1), (Z_MATE, 0), (NEAR, OD, 1), (BRANCH, 2), (BRANCH, 3),
    (ATTEND_BACK, 0), (Z_MATE, 1), (Z_FIRST, 0), (ATTEND_BACK, 1), (QKV_GRADS, 0), (QKV_GRADS, 1),
    (QKV_GRADS, 2), (Z_FIRST, 1), (Z_SECOND, 0), (QKV_GRADS, 3), (FIRST, QKV), (NEAR, UP, 0),
    (NORM_GRADS, 0), (NORM_GRADS, 1), (Z_MATE, 3), (Z_MATE, 2), (Z_SECOND, 1), (NORM_GRADS, 2),
    (Z_FINISH, 0), (Z_FIRST, 3), (NEAR, UP, 1), (NORM_GRADS, 3), (Z_FIRST, 2), (SECOND, OD, 1),
    (Z_SECOND, 3), (Z_MATE, 5), (SECOND, UP, 0), (VEC_ONE,), (NEAR, QKV, 1), (FAR_SIDE, OD, 1),
    (Z_SECOND, 2), (Z_MATE, 4), (Z_FIRST, 5), (SECOND, UP, 1), (FINISH, OD, 1), (NEAR, QKV, 0),
    (Z_FIRST, 4), (Z_FINISH, 1), (FAR_SIDE, UP, 0), (Z_SECOND, 5), (VEC_TWO,), (SECOND, OD, 0),
    (FAR_SIDE, UP, 1), (VEC_THREE,), (Z_FINISH, 3), (SECOND, QKV, 1), (Z_SECOND, 4),
    (SECOND, QKV, 0), (FAR_SIDE, OD, 0), (FINISH, UP, 1), (FAR_SIDE, QKV, 1), (FAR_SIDE, QKV, 0),
    (FINISH, QKV, 1), (Z_FINISH, 2), (FINISH, QKV, 0), (FINISH, OD, 0), (SETTLE,),
    (FINISH, UP, 0), (Z_FINISH, 5), (Z_FINISH, 4),
)


def wide(v):
    return v.astype(WIDE)


def nn(a, b):
    return jnp.dot(a, b, preferred_element_type=WIDE)


def nt(a, b):
    return lax.dot_general(a, b, (((1,), (1,)), ((), ())), preferred_element_type=WIDE)


def turn_over(eye, v):
    return nt(eye[...], v).astype(LOW)


def fill_eye(eye):
    row = lax.broadcasted_iota(jnp.int32, eye.shape, 0)
    eye[...] = wide(row == lax.broadcasted_iota(jnp.int32, eye.shape, 1)).astype(LOW)


def cols(k, size):
    return pl.ds(pl.multiple_of(k * size, size), size)


def turned(v, cos_table, sin_table):
    first = v[:, :LANES]
    lane = lax.broadcasted_iota(jnp.int32, first.shape, 1)
    swapped = jnp.where(
        lane < ROT // 2,
        pltpu.roll(first, LANES - ROT // 2, 1),
        pltpu.roll(first, ROT // 2, 1),
    )
    return jnp.concatenate([first * cos_table + swapped * sin_table, v[:, LANES:]], axis=1)


def soft_columns(query, key, start, first):
    scores = nt(key, query) * (HD**-0.5)
    key_at = lax.broadcasted_iota(jnp.int32, scores.shape, 0)
    query_at = lax.broadcasted_iota(jnp.int32, scores.shape, 1) + first
    allowed = (wide(key_at) >= start) & (key_at <= query_at)
    scores = jnp.where(allowed, scores, masked_score)
    powers = jnp.exp(scores - jnp.max(scores, axis=0, keepdims=True))
    return powers * (1.0 / jnp.sum(powers, axis=0, keepdims=True))


def streamed(count, copies, use):
    for c in copies(0, 0):
        c.start(priority=1)

    @pl.loop(0, count)
    def _(k):
        slot = lax.rem(k, 2)

        @pl.when(k + 1 < count)
        def _():
            for c in copies(k + 1, 1 - slot):
                c.start(priority=1)

        for c in copies(k, slot):
            c.wait()
        use(k, slot)


def play(order, loops, act):
    at = 0
    while at < len(order):
        kind = order[at][0]
        if kind not in loops:
            act(*order[at])
            at += 1
            continue
        hooks, due = {}, []
        end = max(k for k, entry in enumerate(order) if entry[0] == kind)
        for entry in order[at + 1 : end + 1]:
            if entry[0] == kind:
                if due:
                    hooks[entry[1]] = due
                due = []
            else:
                due.append(entry)
        loops[kind](hooks)
        at = end + 1


def forward_kernel(
    x_in, dy_in, lengths, vectors_in, up_in, qkv_in, out_in, down_in,
    dy_out, up_out, qkv_out, od_out, vecs_out, one_out, two_out, unit_out, heads_out, cat_out,
    slope_out, turn_out, soft_out, grad_out,
    xv, len_v, vec_w, one, two, unit, dy_v, up_w, qkv_w, cat, slope, heads, turn, flip_one, flip_two, stage,
    pre_one, pre_two, soft, begin, eye, len_in, vec_s, up_s, qkv_s, od_s, up_f, qkv_f, out_f, down_f,
    send, recv, ring_send, ring_recv, len_sems, local_sems, keep_sems, stage_sems, wide_sems,
):
    y, x, z, core = place()
    zl = z % 2
    tensor = (z // 2) * 2 + core
    head = tensor * 2 + zl
    other = 1 - zl
    partner = device(y, x, z + 1 - 2 * zl, core)
    xp, xm, yp, ym = around(x, 1), around(x, -1), around(y, 1), around(y, -1)
    zp, zm = around(z, 1), around(z, -1)
    xo, yo, zo = around(x, 2), around(y, 2), around(z, 2)
    to_xp, to_xm = device(y, xp, z, core), device(y, xm, z, core)
    to_yp, to_ym = device(yp, x, z, core), device(ym, x, z, core)
    to_zp, to_zm = device(y, x, zp, core), device(y, x, zm, core)
    mate = device(y, x, z, 1 - core)
    line_x = (to_xp, device(y, xo, z, core), to_xm)
    line_y = (to_yp, device(yo, x, z, core), to_ym)
    neighbours = [*line_x, *line_y, to_zp, to_zm, mate]
    greet(neighbours)

    wide_copies = [
        pltpu.make_async_copy(src, dst, wide_sems.at[k])
        for k, (src, dst) in enumerate(
            ((up_in, up_f), (qkv_in, qkv_f), (out_in, out_f), (down_in, down_f))
        )
    ]
    for c in wide_copies:
        c.start(priority=1)
    for r in range(4):
        len_in[r : r + 1, :] = jnp.full((1, LANES), lengths[0, r].astype(WIDE))
    len_in[4:8, :] = jnp.zeros((4, LANES), WIDE)
    fill_eye(eye)
    vec_s[...] = jnp.zeros(vec_s.shape, WIDE)
    vec = wide(vectors_in[...].astype(LOW))
    for h in range(2):
        vec_s[h, 0 : vec.shape[0], 0 : vec.shape[1]] = vec

    def prepare(i):
        if i == UP:
            wide_copies[0].wait()
            n = up_s.shape[-1]
            for h in range(2):
                up_s[h] = up_f[:, h * n : (h + 1) * n].astype(LOW)
        elif i == QKV:
            wide_copies[1].wait()
            for h in range(2):
                for c in range(3):
                    at = slice(c * HD, (c + 1) * HD)
                    qkv_s[h, :, at] = qkv_f[c, :, h * HD : (h + 1) * HD].astype(LOW)
        else:
            wide_copies[2].wait()
            wide_copies[3].wait()
            n = od_s.shape[-1] - HD
            for h in range(2):
                od_s[h, :, 0:HD] = out_f[:, h * HD : (h + 1) * HD].astype(LOW)
                od_s[h, :, HD:] = down_f[:, h * n : (h + 1) * n].astype(LOW)

    w_in = (vec_s, up_s, qkv_s, od_s)
    w_out = (vec_w, up_out, qkv_out, od_out)
    started, note = {}, [None]

    def go(make):
        make().start()
        started[note[0]] = make

    def own_copy(k):
        if k < 4:
            src, dst = w_in[k].at[zl], w_out[k].at[y, x, zl]
        elif k < 6:
            src, dst = rings[k - 4][0], rings[k - 4][1].at[zl, tensor]
        else:
            src, dst = len_in, len_v.at[zl]
        return pltpu.make_async_copy(src, dst, local_sems.at[k])

    rings = ((x_in, xv), (dy_in, dy_out))
    for k in (VEC, 4, 5, 6):
        own_copy(k).start(priority=1)
    for i in (UP, QKV, OD):
        prepare(i)
        own_copy(i).start(priority=1)
    meet(neighbours)

    posts = [mailbox(note, send, recv, i) for i in range(4)]
    ring_posts = [mailbox(note, ring_send, ring_recv, j) for j in range(2)]
    four = (to_xp, to_xm, to_yp, to_ym)

    def slot_of(ref, zz, cc):
        return ref.at[zz % 2, (zz // 2) * 2 + cc]

    def arrived(i, k, ref):
        posts[i](k, ref, ref, mate).wait_recv()

    def ring_arrived(j, k, ref):
        ring_posts[j](k, ref, ref, mate).wait_recv()

    def halves_of(blk):
        n = blk.shape[0] // 2
        return blk.at[pl.ds(0, n)], blk.at[pl.ds(n, n)]

    def swap(i):
        go(lambda: posts[i](32, w_in[i].at[other], w_out[i].at[y, x, zl], partner))

    def own_half(i):
        for d in range(4):
            go(lambda d=d: posts[i](d, w_in[i].at[zl], w_out[i].at[y, x, zl], four[d]))

    def other_half(i):
        mine = lambda: w_out[i].at[y, x, other]
        arrived(i, 32, mine())
        for d in range(4):
            go(lambda d=d: posts[i](4 + d, mine(), mine(), four[d]))

    def round_one_x(i):
        w = w_out[i]
        blk = lambda: w.at[y, xm, zl]
        arrived(i, 0, blk())
        go(lambda blk=blk: posts[i](8, halves_of(blk())[0], halves_of(blk())[0], to_xp))
        go(lambda blk=blk: posts[i](12, blk(), blk(), to_yp))
        go(lambda blk=blk: posts[i](13, blk(), blk(), to_ym))
        blk = lambda: w.at[y, xp, zl]
        arrived(i, 1, blk())
        go(lambda blk=blk: posts[i](9, halves_of(blk())[1], halves_of(blk())[1], to_xm))
        go(lambda blk=blk: posts[i](14, blk(), blk(), to_yp))
        go(lambda blk=blk: posts[i](15, blk(), blk(), to_ym))

    def round_one_y(i):
        w = w_out[i]
        blk = lambda: w.at[ym, x, other]
        arrived(i, 6, blk())
        go(lambda blk=blk: posts[i](10, halves_of(blk())[0], halves_of(blk())[0], to_yp))
        go(lambda blk=blk: posts[i](18, blk(), blk(), to_xp))
        go(lambda blk=blk: posts[i](19, blk(), blk(), to_xm))
        blk = lambda: w.at[yp, x, other]
        arrived(i, 7, blk())
        go(lambda blk=blk: posts[i](11, halves_of(blk())[1], halves_of(blk())[1], to_ym))
        go(lambda blk=blk: posts[i](20, blk(), blk(), to_xp))
        go(lambda blk=blk: posts[i](21, blk(), blk(), to_xm))

    def round_two_a(i):
        w = w_out[i]
        blk = lambda: w.at[ym, x, zl]
        arrived(i, 2, blk())
        go(lambda blk=blk: posts[i](24, blk(), blk(), to_yp))
        blk = lambda: w.at[y, xm, other]
        arrived(i, 4, blk())
        go(lambda blk=blk: posts[i](28, blk(), blk(), to_xp))

    def round_two_b(i):
        w = w_out[i]
        blk = lambda: w.at[y, xo, zl]
        arrived(i, 8, halves_of(blk())[0])
        arrived(i, 9, halves_of(blk())[1])
        go(lambda blk=blk: posts[i](16, blk(), blk(), to_yp))
        go(lambda blk=blk: posts[i](17, blk(), blk(), to_ym))
        blk = lambda: w.at[yo, x, other]
        arrived(i, 10, halves_of(blk())[0])
        arrived(i, 11, halves_of(blk())[1])
        go(lambda blk=blk: posts[i](22, blk(), blk(), to_xp))
        go(lambda blk=blk: posts[i](23, blk(), blk(), to_xm))

    def round_two_c(i):
        w = w_out[i]
        blk = lambda: w.at[ym, xm, zl]
        arrived(i, 12, blk())
        go(lambda blk=blk: posts[i](25, blk(), blk(), to_yp))
        blk = lambda: w.at[yp, xp, zl]
        arrived(i, 15, blk())
        go(lambda blk=blk: posts[i](26, blk(), blk(), to_ym))
        blk = lambda: w.at[ym, xm, other]
        arrived(i, 18, blk())
        go(lambda blk=blk: posts[i](29, blk(), blk(), to_xp))
        blk = lambda: w.at[yp, xp, other]
        arrived(i, 21, blk())
        go(lambda blk=blk: posts[i](30, blk(), blk(), to_xm))

    def round_three(i):
        w = w_out[i]
        blk = lambda: w.at[yp, xo, zl]
        arrived(i, 17, blk())
        go(lambda blk=blk: posts[i](27, blk(), blk(), to_ym))
        blk = lambda: w.at[yo, xp, other]
        arrived(i, 23, blk())
        go(lambda blk=blk: posts[i](31, blk(), blk(), to_xm))

    def last_round(i):
        if i == OD:
            for key in list(started)[:-20]:
                started.pop(key)().wait_send()
        w = w_out[i]
        arrived(i, 3, w.at[yp, x, zl])
        arrived(i, 5, w.at[y, xp, other])
        arrived(i, 13, w.at[yp, xm, zl])
        arrived(i, 14, w.at[ym, xp, zl])
        arrived(i, 16, w.at[ym, xo, zl])
        arrived(i, 19, w.at[ym, xp, other])
        arrived(i, 20, w.at[yp, xm, other])
        arrived(i, 22, w.at[yo, xm, other])
        arrived(i, 24, w.at[yo, x, zl])
        arrived(i, 25, w.at[yo, xm, zl])
        arrived(i, 26, w.at[yo, xp, zl])
        arrived(i, 27, w.at[yo, xo, zl])
        arrived(i, 28, w.at[y, xo, other])
        arrived(i, 29, w.at[ym, xo, other])
        arrived(i, 30, w.at[yp, xo, other])
        arrived(i, 31, w.at[yo, xo, other])

    def ring_own(j):
        a, b = rings[j]
        for k, to in enumerate((to_zp, to_zm, mate)):
            go(lambda k=k, to=to: ring_posts[j](k, a, slot_of(b, z, core), to))

    def ring_on(j):
        b = rings[j][1]
        blk = lambda: slot_of(b, zm, core)
        ring_arrived(j, 0, blk())
        go(lambda blk=blk: ring_posts[j](3, halves_of(blk())[0], halves_of(blk())[0], to_zp))
        go(lambda blk=blk: ring_posts[j](5, blk(), blk(), mate))
        blk = lambda: slot_of(b, zp, core)
        ring_arrived(j, 1, blk())
        go(lambda blk=blk: ring_posts[j](4, halves_of(blk())[1], halves_of(blk())[1], to_zm))
        go(lambda blk=blk: ring_posts[j](6, blk(), blk(), mate))

    def ring_far(j):
        blk = lambda: slot_of(rings[j][1], zo, core)
        ring_arrived(j, 3, halves_of(blk())[0])
        ring_arrived(j, 4, halves_of(blk())[1])
        go(lambda blk=blk: ring_posts[j](7, blk(), blk(), mate))

    def ring_last(j):
        b = rings[j][1]
        ring_arrived(j, 2, slot_of(b, z, 1 - core))
        ring_arrived(j, 5, slot_of(b, zm, 1 - core))
        ring_arrived(j, 6, slot_of(b, zp, 1 - core))
        ring_arrived(j, 7, slot_of(b, zo, 1 - core))

    kept = {}

    def keep(k, src, dst):
        make = lambda: pltpu.make_async_copy(src, dst, keep_sems.at[k])
        make().start(priority=1)
        kept[k] = make

    def fetch(k, src, dst):
        fetched[k] = lambda: pltpu.make_async_copy(src, dst, local_sems.at[7 + k])
        fetched[k]().start(priority=1)

    def fetch_for(i):
        if i == UP:
            own_copy(UP).wait()
            fetch(0, up_out, up_w)
        elif i == QKV:
            own_copy(QKV).wait()
            fetch(1, qkv_out, qkv_w)
        else:
            own_copy(5).wait()
            ring_last(1)
            fetch(2, dy_out, dy_v)

    def tables():
        lengths_copy().wait_recv()
        own_copy(6).wait()

        @pl.loop(0, 8)
        def _(k):
            g, part = k // 4, k % 4
            shape = (LANES, LANES)
            row = wide(lax.broadcasted_iota(jnp.int32, shape, 0) + part * LANES)
            lane = lax.broadcasted_iota(jnp.int32, shape, 1)
            start = jnp.zeros(shape, WIDE)
            end = jnp.zeros((1, LANES), WIDE)
            for s in range(4):
                end = end + len_v[g, s : s + 1, :]
                start = jnp.where(row >= end, jnp.broadcast_to(end, shape), start)
            half_rot = ROT // 2
            step = wide(lane % half_rot) * (-2.0 * math.log(10000.0) / ROT)
            angle = (row - start) * jnp.exp(step)
            sine = jnp.sin(angle)
            rows = cols(k, LANES)
            turn[0, rows] = jnp.where(lane < ROT, jnp.cos(angle), 1.0)
            turn[1, rows] = jnp.where(lane < half_rot, -sine, jnp.where(lane < ROT, sine, 0.0))

        for g in range(2):
            column = wide(lax.broadcasted_iota(jnp.int32, (1, GROUP), 1))
            start = jnp.zeros((1, GROUP), WIDE)
            end = jnp.zeros((1, LANES), WIDE)
            for r in range(4):
                end = end + len_v[g, r : r + 1, :]
                ends = jnp.concatenate([end] * (GROUP // LANES), axis=1)
                start = jnp.where(column >= ends, ends, start)
            begin[g : g + 1, :] = start

        keep(0, turn, turn_out)

    def vectors_x():
        own_copy(VEC).wait()
        arrived(VEC, 32, vec_w.at[y, x, other])
        for k in range(3):
            go(lambda k=k: posts[VEC](k, vec_w.at[y, x], vec_w.at[y, x], line_x[k]))

    def vectors_y():
        for k in range(3):
            arrived(VEC, k, vec_w.at[y, x])
        for k in range(3):
            go(lambda k=k: posts[VEC](3 + k, vec_w.at[y], vec_w.at[y], line_y[k]))

    def vectors():
        for k in range(3):
            arrived(VEC, 3 + k, vec_w.at[y])
        for p in range(RING_SIZE * RING_SIZE):
            lead, tail = vec_w[p // RING_SIZE, p % RING_SIZE, 0], vec_w[p // RING_SIZE, p % RING_SIZE, 1]
            vecs_out[:, p * LANES : (p + 1) * LANES] = lead + pltpu.roll(tail, LANES // 2, 1)

    def norm(zz, cc):
        b = (zz % 2) * RING_SIZE + (zz // 2) * 2 + cc

        @pl.loop(0, 4)
        def _(k):
            v = wide(xv[zz % 2, (zz // 2) * 2 + cc, cols(k, 32)])
            centred = v - jnp.mean(v, axis=-1, keepdims=True)
            var = jnp.mean(centred * centred, axis=-1, keepdims=True)
            u = centred * lax.rsqrt(var + norm_eps)
            to = cols(b * 4 + k, 32)
            unit[to] = u.astype(LOW)
            one[to] = (u * vecs_out[0:1, :] + vecs_out[1:2, :]).astype(LOW)
            two[to] = (u * vecs_out[2:3, :] + vecs_out[3:4, :]).astype(LOW)

    def norms(k):
        if k == 0:
            own_copy(4).wait()
            norm(z, core)
        elif k == 1:
            ring_arrived(0, 2, slot_of(xv, z, 1 - core))
            norm(z, 1 - core)
        elif k == 2:
            norm(zm, core)
            norm(zp, core)
        elif k == 4:
            ring_arrived(0, 5, slot_of(xv, zm, 1 - core))
            norm(zm, 1 - core)
            ring_arrived(0, 6, slot_of(xv, zp, 1 - core))
            norm(zp, 1 - core)
        else:
            norm(zo, core)
            ring_arrived(0, 7, slot_of(xv, zo, 1 - core))
            norm(zo, 1 - core)

    def at_step(hooks, k):
        for due, entries in hooks.items():

            @pl.when(k == due)
            def _():
                for entry in entries:
                    act(*entry)

    def keep_rows():
        if 1 not in kept:
            keep(1, one, one_out)
            keep(2, two, two_out)
            keep(3, unit, unit_out)

    def gelu(pre, m, n):
        size = pre.shape[1]
        rows = pl.ds(m * GROUP, GROUP)
        at = pl.ds(pl.multiple_of(n * size + TILE, TILE), size)
        hidden = pre[...]
        cdf = 0.5 * (1.0 + lax.erf(hidden * inv_root_two))
        cat[rows, at] = (hidden * cdf).astype(LOW)
        bell = hidden * jnp.exp(-0.5 * hidden * hidden) * inv_root_tau
        slope[rows, at] = (cdf + bell).astype(LOW)

    def hidden_tiles(hooks):
        keep_rows()
        fetched[0]().wait()
        size = pre_one.shape[1]
        last = up_w.shape[-1] // size

        @pl.loop(0, last)
        def _(n):
            w = up_w[:, :, :, :, cols(n, size)].reshape(-1, size)
            bias = vecs_out[pl.ds(9 + head // 2, 1), cols((head % 2) * last + n, size)]
            at_step(hooks, 2 * n)
            gelu(pre_two, 1, (n + last - 1) % last)
            pre_one[...] = nn(two[0:GROUP], w) + bias
            at_step(hooks, 2 * n + 1)
            gelu(pre_one, 0, n)
            pre_two[...] = nn(two[GROUP:], w) + bias

        gelu(pre_two, 1, last - 1)
        slope[:, 0:TILE] = jnp.ones((2 * GROUP, TILE), LOW)
        keep(4, slope, slope_out)

    def project(hooks):
        keep_rows()
        fetched[1]().wait()

        @pl.loop(0, 2)
        def _(m):
            at_step(hooks, m)
            rows = cols(m, GROUP)
            all_three = nn(one[rows], qkv_w[...].reshape(-1, 3 * HD))
            for c in range(3):
                pre = all_three[:, c * HD : (c + 1) * HD] + vecs_out[4 + c : 5 + c, cols(head, HD)]
                if c < 2:
                    pre = turned(pre, turn[0, rows], turn[1, rows])
                heads[c, rows] = pre.astype(LOW)

        keep(5, heads, heads_out)

    def attend(hooks):
        @pl.loop(0, 2)
        def _(g):
            at_step(hooks, g)
            for part in range(2):
                rows, keys = cols(2 * g + part, TILE), pl.ds(cols(g, GROUP).start, (part + 1) * TILE)
                start = begin[pl.ds(g, 1), part * TILE : (part + 1) * TILE]
                columns = soft_columns(heads[0, rows], heads[1, keys], start, part * TILE)
                columns = columns.astype(LOW)
                soft[g, part, 0 : (part + 1) * TILE] = columns
                cat[rows, 0:HD] = nn(turn_over(eye, columns), heads[2, keys]).astype(LOW)

        keep(7, soft, soft_out)

    def od_grads(hooks):
        keep(6, cat, cat_out)
        fetched[2]().wait()
        flips = (flip_one, flip_two)

        def flip(to, k, e):
            tile = dy_v[:, :, :, cols(2 * k + e, TILE)].reshape(-1, TILE)
            to[e * TILE : (e + 1) * TILE, :] = turn_over(eye, tile)

        def staged(k, half):
            return pltpu.make_async_copy(stage.at[half], grad_out.at[k], stage_sems.at[half])

        for e in range(2):
            flip(flip_one, 0, e)

        @pl.loop(0, 2)
        def _(kk):
            for half in range(2):
                k = 2 * kk + half
                at_step(hooks, k)

                @pl.when(kk > 0)
                def _():
                    staged(k - 2, half).wait()

                for part, at in enumerate((WIDE_PART, REST)):
                    res = nn(flips[half][...], cat[:, at]).astype(LOW)
                    flip(flips[1 - half], (k + 1) % RING_SIZE, part)
                    stage[half, :, :, :, at] = res.reshape(RING_SIZE, 2, -1, at.stop - at.start)

                staged(k, half).start(priority=1)

        for half in range(2):
            staged(2 + half, half).wait()

    fetched = {}
    def lengths_copy():
        return pltpu.make_async_remote_copy(
            src_ref=len_in,
            dst_ref=len_v.at[zl],
            send_sem=len_sems.at[0],
            recv_sem=len_sems.at[1],
            device_id=partner,
            device_id_type=MESH,
        )

    moves = {
        SWAP: swap,
        OWN: own_half,
        OTHER: other_half,
        ROUND_ONE_X: round_one_x,
        ROUND_ONE_Y: round_one_y,
        ROUND_TWO_A: round_two_a,
        ROUND_TWO_B: round_two_b,
        ROUND_TWO_C: round_two_c,
        ROUND_THREE: round_three,
        LAST_ROUND: last_round,
        RING: ring_own,
        RING_ON: ring_on,
        RING_FAR: ring_far,
        TABLES: tables,
        VECTORS_X: vectors_x,
        VECTORS_Y: vectors_y,
        VECTORS: vectors,
        NORM: norms,
        FETCH: fetch_for,
    }

    def act(kind, *args):
        moves[kind](*args)

    loops = {HIDDEN: hidden_tiles, PROJECT: project, ATTEND: attend, OD_GRADS: od_grads}
    lengths_copy().start()
    play(FORWARD_ORDER, loops, act)
    own_copy(3).wait()
    lengths_copy().wait_send()
    for make in started.values():
        make().wait_send()
    for make in kept.values():
        make().wait()


def forward(rows, cot, lengths, vectors, weights):
    tokens, model = rows.shape
    total = 2 * RING_SIZE * tokens
    up, qkv, out_w, down = weights
    owned = up.shape[0]
    widths = (LANES, up.shape[1] // 2, 3 * HD, (out_w.shape[1] + down.shape[1]) // 2)
    halves = [(2, 16, LANES), *((2, owned, w) for w in widths[1:])]
    plane = [(RING_SIZE, RING_SIZE, *h) for h in halves]
    cat_cols = widths[3]
    shape = jax.ShapeDtypeStruct
    out = [
        shape((2, RING_SIZE, tokens, model), LOW),
        shape(plane[1], LOW),
        shape(plane[2], LOW),
        shape(plane[3], LOW),
        shape((16, model), WIDE),
        shape((total, model), LOW),
        shape((total, model), LOW),
        shape((total, model), LOW),
        shape((3, total, HD), LOW),
        shape((total, cat_cols), LOW),
        shape((total, cat_cols), LOW),
        shape((2, total, LANES), WIDE),
        shape((2, 2, GROUP, TILE), LOW),
        shape(plane[3], LOW),
    ]
    specs = [VMEM if k == 4 else ANY for k in range(len(out))]
    return pl.pallas_call(
        forward_kernel,
        out_shape=out,
        in_specs=[ANY, ANY, pl.BlockSpec(memory_space=pltpu.SMEM), VMEM, ANY, ANY, ANY, ANY],
        out_specs=specs,
        scratch_shapes=[
            pltpu.VMEM((2, RING_SIZE, tokens, model), LOW),
            pltpu.VMEM((2, 8, LANES), WIDE),
            pltpu.VMEM(plane[0], WIDE),
            pltpu.VMEM((total, model), LOW),
            pltpu.VMEM((total, model), LOW),
            pltpu.VMEM((total, model), LOW),
            pltpu.VMEM((2, RING_SIZE, tokens, model), LOW),
            pltpu.VMEM(plane[1], LOW),
            pltpu.VMEM(plane[2], LOW),
            pltpu.VMEM((total, cat_cols), LOW),
            pltpu.VMEM((total, cat_cols), LOW),
            pltpu.VMEM((3, total, HD), LOW),
            pltpu.VMEM((2, total, LANES), WIDE),
            pltpu.VMEM((GROUP, total), LOW),
            pltpu.VMEM((GROUP, total), LOW),
            pltpu.VMEM((2, RING_SIZE, 2, owned, cat_cols), LOW),
            pltpu.VMEM((GROUP, GROUP), WIDE),
            pltpu.VMEM((GROUP, GROUP), WIDE),
            pltpu.VMEM((2, 2, GROUP, TILE), LOW),
            pltpu.VMEM((8, GROUP), WIDE),
            pltpu.VMEM((TILE, TILE), LOW),
            pltpu.VMEM((8, LANES), WIDE),
            pltpu.VMEM(halves[0], WIDE),
            *(pltpu.VMEM(h, LOW) for h in halves[1:]),
            *(pltpu.VMEM(w.shape, WIDE) for w in weights),
            pltpu.SemaphoreType.DMA((4, PLANE_MESSAGES)),
            pltpu.SemaphoreType.DMA((4, PLANE_MESSAGES)),
            pltpu.SemaphoreType.DMA((2, RING_MESSAGES)),
            pltpu.SemaphoreType.DMA((2, RING_MESSAGES)),
            pltpu.SemaphoreType.DMA((2,)),
            pltpu.SemaphoreType.DMA((10,)),
            pltpu.SemaphoreType.DMA((8,)),
            pltpu.SemaphoreType.DMA((2,)),
            pltpu.SemaphoreType.DMA((4,)),
        ],
        compiler_params=pltpu.CompilerParams(
            collective_id=0, has_side_effects=True, vmem_limit_bytes=62 * 2**20
        ),
        name="forward_and_gather",
    )(rows, cot, lengths, vectors, *weights)


def backward_kernel(
    dy_in, up_in, qkv_in, od_in, vecs, one_in, two_in, unit_in, heads_in, cat_in, slope_in,
    turn_in, soft_in, od_grad,
    own_od_out, own_up_out, own_qkv_out, swap_od, swap_up, swap_qkv, vec_out, u_zero_out, u_one_out,
    own_od, own_up, own_qkv, u_zero, u_one,
    up_grad, qkv_grad, dcat, cat, heads, turn, soft, flip_one, flip_two, vecg, vec_block,
    od_near, od_me, od_full, tiles, eye,
    part_zero, both_zero, zfar_zero, znear_zero, part_one, both_one, zfar_one, znear_one,
    far_od, near_od, far2_od, near2_od, out_od,
    far_up, near_up, far2_up, near2_up, out_up,
    far_qkv, near_qkv, far2_qkv, near2_qkv, out_qkv,
    vec_x, vec_y, vec_z, vec_row, vec_own,
    send, recv, z_send, z_recv, v_send, v_recv, load_sems, stream_sems, out_sems,
):
    y, x, z, core = place()
    zl = z % 2
    head = ((z // 2) * 2 + core) * 2 + zl
    other = 1 - zl
    partner = device(y, x, z + 1 - 2 * zl, core)
    xp, xm, yp, ym = around(x, 1), around(x, -1), around(y, 1), around(y, -1)
    zp, zm = around(z, 1), around(z, -1)
    xo, yo, zo = around(x, 2), around(y, 2), around(z, 2)
    to_x = (device(y, xp, z, core), device(y, xm, z, core))
    to_y = (device(yp, x, z, core), device(ym, x, z, core))
    to_z = (partner, device(y, x, around(z, 2 * zl - 1), core))
    mate = device(y, x, z, 1 - core)
    line_x = (to_x[0], device(y, xo, z, core), to_x[1])
    line_y = (to_y[0], device(yo, x, z, core), to_y[1])
    line_z = [mate]
    for k in (1, 2, 3):
        for c in (0, 1):
            line_z.append(device(y, x, around(z, k), (core + c) % 2))
    neighbours = [*line_x, *line_y, *line_z]
    greet(neighbours)

    def load(k, src, dst):
        copy = pltpu.make_async_copy(src, dst, load_sems.at[k])
        copy.start(priority=1)
        return copy

    half_model = part_zero.shape[-1]
    loads = []
    for c in range(2):
        at = slice(c * half_model, (c + 1) * half_model)
        loads.append(load(c, dy_in.at[:, :, :, :, at], part_zero.at[c]))
    thirds = (slice(0, 512), slice(512, 1024), slice(1024, 1280))
    third_loads = []
    for k, at in enumerate(thirds):
        od_load = load(13 + k, od_in.at[:, :, :, :, at], od_full.at[:, :, :, :, at])
        third_loads.append((od_load, load((2, 16, 17)[k], slope_in.at[:, at], dcat.at[:, at])))
    near_loads = []
    for way, half in enumerate((zl, other)):
        for d in range(2):
            two = pl.ds(2 * d, 2)
            src = (two, (xp, xm)[d], half) if way == 0 else ((yp, ym)[d], two, half)
            near_loads.append(load(3 + 2 * way + d, od_grad.at[src], od_near.at[way, d]))
        every = pl.ds(0, RING_SIZE)
        src = (every, x, half) if way == 0 else (y, every, half)
        near_loads.append(load(7 + way, od_grad.at[src], od_me.at[way]))
    late = [
        load(9, heads_in, heads),
        load(10, turn_in, turn),
        load(11, cat_in, cat),
        load(12, soft_in, soft),
    ]
    meet(neighbours)

    started, note = {}, [None]

    def go(make):
        make().start()
        started[note[0]] = make

    g_ref = {OD: od_grad, UP: up_grad, QKV: qkv_grad}
    bufs = {
        OD: (far_od, near_od, far2_od, near2_od, out_od, own_od, swap_od),
        UP: (far_up, near_up, far2_up, near2_up, out_up, own_up, swap_up),
        QKV: (far_qkv, near_qkv, far2_qkv, near2_qkv, out_qkv, own_qkv, swap_qkv),
    }
    posts = {i: mailbox(note, send, recv, i - 1) for i in (UP, QKV, OD)}
    z_posts = [mailbox(note, z_send, z_recv, j) for j in range(6)]
    v_post = mailbox(note, v_send, v_recv)

    def arrived(i, k, ref):
        posts[i](k, ref, ref, mate).wait_recv()

    def z_arrived(j, k, ref):
        z_posts[j](k, ref, ref, mate).wait_recv()

    halves = (zl, other)
    first_to, second_to = (to_x, to_y), (to_y, to_x)
    first = ((xp, xm, xo, x), (yp, ym, yo, y))
    second = ((yp, ym, yo, y), (xp, xm, xo, x))
    pair = (pl.ds(0, 2), pl.ds(2, 2))
    part_rows = (pl.ds(0, 32), pl.ds(32, 32))

    def block(i, way, along, across):
        if way == 0:
            return g_ref[i].at[across, along, halves[0]]
        return g_ref[i].at[along, across, halves[1]]

    def near_value(i, way, d, k):
        if i == OD:
            return od_near[way, d, k]
        return block(i, way, first[way][d], k + 2 * d)[...]

    def me_value(i, way, k, rows):
        if i == OD:
            return od_me[way, k, rows]
        return block(i, way, first[way][3], k).at[rows][...]

    def send_first(i):
        far, near = bufs[i][:2]
        for way in range(2):
            for d in range(2):
                go(
                    lambda way=way, d=d: posts[i](
                        way * 12 + d,
                        block(i, way, first[way][2], pair[d]),
                        far.at[way, d],
                        first_to[way][d],
                    )
                )
        for way in range(2):
            for d in range(2):
                go(
                    lambda way=way, d=d: posts[i](
                        way * 12 + 2 + d,
                        block(i, way, first[way][d], pair[1 - d]),
                        near.at[way, d, pair[1 - d]],
                        first_to[way][d],
                    )
                )

    def send_near(i, way):
        far, near = bufs[i][:2]
        for d in range(2):
            arrived(i, way * 12 + d, far.at[way, d])
            for k in range(2):
                far[way, d, k] = far[way, d, k] + near_value(i, way, d, k)
            go(
                lambda d=d: posts[i](
                    way * 12 + 4 + d, far.at[way, d], near.at[way, d, pair[d]], first_to[way][d]
                )
            )

    def send_second(i, way):
        far, near, far_two, near_two = bufs[i][:4]
        for d in range(2):
            arrived(i, way * 12 + 2 + d, near.at[way, d, pair[1 - d]])
            arrived(i, way * 12 + 4 + d, near.at[way, d, pair[d]])

        @pl.loop(0, 2 * RING_SIZE)
        def _(t):
            k, rows = t // 2, cols(t % 2, 32)
            total = near[way, 0, k, rows] + near[way, 1, k, rows]
            near[way, 0, k, rows] = total + me_value(i, way, k, rows)

        for d in range(2):
            go(
                lambda d=d: posts[i](
                    way * 12 + 6 + d,
                    near.at[way, 0, second[way][2], part_rows[d]],
                    far_two.at[way, d],
                    second_to[way][d],
                )
            )
        for d in range(2):
            go(
                lambda d=d: posts[i](
                    way * 12 + 8 + d,
                    near.at[way, 0, second[way][d], part_rows[1 - d]],
                    near_two.at[way, d, part_rows[1 - d]],
                    second_to[way][d],
                )
            )

    def send_last(i, way):
        far, near, far_two, near_two = bufs[i][:4]
        for d in range(2):
            arrived(i, way * 12 + 6 + d, far_two.at[way, d])
            rows = part_rows[d]
            far_two[way, d] = far_two[way, d] + near[way, 0, second[way][d], rows]
            go(
                lambda d=d: posts[i](
                    way * 12 + 10 + d,
                    far_two.at[way, d],
                    near_two.at[way, d, part_rows[d]],
                    second_to[way][d],
                )
            )

    def finish(i, way):
        near, near_two, out, mine, swapped = (bufs[i][k] for k in (1, 3, 4, 5, 6))
        for d in range(2):
            arrived(i, way * 12 + 8 + d, near_two.at[way, d, part_rows[1 - d]])
            arrived(i, way * 12 + 10 + d, near_two.at[way, d, part_rows[d]])
        total = wide(near[way, 0, second[way][3]]) + wide(near_two[way, 0]) + wide(near_two[way, 1])
        if way == 1:
            out[...] = total.astype(LOW)
            go(lambda: posts[i](24, out, swapped, partner))
        else:
            mine[...] = total.astype(LOW)
            out_copy(i - 1).start(priority=1)

    def z_bufs(j):
        if j < 2:
            return [r.at[j] for r in (part_zero, both_zero, zfar_zero, znear_zero)]
        return [r.at[j - 2] for r in (part_one, both_one, zfar_one, znear_one)]

    def z_rows(j):
        lead = 64 if j < 2 else 16
        return pl.ds(0, lead), pl.ds(lead, near_rows - lead)

    near_rows = znear_zero.shape[2]
    z_ends = (z + 1 - 2 * zl, around(z, 2 * zl - 1))

    def z_to_mate(j):
        go(lambda: z_posts[j](0, z_bufs(j)[0].at[:, :, 1 - core], z_bufs(j)[1], mate))

    def z_block(j, zz):
        return z_bufs(j)[1].at[zz % 2, zz // 2]

    def z_first(j):
        part, both, far, near = z_bufs(j)
        z_arrived(j, 0, both)

        @pl.loop(0, 8)
        def _(k):
            b, c, rows = k // 4, (k // 2) % 2, cols(k % 2, 64)
            both[b, c, rows] = both[b, c, rows] + part[b, c, core, rows]

        rows = z_rows(j)
        for d in range(2):
            go(
                lambda d=d: z_posts[j](
                    1 + d, z_block(j, zo).at[rows[d]], z_bufs(j)[2].at[rows[d]], to_z[d]
                )
            )
        for d in range(2):
            go(
                lambda d=d: z_posts[j](
                    3 + d,
                    z_block(j, z_ends[d]).at[rows[d]],
                    z_bufs(j)[3].at[d, rows[d]],
                    to_z[d],
                )
            )

    def z_second(j):
        part, both, far, near = z_bufs(j)
        rows = z_rows(j)
        for d in range(2):
            z_arrived(j, 1 + d, far.at[rows[d]])
            zz = z_ends[1 - d]
            far[rows[d]] = far[rows[d]] + both[zz % 2, zz // 2, rows[d]]
            go(
                lambda d=d: z_posts[j](
                    6 - d, z_bufs(j)[2].at[rows[d]], z_bufs(j)[3].at[1 - d, rows[d]], to_z[1 - d]
                )
            )

    def z_finish(j):
        part, both, far, near = z_bufs(j)
        rows = z_rows(j)
        for d in range(2):
            z_arrived(j, 3 + d, near.at[d, rows[d]])
            z_arrived(j, 5 + d, near.at[d, rows[1 - d]])
        out, at = (u_zero, j) if j < 2 else (u_one, j - 2)
        width = near.shape[-1]
        for k in range(2):
            rows = pl.ds(64 * k, 64)
            total = wide(both[zl, z // 2, rows]) + wide(near[0, rows]) + wide(near[1, rows])
            out[rows, at * width : (at + 1) * width] = total.astype(LOW)
        out_copy(3 + j).start(priority=1)

    def at_step(hooks, k):
        for due, entries in hooks.items():

            @pl.when(k == due)
            def _():
                for entry in entries:
                    act(*entry)

    def out_copy(k):
        if k < 3:
            src, dst = ((own_up, own_up_out), (own_qkv, own_qkv_out), (own_od, own_od_out))[k]
        else:
            j = k - 3
            src, dst = (u_zero, u_zero_out) if j < 2 else (u_one, u_one_out)
            width = src.shape[1] // (2 if j < 2 else 4)
            at = pl.ds((j if j < 2 else j - 2) * width, width)
            src, dst = src.at[:, at], dst.at[:, at]
        return pltpu.make_async_copy(src, dst, out_sems.at[k])

    def cat_grads(hooks):
        for step, (m, at) in enumerate(((m, at) for at in thirds for m in range(2))):
            for entry in hooks.get(step, ()):
                act(*entry)
            if m == 0:
                for c in third_loads[step // 2]:
                    c.wait()
            w = od_full[:, :, :, :, at].reshape(-1, at.stop - at.start)
            rows = pl.ds(m * GROUP, GROUP)
            grad = nn(part_zero[0, m].reshape(GROUP, -1), w[:half_model])
            grad = grad + nn(part_zero[1, m].reshape(GROUP, -1), w[half_model:])
            dcat[rows, at] = (grad * wide(dcat[rows, at])).astype(LOW)

    def weight_grads(hooks, sem, source, rights, to, bias):
        flips = (flip_one, flip_two)
        size = to.shape[-1] // len(rights)

        def copy(k, half):
            at = stream_sems.at[sem, half]
            return pltpu.make_async_copy(source.at[:, cols(k, GROUP)], tiles.at[half], at)

        def flip(half, e):
            at = slice(e * TILE, (e + 1) * TILE)
            flips[half][at, :] = turn_over(eye, tiles[half, :, at])

        for half in range(2):
            copy(half, half).start(priority=1)
        copy(0, 0).wait()

        for e in range(2):
            flip(0, e)

        @pl.loop(0, 2)
        def _(kk):
            for half in range(2):
                k = 2 * kk + half
                at_step(hooks, k)
                if half == 0:
                    copy(k + 1, 1).wait()
                else:

                    @pl.when(kk == 0)
                    def _():
                        copy(k + 1, 0).wait()

                @pl.when(kk == 0)
                def _():
                    copy(k + 2, half).start(priority=1)

                for n, right in enumerate(rights):
                    res = nn(flips[half][...], right[...])
                    row, at = bias(n)
                    vecg[row, at] = res[GROUP : GROUP + 1]
                    part = res[0:GROUP].astype(LOW)
                    to[k, :, :, :, n * size : (n + 1) * size] = part.reshape(RING_SIZE, 2, -1, size)
                for e in range(2):
                    flip(1 - half, e)

    def attend_back(hooks):
        @pl.loop(0, 2)
        def _(g):
            at_step(hooks, g)
            dkey, dvalue = [], []
            for part in range(2):
                rows, count = cols(2 * g + part, TILE), (part + 1) * TILE
                keys = pl.ds(cols(g, GROUP).start, count)
                columns = soft[g, part, 0:count]
                query, key, grad = heads[0, rows], heads[1, keys], dcat[rows, 0:HD]
                dsoft = nt(heads[2, keys], grad)
                inner = jnp.sum(wide(columns) * dsoft, axis=0, keepdims=True)
                dscore = (wide(columns) * (dsoft - inner)).astype(LOW)
                dquery = nn(turn_over(eye, dscore), key) * (HD**-0.5)
                heads[0, rows] = turned(dquery, turn[0, rows], -turn[1, rows]).astype(LOW)
                dkey.append(nn(dscore, query))
                dvalue.append(nn(columns, grad))
            for part in range(2):
                rows, at = cols(2 * g + part, TILE), slice(part * TILE, (part + 1) * TILE)
                whole_key, whole_value = dkey[1][at], dvalue[1][at]
                if part == 0:
                    whole_key, whole_value = whole_key + dkey[0], whole_value + dvalue[0]
                whole_key = turned(whole_key * (HD**-0.5), turn[0, rows], -turn[1, rows])
                heads[1, rows] = whole_key.astype(LOW)
                heads[2, rows] = whole_value.astype(LOW)

    def branch(hooks):
        @pl.loop(0, RING_SIZE)
        def _(k):
            at_step(hooks, k)
            w = od_full[k].reshape(GROUP, -1)
            for m in range(2):
                res = nt(cat[m * GROUP : (m + 1) * GROUP], w).astype(LOW)
                part_zero[k // 2, m, :, :, :, cols(k % 2, GROUP)] = res.reshape(2, 2, -1, GROUP)

    def norm_grads(hooks):
        up_at, qkv_at = slice(0, up_in.shape[-1]), slice(0, qkv_in.shape[-1])

        def copies(k, slot):
            return [
                pltpu.make_async_copy(
                    qkv_in.at[k], od_full.at[2 + slot, :, :, :, qkv_at], stream_sems.at[2, slot]
                ),
                pltpu.make_async_copy(
                    up_in.at[k], od_full.at[slot, :, :, :, up_at], stream_sems.at[3, slot]
                ),
                pltpu.make_async_copy(
                    unit_in.at[:, cols(k, GROUP)], tiles.at[slot], stream_sems.at[4, slot]
                ),
            ]

        def use(k, slot):
            at_step(hooks, k)
            w_one = od_full[2 + slot, :, :, :, qkv_at].reshape(GROUP, -1)
            w_two = od_full[slot, :, :, :, up_at].reshape(GROUP, -1)
            at = cols(k, GROUP)
            sums = [jnp.zeros((1, GROUP), WIDE)] * 4
            for part in range(4):
                m, inner = part // 2, part % 2
                rows = pl.ds(part * TILE, TILE)
                a = nt(heads[0, rows], w_one[:, 0:HD])
                for c in (1, 2):
                    a = a + nt(heads[c, rows], w_one[:, c * HD : (c + 1) * HD])
                b = nt(dcat[rows, TILE:], w_two)
                u = wide(tiles[slot, rows])
                res = (a * vecs[0:1, at] + b * vecs[2:3, at]).astype(LOW)
                part_one[k, m, inner] = res.reshape(2, -1, GROUP)
                new = (a * u, a, b * u, b)
                sums = [s + jnp.sum(v, axis=0, keepdims=True) for s, v in zip(sums, new)]
            for r in range(4):
                vecg[r : r + 1, at] = sums[r]

        streamed(RING_SIZE, copies, use)

    def vec_first():
        lane = lax.broadcasted_iota(jnp.int32, (16, LANES), 1)
        for p in range(RING_SIZE * RING_SIZE):
            v = vecg[:, p * LANES : (p + 1) * LANES]
            lead = jnp.where(lane < LANES // 2, v, 0.0)
            tail = jnp.where(lane < LANES // 2, pltpu.roll(v, LANES // 2, 1), 0.0)
            vec_block[p // RING_SIZE, p % RING_SIZE, 0] = lead
            vec_block[p // RING_SIZE, p % RING_SIZE, 1] = tail
        for k in range(3):
            go(lambda k=k: v_post(k, vec_block.at[:, around(x, k + 1)], vec_x.at[k], line_x[k]))

    def vec_second():
        for k in range(3):
            v_post(k, vec_x.at[k], vec_x.at[k], mate).wait_recv()
        for r in range(RING_SIZE):
            vec_row[r] = vec_block[r, x] + vec_x[0, r] + vec_x[1, r] + vec_x[2, r]
        for k in range(3):
            go(lambda k=k: v_post(3 + k, vec_row.at[around(y, k + 1)], vec_y.at[k], line_y[k]))

    def vec_third():
        for k in range(3):
            v_post(3 + k, vec_y.at[k], vec_y.at[k], mate).wait_recv()
        vec_own[...] = vec_row[y] + vec_y[0] + vec_y[1] + vec_y[2]
        for k in range(7):
            there = lambda k=k: zl if k == 0 else (z + (k + 1) // 2) % 2
            go(
                lambda k=k, there=there: v_post(
                    6 + k, vec_own.at[there()], vec_z.at[k], line_z[k]
                )
            )

    def vec_finish():
        total = vec_own[zl]
        for k in range(7):
            v_post(6 + k, vec_z.at[k], vec_z.at[k], mate).wait_recv()
            total = total + vec_z[k]
        vec_out[...] = total

    def wait_loads():
        vecg[...] = jnp.zeros(vecg.shape, WIDE)
        fill_eye(eye)
        for ref in (flip_one, flip_two):
            ref[GROUP:, :] = jnp.ones((16, ref.shape[1]), LOW)
        for c in loads:
            c.wait()
        for c in range(2):
            total = jnp.sum(wide(part_zero[c, zl, z // 2, core]), axis=0, keepdims=True)
            for r in (7, 8):
                vecg[r : r + 1, c * half_model : (c + 1) * half_model] = total

    def up_weight_grads(hooks):
        for c in near_loads:
            c.wait()
        def bias(n):
            return pl.ds(9 + head // 2, 1), cols((head % 2) * 2 + n, GROUP)

        rights = [dcat.at[:, TILE + n * GROUP : TILE + (n + 1) * GROUP] for n in range(2)]
        weight_grads(hooks, 5, two_in, rights, up_grad, bias)
        for c in late:
            c.wait()

    def qkv_weight_grads(hooks):
        def bias(n):
            return pl.ds(4 + n, 1), cols(head, HD)

        weight_grads(hooks, 6, one_in, [heads.at[c] for c in range(3)], qkv_grad, bias)

    def settle():
        for key in list(started)[:-20]:
            started.pop(key)().wait_send()

    moves = {
        SETTLE: settle,
        FIRST: send_first,
        NEAR: send_near,
        SECOND: send_second,
        FAR_SIDE: send_last,
        FINISH: finish,
        Z_MATE: z_to_mate,
        Z_FIRST: z_first,
        Z_SECOND: z_second,
        Z_FINISH: z_finish,
        LOADS: wait_loads,
        VEC_ONE: vec_first,
        VEC_TWO: vec_second,
        VEC_THREE: vec_third,
    }

    def act(kind, *args):
        moves[kind](*args)

    loops = {
        CAT_GRADS: cat_grads,
        UP_GRADS: up_weight_grads,
        BRANCH: branch,
        ATTEND_BACK: attend_back,
        QKV_GRADS: qkv_weight_grads,
        NORM_GRADS: norm_grads,
    }
    play(BACKWARD_ORDER, loops, act)
    vec_finish()
    for i in (UP, QKV, OD):
        arrived(i, 24, bufs[i][6])
    for k in range(9):
        out_copy(k).wait()
    for make in started.values():
        make().wait_send()


def backward(held):
    dy, up_full, qkv_full, od_full, vecs, one, two, unit, heads, cat, slope, turn, soft, _ = held
    total, model = one.shape
    tokens = dy.shape[2]
    owned = od_full.shape[3]
    widths = [w.shape[-1] for w in (od_full, up_full, qkv_full)]
    shape = jax.ShapeDtypeStruct
    out = [shape((owned, w), LOW) for w in widths]
    out += [shape((owned, w), LOW) for w in widths]
    out += [shape((16, LANES), WIDE)]
    out += [shape((tokens, model), LOW)] * 2
    plane = (RING_SIZE, RING_SIZE, 2, owned)
    scratch = [pltpu.VMEM((owned, w), LOW) for w in widths]
    scratch += [pltpu.VMEM((tokens, model), LOW)] * 2
    scratch += [
        pltpu.VMEM((*plane, widths[1]), LOW),
        pltpu.VMEM((*plane, widths[2]), LOW),
        pltpu.VMEM(slope.shape, LOW),
        pltpu.VMEM(cat.shape, LOW),
        pltpu.VMEM(heads.shape, LOW),
        pltpu.VMEM(turn.shape, WIDE),
        pltpu.VMEM(soft.shape, LOW),
        pltpu.VMEM((GROUP + 16, total), LOW),
        pltpu.VMEM((GROUP + 16, total), LOW),
        pltpu.VMEM((16, model), WIDE),
        pltpu.VMEM((RING_SIZE, RING_SIZE, 2, 16, LANES), WIDE),
        pltpu.VMEM((2, 2, 2, owned, widths[0]), LOW),
        pltpu.VMEM((2, RING_SIZE, owned, widths[0]), LOW),
        pltpu.VMEM((*plane, widths[0]), LOW),
        pltpu.VMEM((2, total, GROUP), LOW),
        pltpu.VMEM((TILE, TILE), LOW),
    ]
    for n in (2, 4):
        w = model // n
        scratch += [
            pltpu.VMEM((n, 2, 2, 2, tokens, w), LOW),
            pltpu.VMEM((n, 2, 2, tokens, w), LOW),
            pltpu.VMEM((n, tokens, w), LOW),
            pltpu.VMEM((n, 2, tokens, w), LOW),
        ]
    for w in widths:
        scratch += [
            pltpu.VMEM((2, 2, 2, owned, w), LOW),
            pltpu.VMEM((2, 2, RING_SIZE, owned, w), LOW),
            pltpu.VMEM((2, 2, owned // 2, w), LOW),
            pltpu.VMEM((2, 2, owned, w), LOW),
            pltpu.VMEM((owned, w), LOW),
        ]
    scratch += [
        pltpu.VMEM((3, RING_SIZE, 2, 16, LANES), WIDE),
        pltpu.VMEM((3, 2, 16, LANES), WIDE),
        pltpu.VMEM((7, 16, LANES), WIDE),
        pltpu.VMEM((RING_SIZE, 2, 16, LANES), WIDE),
        pltpu.VMEM((2, 16, LANES), WIDE),
        pltpu.SemaphoreType.DMA((3, 25)),
        pltpu.SemaphoreType.DMA((3, 25)),
        pltpu.SemaphoreType.DMA((6, 7)),
        pltpu.SemaphoreType.DMA((6, 7)),
        pltpu.SemaphoreType.DMA((13,)),
        pltpu.SemaphoreType.DMA((13,)),
        pltpu.SemaphoreType.DMA((18,)),
        pltpu.SemaphoreType.DMA((7, 2)),
        pltpu.SemaphoreType.DMA((9,)),
    ]
    specs = [VMEM if k == 4 else ANY for k in range(14)]
    return pl.pallas_call(
        backward_kernel,
        out_shape=out,
        in_specs=specs,
        out_specs=[VMEM if k == 6 else ANY for k in range(len(out))],
        scratch_shapes=scratch,
        compiler_params=pltpu.CompilerParams(
            collective_id=1, has_side_effects=True, vmem_limit_bytes=63 * 2**20
        ),
        name="backward_and_reduce",
    )(dy.reshape(2, 2, 2, tokens, model), *held[1:])


def adamw(weight, gradient, moment, square, step_rate, decay_rate):
    moment_new = beta_first * moment + (1.0 - beta_first) * gradient
    square_new = beta_second * square + (1.0 - beta_second) * gradient * gradient
    first_fix = 1.0 / (1.0 - beta_first**UPDATE_STEP)
    second_fix = 1.0 / (1.0 - beta_second**UPDATE_STEP)
    fixed = square_new * second_fix
    below = fixed * lax.rsqrt(fixed) + adam_eps
    inverse = pl.reciprocal(below, approx=True)
    inverse = inverse * (2.0 - below * inverse)
    direction = moment_new * first_fix * inverse
    weight_new = weight - step_rate * (direction + decay_rate * weight)
    return (weight_new, moment_new, square_new)


def update_kernel(*refs):
    (own_od, own_up, own_qkv, swap_od, swap_up, swap_qkv, vec_sum, u_zero, u_one, x_in, dy_in) = refs[:11]
    vecs, state, outs = refs[11], refs[12:27], refs[27:44]
    grads, rows_in, held = refs[44:50], refs[50:54], refs[54:69]
    block_v, grad_v, in_sems, out_sems = refs[69:]
    zl = lax.axis_index("dp") % 2
    started = []

    def load(src, dst):
        copy = pltpu.make_async_copy(src, dst, in_sems.at[len(started)])
        copy.start(priority=len(started) % 2)
        started.append(copy)
        return copy

    stored = []

    def store(src, dst):
        copy = pltpu.make_async_copy(src, dst, out_sems.at[len(stored)])
        copy.start(priority=len(stored) % 2)
        stored.append(copy)

    sources = (own_od, own_up, own_qkv, swap_od, swap_up, swap_qkv)
    row_waits = [load(a, b) for a, b in zip((x_in, u_zero, u_one, dy_in), rows_in)]
    waits = {}
    for i, parts in ((2, (1, 4)), (3, (0, 3)), (0, (2, 5)), (1, ())):
        waits[i] = [load(sources[k], grads[k]) for k in parts]
        waits[i] += [load(state[3 * i + k], held[3 * i + k]) for k in range(3)]
    vec_waits = [load(state[12 + k], held[12 + k]) for k in range(3)]

    def new(i, at, gradient, rate, decay):
        three = held[3 * i : 3 * i + 3]
        weight, moment, square = (r[at] for r in three)
        for r, v in zip(three, adamw(weight, gradient, moment, square, rate, decay)):
            r[at] = v

    def done(i):
        for k in range(3):
            store(held[3 * i + k], outs[2 + 3 * i + k])

    def part(k, h, at):
        return wide(jnp.where(zl == h, grads[k][at], grads[k + 3][at]))

    def rows_of(k, size):
        return pl.ds(pl.multiple_of(k * size, size), size)

    for c in row_waits:
        c.wait()
    x_v, zero_v, one_v, dy_v = rows_in

    @pl.loop(0, 4)
    def _(k):
        rows = rows_of(k, 32)
        v = wide(x_v[rows])
        block_v[rows] = (v + wide(zero_v[rows]) + vecs[7:8, :] + vecs[8:9, :]).astype(LOW)
        centred = v - jnp.mean(v, axis=-1, keepdims=True)
        scale = lax.rsqrt(jnp.mean(centred * centred, axis=-1, keepdims=True) + norm_eps)
        unit = centred * scale
        g = wide(one_v[rows])
        g = g - jnp.mean(g, axis=-1, keepdims=True) - unit * jnp.mean(g * unit, axis=-1, keepdims=True)
        grad_v[rows] = wide(dy_v[rows]) + scale * g

    store(block_v, outs[0])
    store(grad_v, outs[1])
    for c in waits[2]:
        c.wait()

    @pl.loop(0, 4)
    def _(k):
        rows = rows_of(k, 16)
        for h in range(2):
            n = grads[1].shape[1]
            g = part(1, h, (rows, slice(0, n)))
            new(2, (rows, slice(h * n, (h + 1) * n)), g, matrix_rate, matrix_decay)

    done(2)
    for c in waits[3]:
        c.wait()

    @pl.loop(0, 4)
    def _(k):
        rows = rows_of(k, 16)
        n = grads[0].shape[1] - HD
        for h in range(2):
            g = part(0, h, (rows, slice(HD, HD + n)))
            new(3, (rows, slice(h * n, (h + 1) * n)), g, matrix_rate, matrix_decay)

    done(3)
    for c in waits[0]:
        c.wait()

    @pl.loop(0, 4)
    def _(k):
        rows = rows_of(k, 16)
        for c in range(3):
            for h in range(2):
                g = part(2, h, (rows, slice(c * HD, (c + 1) * HD)))
                new(0, (c, rows, slice(h * HD, (h + 1) * HD)), g, matrix_rate, matrix_decay)

    done(0)
    for c in waits[1]:
        c.wait()

    @pl.loop(0, 4)
    def _(k):
        rows = rows_of(k, 16)
        for h in range(2):
            g = part(0, h, (rows, slice(0, HD)))
            new(1, (rows, slice(h * HD, (h + 1) * HD)), g, matrix_rate, matrix_decay)

    done(1)
    for c in vec_waits:
        c.wait()
    at = (slice(None), slice(None))
    shape = held[12].shape
    new(4, at, vec_sum[0 : shape[0], 0 : shape[1]], vector_rate, 0.0)
    done(4)
    for c in stored:
        c.wait()


def update(reduced, rows, cot, vecs, state):
    own, vec_sum, sums = reduced[:6], reduced[6], reduced[7:]
    shape = jax.ShapeDtypeStruct
    out = [shape(rows.shape, LOW), shape(rows.shape, WIDE)]
    out += [shape(a.shape, WIDE) for a in state]
    scratch = [pltpu.VMEM(a.shape, a.dtype) for a in (*own, rows, *sums, cot, *state)]
    scratch += [
        pltpu.VMEM(rows.shape, LOW),
        pltpu.VMEM(rows.shape, WIDE),
        pltpu.SemaphoreType.DMA((25,)),
        pltpu.SemaphoreType.DMA((17,)),
    ]
    specs = [ANY] * 6 + [VMEM] + [ANY] * 4 + [VMEM] + [ANY] * 15
    return pl.pallas_call(
        update_kernel,
        out_shape=out,
        in_specs=specs,
        out_specs=[ANY] * len(out),
        scratch_shapes=scratch,
        compiler_params=pltpu.CompilerParams(vmem_limit_bytes=63 * 2**20),
        name="update",
    )(*own, vec_sum, *sums, rows, cot, vecs, *state)


def local(
    inputs,
    cotangent,
    lengths,
    qkv_weight,
    out_weight,
    up_weight,
    down_weight,
    norm_vectors,
    qkv_mean,
    qkv_square,
    out_mean,
    out_square,
    up_mean,
    up_square,
    down_mean,
    down_square,
    vector_mean,
    vector_square,
):
    weights = (up_weight, qkv_weight, out_weight.T, down_weight.T)
    held = forward(inputs, cotangent, lengths, norm_vectors, weights)
    state = (
        *(qkv_weight, qkv_mean, qkv_square),
        *(out_weight.T, out_mean.T, out_square.T),
        *(up_weight, up_mean, up_square),
        *(down_weight.T, down_mean.T, down_square.T),
        *(norm_vectors, vector_mean, vector_square),
    )
    out = list(update(backward(held), inputs, cotangent, held[4], state))
    for k in (5, 6, 7, 11, 12, 13):
        out[k] = out[k].T
    return tuple(out)


def solution(mesh):
    placed = (
        P(("dp", "tensor"), None),
        P(("dp", "tensor"), None),
        P("dp", None),
        P(None, "dp", "tensor"),
        P("tensor", "dp"),
        P("dp", "tensor"),
        P("tensor", "dp"),
        P(None, "dp"),
        P(None, "dp", "tensor"),
        P(None, "dp", "tensor"),
        P("tensor", "dp"),
        P("tensor", "dp"),
        P("dp", "tensor"),
        P("dp", "tensor"),
        P("tensor", "dp"),
        P("tensor", "dp"),
        P(None, "dp"),
        P(None, "dp"),
    )
    return jax.shard_map(
        local,
        mesh=mesh,
        in_specs=placed,
        out_specs=(
            P(("dp", "tensor"), None),
            P(("dp", "tensor"), None),
            P(None, "dp", "tensor"),
            P(None, "dp", "tensor"),
            P(None, "dp", "tensor"),
            P("tensor", "dp"),
            P("tensor", "dp"),
            P("tensor", "dp"),
            P("dp", "tensor"),
            P("dp", "tensor"),
            P("dp", "tensor"),
            P("tensor", "dp"),
            P("tensor", "dp"),
            P("tensor", "dp"),
            P(None, "dp"),
            P(None, "dp"),
            P(None, "dp"),
        ),
        check_vma=False,
    )
```
